512 devices in a mesh: dp: 4 (over x), ctx: 16 (over z), head: 8 (over y, core).
Axes of the slice: x: 4, y: 4, z: 16, core: 2. Of those that a mesh axis runs over, the one named last changes fastest.
Arguments:
- queries: bfloat16 [8192, 4096], P(('dp', 'ctx'), 'head'), parts along dimension 0, may hold values from -4.5 to 4.5
- context_keys: bfloat16 [131072, 1024], P(('dp', 'ctx'), 'head'), parts along dimension 0, may hold values from -4.5 to 4.5
- context_values: bfloat16 [131072, 1024], P(('dp', 'ctx'), 'head'), parts along dimension 0, may hold values from -4.5 to 4.5
- own_keys: bfloat16 [8192, 1024], P(('dp', 'ctx'), 'head'), parts along dimension 0, may hold values from -4.5 to 4.5
- own_values: bfloat16 [8192, 1024], P(('dp', 'ctx'), 'head'), parts along dimension 0, may hold values from -4.5 to 4.5
- out_grad: bfloat16 [8192, 4096], P(('dp', 'ctx'), 'head'), parts along dimension 0, may hold values from -4.5 to 4.5
- block_ids: int32 [64, 24], P('dp'), parts along dimension 0, may hold values from -1 to 255, as said below
Outputs:
- attended: bfloat16 [8192, 4096], P(('dp', 'ctx'), 'head'), parts along dimension 0
- query_grad: bfloat16 [8192, 4096], P(('dp', 'ctx'), 'head'), parts along dimension 0
- key_grad: bfloat16 [131072, 1024], P(('dp', 'ctx'), 'head'), parts along dimension 0
- value_grad: bfloat16 [131072, 1024], P(('dp', 'ctx'), 'head'), parts along dimension 0
- own_key_grad: bfloat16 [8192, 1024], P(('dp', 'ctx'), 'head'), parts along dimension 0
- own_value_grad: bfloat16 [8192, 1024], P(('dp', 'ctx'), 'head'), parts along dimension 0
The draws below stay inside these ranges and needn't reach their ends.
There are 4 independent parts, one for each index of `dp`. The reference program is written for one: setup_inputs(seed, part) draws one part's arguments, and reference() takes and returns one part's arrays. A program takes and returns all parts, laid end to end along the dimension named above; each array names one. Nothing has to cross between parts.
Inputs may be any that keep to these rules, and one draw needn't show every extreme that they name: `block_ids`: each row lists distinct blocks in ascending order, then -1 in unused slots. At most 2 listed blocks of one row have the same b // 16, and some row reaches that; some row fills all 24 slots.
All inputs are finite; a program needn't handle non-finite values.
Results may differ from the reference program's by a relative error of at most 0.012.
The reference program's roundings to bfloat16 on the way count: a program that leaves them out, or rounds other values in their place, can miss the bound.
Values may be sent and summed in bfloat16 or wider, within the bound.
A program may use at most 128 MiB of HBM per device.

```python
import math
import jax
import jax.numpy as jnp
from jax import lax

QH = 32
KVH = 8
DH = 128
BLK = 128
CLEN = 128
PER_SRC = 2
CB_DEV = 16
CANDS = 16
MAXB = 24
CB = 256
CTX_TOK = 32768
CAND_TOK = 2048
N_CTX = 16


def draw_queries(key, part):
    key = jax.random.fold_in(key, 3)
    return jnp.clip(jax.random.normal(key, (CAND_TOK, QH * DH), jnp.float32), -4.5, 4.5).astype(jnp.bfloat16)


def draw_context_keys(key, part):
    key = jax.random.fold_in(key, 5)
    return jnp.clip(jax.random.normal(key, (CTX_TOK, KVH * DH), jnp.float32), -4.5, 4.5).astype(jnp.bfloat16)


def block_order(row_key):
    return jax.random.permutation(row_key, CB_DEV)


def source_order(row_key):
    return jax.random.permutation(row_key, N_CTX)


def draw_block_ids(key, part):
    key = jax.random.fold_in(key, 7)
    pick_key, base_key, extra_key, heavy_key, dense_key = jax.random.split(key, 5)
    orders = jax.vmap(block_order)(jax.random.split(pick_key, CANDS * N_CTX))
    picks = jnp.sort(orders[:, :PER_SRC], axis=1).reshape(CANDS, N_CTX, PER_SRC).astype(jnp.int32)
    ranks = jax.vmap(source_order)(jax.random.split(heavy_key, CANDS))
    heavy = (ranks < N_CTX // 2).astype(jnp.int32)
    counts = jax.random.randint(base_key, (CANDS, N_CTX), 0, 2) + heavy * jax.random.randint(extra_key, (CANDS, N_CTX), 0, 2)
    dense = jax.random.randint(dense_key, (), 0, CANDS)
    counts = jnp.where((jnp.arange(CANDS) == dense)[:, None], 1 + heavy, counts)
    sources = jnp.arange(N_CTX, dtype=jnp.int32)[None, :, None]
    global_ids = (sources * CB_DEV + picks).reshape(CANDS, N_CTX * PER_SRC)
    valid = (jnp.arange(PER_SRC)[None, None, :] < counts[:, :, None]).reshape(CANDS, N_CTX * PER_SRC)
    order_key = jnp.where(valid, jnp.arange(N_CTX * PER_SRC, dtype=jnp.int32)[None, :], N_CTX * PER_SRC)
    order = jnp.argsort(order_key, axis=1, stable=True)[:, :MAXB]
    chosen_ids = jnp.take_along_axis(global_ids, order, axis=1)
    chosen_valid = jnp.take_along_axis(valid, order, axis=1)
    return jnp.where(chosen_valid, chosen_ids, -1).astype(jnp.int32)


def shard_levels(own_key, extent, cuts, smallest, top_value):
    def one(dim, parts):
        draws = jax.random.uniform(jax.random.fold_in(jax.random.fold_in(own_key, 6), dim), (parts,), jnp.float32, smallest / len(cuts), top_value / len(cuts))
        return jnp.repeat(jnp.exp(draws), extent[dim] // parts).reshape((-1,) + (1,) * (len(extent) - dim - 1))

    gain = one(*cuts[0])
    for cut in cuts[1:]:
        gain = gain * one(*cut)
    return gain


def centred(own_key, extent, width, most, cuts=(), held_as=jnp.bfloat16):
    level = shard_levels(own_key, extent, cuts, -0.22, 0.18) if cuts else 1.0
    entries = jax.random.normal(own_key, extent, jnp.float32) * width * level
    return jnp.minimum(jnp.maximum(entries, -most), most).astype(held_as)


def setup_inputs(seed: int = 0, part: int = 0) -> dict:
    keys = jax.random.split(jax.random.key(seed), 8)
    part_keys = jax.random.split(jax.random.fold_in(keys[7], part), 8)
    return {
        "queries": draw_queries(jax.random.fold_in(jax.random.fold_in(keys[7], part), 71), part),
        "context_keys": draw_context_keys(jax.random.fold_in(jax.random.fold_in(keys[7], part), 71), part),
        "context_values": centred(part_keys[2], (CTX_TOK, KVH * DH), 1.0, 4.5, ((0, 16), (1, 8))),
        "own_keys": centred(part_keys[3], (CAND_TOK, KVH * DH), 1.0, 4.5, ((0, 16), (1, 8))),
        "own_values": centred(part_keys[4], (CAND_TOK, KVH * DH), 1.0, 4.5, ((0, 16), (1, 8))),
        "out_grad": centred(part_keys[5], (CAND_TOK, QH * DH), 1.0, 4.5, ((0, 16), (1, 8))),
        "block_ids": draw_block_ids(jax.random.fold_in(jax.random.fold_in(keys[7], part), 71), part),
    }


MASKED_SCORE = -1e+30

def reference(queries, context_keys, context_values, own_keys, own_values, out_grad, block_ids):
    group_ratio = QH // KVH
    score_scale = 1.0 / math.sqrt(DH)
    key_blocks = context_keys.reshape(CB, BLK, KVH, DH)
    value_blocks = context_values.reshape(CB, BLK, KVH, DH)
    causal = jnp.arange(CLEN)[:, None] >= jnp.arange(CLEN)[None, :]

    def one_list(running, candidate):
        key_sums, value_sums = running
        listed = block_ids[candidate]
        listed_live = listed >= 0
        safe_ids = jnp.where(listed_live, listed, 0).astype(jnp.int32)
        row_start = (candidate * CLEN).astype(jnp.int32)
        query_rows = lax.dynamic_slice_in_dim(queries, row_start, CLEN, 0).reshape(CLEN, KVH, group_ratio, DH).astype(jnp.float32)
        grad_rows = lax.dynamic_slice_in_dim(out_grad, row_start, CLEN, 0).reshape(CLEN, KVH, group_ratio, DH).astype(jnp.float32)
        own_key_rows = lax.dynamic_slice_in_dim(own_keys, row_start, CLEN, 0).reshape(CLEN, KVH, DH)
        own_value_rows = lax.dynamic_slice_in_dim(own_values, row_start, CLEN, 0).reshape(CLEN, KVH, DH)
        key_rows = jnp.concatenate([key_blocks[safe_ids].reshape(MAXB * BLK, KVH, DH), own_key_rows], 0).astype(jnp.float32)
        value_rows = jnp.concatenate([value_blocks[safe_ids].reshape(MAXB * BLK, KVH, DH), own_value_rows], 0).astype(jnp.float32)
        far_seen = jnp.broadcast_to(jnp.repeat(listed_live, BLK)[None, :], (CLEN, MAXB * BLK))
        visible = jnp.concatenate([far_seen, causal], 1)
        scores = jnp.einsum('igrd,jgd->grij', query_rows, key_rows) * score_scale
        scores = jnp.where(visible, scores, MASKED_SCORE)
        maxima = lax.optimization_barrier(jnp.max(scores, axis=-1))
        totals = lax.optimization_barrier(jnp.sum(jnp.where(visible, jnp.exp(scores - maxima[..., None]), 0.0), axis=-1))
        logsum = maxima + jnp.log(totals)
        far_part = scores[..., :MAXB * BLK].reshape(KVH, group_ratio, CLEN, MAXB, BLK)
        block_max = lax.optimization_barrier(jnp.max(far_part, axis=-1))
        source_ids = jnp.where(listed_live, listed // CB_DEV, -1)
        same_source = (source_ids[:, None] == source_ids[None, :]) & listed_live[:, None] & listed_live[None, :]
        source_max = lax.optimization_barrier(jnp.max(jnp.where(same_source, block_max[..., None, :], MASKED_SCORE), axis=-1))
        far_local = jnp.where(listed_live[:, None], jnp.exp(far_part - source_max[..., None]), 0.0)
        own_part = scores[..., MAXB * BLK:]
        own_max = lax.optimization_barrier(jnp.max(own_part, axis=-1))
        own_local = jnp.where(causal, jnp.exp(own_part - own_max[..., None]), 0.0)
        local = jnp.concatenate([far_local.reshape(KVH, group_ratio, CLEN, MAXB * BLK), own_local], -1)
        local_rounded = lax.optimization_barrier(local.astype(jnp.bfloat16)).astype(jnp.float32)
        far_factor = jnp.repeat(jnp.exp(source_max - logsum[..., None]), BLK, axis=-1)
        own_factor = jnp.broadcast_to(jnp.exp(own_max - logsum)[..., None], own_part.shape)
        factor = jnp.concatenate([far_factor, own_factor], -1)
        output = jnp.einsum('grij,jgd->igrd', local_rounded * factor, value_rows)
        weights = jnp.where(visible, jnp.exp(scores - logsum[..., None]), 0.0)
        rounded = lax.optimization_barrier(weights.astype(jnp.bfloat16)).astype(jnp.float32)
        deltas = lax.optimization_barrier(jnp.sum(grad_rows * output, axis=-1)).transpose(1, 2, 0)
        grad_weights = jnp.einsum('igrd,jgd->grij', grad_rows, value_rows)
        grad_scores = lax.optimization_barrier((weights * (grad_weights - deltas[..., None])).astype(jnp.bfloat16)).astype(jnp.float32)
        query_grad = jnp.einsum('grij,jgd->igrd', grad_scores, key_rows) * score_scale
        key_grad = jnp.einsum('grij,igrd->jgd', grad_scores, query_rows) * score_scale
        value_grad = jnp.einsum('grij,igrd->jgd', rounded, grad_rows)
        live_rows = listed_live[:, None, None, None]
        far_keys = jnp.where(live_rows, key_grad[:MAXB * BLK].reshape(MAXB, BLK, KVH, DH), 0.0)
        far_values = jnp.where(live_rows, value_grad[:MAXB * BLK].reshape(MAXB, BLK, KVH, DH), 0.0)
        key_sums = key_sums.at[safe_ids].add(far_keys)
        value_sums = value_sums.at[safe_ids].add(far_values)
        emitted = (output.astype(jnp.bfloat16).reshape(CLEN, QH * DH), query_grad.astype(jnp.bfloat16).reshape(CLEN, QH * DH), key_grad[MAXB * BLK:].astype(jnp.bfloat16).reshape(CLEN, KVH * DH), value_grad[MAXB * BLK:].astype(jnp.bfloat16).reshape(CLEN, KVH * DH))
        return ((key_sums, value_sums), emitted)
    zero_sums = jnp.zeros((CB, BLK, KVH, DH), jnp.float32)
    (key_sums, value_sums), pieces = lax.scan(one_list, (zero_sums, zero_sums), jnp.arange(CANDS, dtype=jnp.int32))
    attended = pieces[0].reshape(CAND_TOK, QH * DH)
    query_grad = pieces[1].reshape(CAND_TOK, QH * DH)
    own_key_grad = pieces[2].reshape(CAND_TOK, KVH * DH)
    own_value_grad = pieces[3].reshape(CAND_TOK, KVH * DH)
    key_grad = key_sums.astype(jnp.bfloat16).reshape(CTX_TOK, KVH * DH)
    value_grad = value_sums.astype(jnp.bfloat16).reshape(CTX_TOK, KVH * DH)
    return (attended, query_grad, key_grad, value_grad, own_key_grad, own_value_grad)
```

```python
import math

import jax
import jax.numpy as jnp
from jax import lax
from jax.experimental import pallas as pl
from jax.experimental.pallas import tpu as pltpu
from jax.sharding import PartitionSpec as P

N = 16
BLK = 128
DH = 128
HEADS = 4
ROWS = HEADS * 128
KEYS = 2 * BLK
SLOTS = 24
CB_DEV = 16
SCALE = 1.0 / math.sqrt(DH)
HIDDEN = -1e30
FLOOR = -1e25
WIDE = 2
FAR = 8
F32 = jnp.float32
BF16 = jnp.bfloat16
NT = (((1,), (1,)), ((), ()))
NN = (((1,), (0,)), ((), ()))


def dot(a, b, dims=NN):
    return lax.dot_general(a, b, dims, preferred_element_type=F32)


def wrap(x):
    return lax.rem(x + 2 * N, N)


def head(h):
    return slice(h * 128, (h + 1) * 128)


def pick_blocks(ids_ref, c, low):
    first = jnp.int32(CB_DEV)
    last = jnp.int32(-1)
    count = jnp.int32(0)
    for j in range(SLOTS):
        b = ids_ref[c, j] - low
        inside = (b >= 0) & (b < CB_DEV)
        first = jnp.where(inside, jnp.minimum(first, b), first)
        last = jnp.where(inside, jnp.maximum(last, b), last)
        count = count + jnp.where(inside, 1, 0)
    return jnp.minimum(first, CB_DEV - 1), jnp.maximum(last, 0), count


def ring_kernel(
    ids_ref, q_ref, k_ref, v_ref, ok_ref, ov_ref, g_ref,
    att_ref, qg_ref, okg_ref, ovg_ref, dks_ref, dvs_ref,
    q_all, g_all, nk, nv, lw, dp, ou, qu,
    own_lw, own_dp, own_ou, own_qu, own_st, own_del,
    st_out, st_in, del_out, del_in, lse_all, delta_all,
    ds_t, p_t, sb, rb, sf, rf,
    g_send, g_recv, c_send, c_recv, st_s, st_r, de_s, de_r, ls_s, ls_r, dl_s, dl_r,
):
    me = lax.axis_index("ctx")
    low = me * CB_DEV
    nbr = (wrap(me + 1), wrap(me - 1))

    barrier = pltpu.get_barrier_semaphore()

    def greet(p, _):
        pl.semaphore_signal(barrier, inc=1, device_id={"ctx": wrap(me + p)})
        return 0

    lax.fori_loop(1, N, greet, 0)
    for h in range(HEADS):
        q_all[me, head(h), :] = q_ref[:, head(h)]
        g_all[me, head(h), :] = g_ref[:, head(h)]
    pl.semaphore_wait(barrier, N - 1)

    def gather_copy(stream, D, t, half, c):
        buf = (q_all, g_all)[stream]
        part = buf.at[c, pl.ds(half * 256, 256)]
        return pltpu.make_async_remote_copy(
            src_ref=part, dst_ref=part,
            send_sem=g_send.at[stream, D, t - 1, half], recv_sem=g_recv.at[stream, D, t - 1, half],
            device_id={"ctx": nbr[D]},
        )

    def chunk_at(D, t):
        return wrap(me - t) if D == 0 else wrap(me + t)

    def gather_step(stream, t):
        for half in range(2):
            for D in range(2):
                steps = 8 if D == stream else 7
                if isinstance(t, int) and t > steps:
                    continue
                c = chunk_at(D, t)
                gather_copy(stream, D, t, half, c).wait_recv()
                if not isinstance(t, int) or t < steps:
                    gather_copy(stream, D, t + 1, half, c).start()

    def gather_first(stream):
        for half in range(2):
            for D in range(2):
                gather_copy(stream, D, 1, half, me).start()

    def gather_sent(stream, t):
        for half in range(2):
            for D in range(2):
                if isinstance(t, int) and t > (8 if D == stream else 7):
                    continue
                gather_copy(stream, D, t, half, me).wait_send()

    def to_candidate(src, dst, send, recv, c, slot):
        return pltpu.make_async_remote_copy(
            src_ref=src.at[c], dst_ref=dst.at[slot], send_sem=send.at[c], recv_sem=recv.at[slot],
            device_id={"ctx": c},
        )

    def to_holder(buf, send, recv, slot, p):
        return pltpu.make_async_remote_copy(
            src_ref=buf.at[slot], dst_ref=buf.at[slot], send_sem=send.at[p], recv_sem=recv.at[slot],
            device_id={"ctx": wrap(me + p)},
        )

    def each_peer(fn):
        def body(p, _):
            fn(p)
            return 0

        lax.fori_loop(1, N, body, 0)

    def scores(c):
        first, last, count = pick_blocks(ids_ref, c, low)
        nk[c, :BLK, :] = k_ref[first]
        nk[c, BLK:, :] = k_ref[last]
        nv[c, :BLK, :] = v_ref[first]
        nv[c, BLK:, :] = v_ref[last]
        bias0 = jnp.where(count >= 1, 0.0, HIDDEN).astype(F32)
        bias1 = jnp.where(count >= 2, 0.0, HIDDEN).astype(F32)
        keys = nk[c]
        vt = nv[c].T
        for h in range(HEADS):
            s = dot(keys, q_all[c, head(h), :], NT) * SCALE
            s0 = s[:BLK] + bias0
            s1 = s[BLK:] + bias1
            m = jnp.max(jnp.maximum(s0, s1), axis=0, keepdims=True)
            m = jnp.maximum(m, FLOOR)
            e = jnp.exp(jnp.concatenate([s0, s1], axis=0) - m)
            lw[c, :, head(h)] = e
            st_out[c, h : h + 1, :] = m
            st_out[c, HEADS + h : HEADS + h + 1, :] = jnp.sum(e, axis=0, keepdims=True)
            ou[c, :, head(h)] = dot(vt, e.astype(BF16))

    def send_scores(c):
        scores(c)
        to_candidate(st_out, st_in, st_s, st_r, c, me).start()

    def weights_grad(c):
        vals = nv[c]
        for h in range(HEADS):
            d = dot(vals, g_all[c, head(h), :], NT)
            dp[c, :, head(h)] = d
            e = lw[c, :, head(h)].astype(BF16).astype(F32)
            del_out[c, h : h + 1, :] = jnp.sum(e * d, axis=0, keepdims=True)

    def send_weights_grad(c):
        weights_grad(c)
        to_candidate(del_out, del_in, de_s, de_r, c, me).start()

    def grads(c):
        kt = nk[c].T
        f = jnp.exp(st_out[c, :HEADS, :] - lse_all[c, :HEADS, :])
        for h in range(HEADS):
            w = lw[c, :, head(h)] * f[h : h + 1, :]
            p_t[:, head(h)] = w.astype(BF16)
            ds = (w * (dp[c, :, head(h)] - delta_all[c, h : h + 1, :])).astype(BF16)
            ds_t[:, head(h)] = ds
            qu[c, :, head(h)] = dot(kt, ds)
        dks_ref[c] = dot(ds_t[...], q_all[c]) * SCALE
        dvs_ref[c] = dot(p_t[...], g_all[c])

    def own_scores():
        keys = ok_ref[...]
        vt = ov_ref[...].T
        seen = lax.broadcasted_iota(jnp.int32, (BLK, 128), 0) <= lax.broadcasted_iota(jnp.int32, (BLK, 128), 1)
        for h in range(HEADS):
            s = jnp.where(seen, dot(keys, q_all[me, head(h), :], NT) * SCALE, HIDDEN)
            m = jnp.max(s, axis=0, keepdims=True)
            e = jnp.exp(s - m)
            own_lw[:, head(h)] = e
            own_st[h : h + 1, :] = m
            own_st[HEADS + h : HEADS + h + 1, :] = jnp.sum(e, axis=0, keepdims=True)
            own_ou[:, head(h)] = dot(vt, e.astype(BF16))

    def own_weights_grad():
        vals = ov_ref[...]
        for h in range(HEADS):
            d = dot(vals, g_all[me, head(h), :], NT)
            own_dp[:, head(h)] = d
            e = own_lw[:, head(h)].astype(BF16).astype(F32)
            own_del[h : h + 1, :] = jnp.sum(e * d, axis=0, keepdims=True)

    def own_grads():
        kt = ok_ref[...].T
        f = jnp.exp(own_st[:HEADS, :] - lse_all[me, :HEADS, :])
        for h in range(HEADS):
            w = own_lw[:, head(h)] * f[h : h + 1, :]
            p_t[:BLK, head(h)] = w.astype(BF16)
            ds = (w * (own_dp[:, head(h)] - delta_all[me, h : h + 1, :])).astype(BF16)
            ds_t[:BLK, head(h)] = ds
            own_qu[:, head(h)] = dot(kt, ds)
        okg_ref[...] = (dot(ds_t[:BLK, :], q_all[me]) * SCALE).astype(BF16)
        ovg_ref[...] = dot(p_t[:BLK, :], g_all[me]).astype(BF16)

    def combine_logsum():
        st_in[me] = st_out[me]
        each_peer(lambda p: to_candidate(st_out, st_in, st_s, st_r, wrap(me + p), wrap(me + p)).wait_recv())
        maxima = st_in[:, :HEADS, :]
        totals = st_in[:, HEADS:, :]
        own_max = own_st[:HEADS, :]
        top = jnp.maximum(jnp.max(maxima, axis=0), own_max)
        total = own_st[HEADS:, :] * jnp.exp(own_max - top) + jnp.sum(totals * jnp.exp(maxima - top[None]), axis=0)
        lse_all[me, :HEADS, :] = top + jnp.log(total)
        each_peer(lambda p: to_holder(lse_all, ls_s, ls_r, me, p).start())

    def combine_deltas():
        del_in[me] = del_out[me]
        each_peer(lambda p: to_candidate(del_out, del_in, de_s, de_r, wrap(me + p), wrap(me + p)).wait_recv())
        logsum = lse_all[me, :HEADS, :]
        total = own_del[:HEADS, :] * jnp.exp(own_st[:HEADS, :] - logsum)
        total = total + jnp.sum(del_in[:, :HEADS, :] * jnp.exp(st_in[:, :HEADS, :] - logsum[None]), axis=0)
        delta_all[me, :HEADS, :] = total
        each_peer(lambda p: to_holder(delta_all, dl_s, dl_r, me, p).start())

    def buffers(chain, D, d):
        if isinstance(d, int) and d <= WIDE:
            return sf.at[chain, D, d - 1], rf.at[chain, D, d - 1]
        return sb.at[chain, D, d - 1 - WIDE], rb.at[chain, D, d - 1 - WIDE]

    def chain_copy(chain, D, d, half):
        src, dst = buffers(chain, D, d)
        rows = pl.ds(half * 64, 64)
        return pltpu.make_async_remote_copy(
            src_ref=src.at[rows], dst_ref=dst.at[rows],
            send_sem=c_send.at[chain, D, d - 1, half], recv_sem=c_recv.at[chain, D, d - 1, half],
            device_id={"ctx": nbr[D]},
        )

    def factor(c):
        return jnp.exp(st_out[c, :HEADS, :] - lse_all[c, :HEADS, :])

    def chain_step(chain, i):
        for half in range(2):
            rows = slice(half * 64, half * 64 + 64)
            for D in range(2):
                d = (8 if D == chain else 7) - i
                if isinstance(d, int) and d < 1:
                    continue
                c = wrap(me + d) if D == 0 else wrap(me - d)
                started = not isinstance(i, int) or i > 0
                if started:
                    chain_copy(chain, D, d + 1, half).wait_recv()
                    arrived = buffers(chain, D, d + 1)[1]
                out = buffers(chain, D, d)[0]
                f = factor(c) if chain == 0 else None
                for h in range(HEADS):
                    if chain == 0:
                        x = ou[c, rows, head(h)] * f[h : h + 1, :]
                    else:
                        x = qu[c, rows, head(h)]
                    if started:
                        x = x + arrived[rows, head(h)].astype(F32)
                    out[rows, head(h)] = x.astype(out.dtype)
                chain_copy(chain, D, d, half).start()

    def chain_sent(chain, i):
        for half in range(2):
            for D in range(2):
                d = (8 if D == chain else 7) - i
                if isinstance(d, int) and d < 1:
                    continue
                chain_copy(chain, D, d, half).wait_send()

    def chain_arrived(chain, D):
        for half in range(2):
            chain_copy(chain, D, 1, half).wait_recv()

    def chain_grads(i):
        for D in range(2):
            d = (8 if D == 1 else 7) - i
            if isinstance(d, int) and d < 1:
                continue
            grads(wrap(me + d) if D == 0 else wrap(me - d))

    def loop(lo, hi, fn):
        def body(t, _):
            fn(t)
            return 0

        lax.fori_loop(lo, hi, body, 0)

    gather_first(0)
    own_scores()
    scores(me)

    def query_step(t):
        gather_step(0, t)
        send_scores(chunk_at(0, t))
        send_scores(chunk_at(1, t))

    loop(1, 7, query_step)
    gather_step(0, 7)
    gather_first(1)
    send_scores(chunk_at(0, 7))
    send_scores(chunk_at(1, 7))
    gather_step(0, 8)
    send_scores(chunk_at(0, 8))

    def grad_step(t):
        gather_step(1, t)
        gather_sent(0, t)
        send_weights_grad(chunk_at(0, t))
        send_weights_grad(chunk_at(1, t))

    loop(1, 4, grad_step)
    combine_logsum()
    weights_grad(me)
    own_weights_grad()
    loop(4, 7, grad_step)
    gather_step(1, 7)
    each_peer(lambda p: to_holder(lse_all, ls_s, ls_r, wrap(me + p), p).wait_recv())
    chain_step(0, 0)
    gather_sent(0, 7)
    gather_sent(0, 8)
    send_weights_grad(chunk_at(0, 7))
    send_weights_grad(chunk_at(1, 7))
    gather_step(1, 8)
    send_weights_grad(chunk_at(1, 8))

    def output_step(i):
        chain_step(0, i)
        gather_sent(1, i)

    loop(1, 3, output_step)
    combine_deltas()
    loop(3, 5, output_step)
    each_peer(lambda p: to_candidate(st_out, st_in, st_s, st_r, wrap(me + p), me).wait_send())
    each_peer(lambda p: to_holder(lse_all, ls_s, ls_r, me, p).wait_send())
    chain_step(0, 5)
    for t in range(5, 9):
        gather_sent(1, t)
    each_peer(lambda p: to_holder(delta_all, dl_s, dl_r, wrap(me + p), p).wait_recv())
    chain_grads(0)
    chain_step(0, 6)
    chain_step(1, 0)
    chain_grads(1)
    chain_step(0, 7)

    def return_step(i):
        chain_step(1, i)
        chain_sent(0, i)
        chain_grads(i + 1)

    loop(1, 3, return_step)
    chain_arrived(0, 0)
    chain_arrived(0, 1)
    f_own = jnp.exp(own_st[:HEADS, :] - lse_all[me, :HEADS, :])
    f_me = factor(me)
    for h in range(HEADS):
        x = own_ou[:, head(h)] * f_own[h : h + 1, :] + ou[me, :, head(h)] * f_me[h : h + 1, :]
        x = x + rf[0, 0, 0, :, head(h)] + rf[0, 1, 0, :, head(h)]
        att_ref[:, head(h)] = x.T.astype(BF16)
    loop(3, 5, return_step)
    chain_step(1, 5)
    chain_grads(6)
    chain_sent(0, 0)
    for i in range(5, 8):
        chain_sent(0, i)
    chain_step(1, 6)
    chain_grads(7)
    chain_step(1, 7)
    grads(me)
    own_grads()
    each_peer(lambda p: to_candidate(del_out, del_in, de_s, de_r, wrap(me + p), me).wait_send())
    each_peer(lambda p: to_holder(delta_all, dl_s, dl_r, me, p).wait_send())
    for i in range(5):
        chain_sent(1, i)
    chain_arrived(1, 0)
    chain_arrived(1, 1)
    for h in range(HEADS):
        x = own_qu[:, head(h)] + qu[me, :, head(h)] + rf[1, 0, 0, :, head(h)] + rf[1, 1, 0, :, head(h)]
        qg_ref[:, head(h)] = (x * SCALE).T.astype(BF16)
    for i in range(5, 8):
        chain_sent(1, i)


def ring(ids, q, k, v, ok, ov, g):
    vm = pl.BlockSpec(memory_space=pltpu.VMEM)
    shape = jax.ShapeDtypeStruct
    V = pltpu.VMEM
    D = pltpu.SemaphoreType.DMA
    stats = V((N, 8, 128), F32)
    return pl.pallas_call(
        ring_kernel,
        in_specs=[pl.BlockSpec(memory_space=pltpu.SMEM)] + [vm] * 6,
        out_specs=[vm] * 6,
        out_shape=[
            shape((128, ROWS), BF16), shape((128, ROWS), BF16),
            shape((BLK, DH), BF16), shape((BLK, DH), BF16),
            shape((N, KEYS, DH), F32), shape((N, KEYS, DH), F32),
        ],
        scratch_shapes=[
            V((N, ROWS, DH), BF16), V((N, ROWS, DH), BF16),
            V((N, KEYS, DH), BF16), V((N, KEYS, DH), BF16),
            V((N, KEYS, ROWS), F32), V((N, KEYS, ROWS), F32),
            V((N, DH, ROWS), F32), V((N, DH, ROWS), F32),
            V((BLK, ROWS), F32), V((BLK, ROWS), F32), V((DH, ROWS), F32), V((DH, ROWS), F32),
            V((8, 128), F32), V((8, 128), F32),
            stats, stats, stats, stats, stats, stats,
            V((KEYS, ROWS), BF16), V((KEYS, ROWS), BF16),
            V((2, 2, FAR - WIDE, DH, ROWS), BF16), V((2, 2, FAR - WIDE, DH, ROWS), BF16),
            V((2, 2, WIDE, DH, ROWS), F32), V((2, 2, WIDE, DH, ROWS), F32),
            D((2, 2, 8, 2)), D((2, 2, 8, 2)), D((2, 2, 8, 2)), D((2, 2, 8, 2)),
            D((N,)), D((N,)), D((N,)), D((N,)), D((N,)), D((N,)), D((N,)), D((N,)),
        ],
        compiler_params=pltpu.CompilerParams(
            collective_id=0, has_side_effects=True, vmem_limit_bytes=60 * 1024 * 1024
        ),
        name="ring_attention",
    )(ids, q, k, v, ok, ov, g)


def sums_kernel(
    ids_ref, att_in, qg_in, okg_in, ovg_in, dks_ref, dvs_ref,
    att_ref, qg_ref, okg_ref, ovg_ref, dk_ref, dv_ref, dk, dv,
):
    low = lax.axis_index("ctx") * CB_DEV
    att_ref[...] = att_in[...]
    qg_ref[...] = qg_in[...]
    okg_ref[...] = okg_in[...]
    ovg_ref[...] = ovg_in[...]
    dk[...] = jnp.zeros_like(dk)
    dv[...] = jnp.zeros_like(dv)

    def add(c, _):
        first, last, count = pick_blocks(ids_ref, c, low)

        @pl.when(count >= 1)
        def _():
            dk[first] += dks_ref[c, :BLK, :]
            dv[first] += dvs_ref[c, :BLK, :]

        @pl.when(count >= 2)
        def _():
            dk[last] += dks_ref[c, BLK:, :]
            dv[last] += dvs_ref[c, BLK:, :]

        return 0

    lax.fori_loop(0, N, add, 0)
    dk_ref[...] = dk[...].astype(BF16)
    dv_ref[...] = dv[...].astype(BF16)


def sums(ids, *parts):
    vm = pl.BlockSpec(memory_space=pltpu.VMEM)
    shape = jax.ShapeDtypeStruct
    return pl.pallas_call(
        sums_kernel,
        in_specs=[pl.BlockSpec(memory_space=pltpu.SMEM)] + [vm] * 6,
        out_specs=[vm] * 6,
        out_shape=[
            shape((128, ROWS), BF16), shape((128, ROWS), BF16),
            shape((BLK, DH), BF16), shape((BLK, DH), BF16),
            shape((CB_DEV, BLK, DH), BF16), shape((CB_DEV, BLK, DH), BF16),
        ],
        scratch_shapes=[pltpu.VMEM((CB_DEV, BLK, DH), F32), pltpu.VMEM((CB_DEV, BLK, DH), F32)],
        compiler_params=pltpu.CompilerParams(vmem_limit_bytes=32 * 1024 * 1024),
        name="block_sums",
    )(ids, *parts)


def on_device(queries, context_keys, context_values, own_keys, own_values, out_grad, block_ids):
    k = context_keys.reshape(CB_DEV, BLK, DH)
    v = context_values.reshape(CB_DEV, BLK, DH)
    parts = ring(block_ids, queries, k, v, own_keys, own_values, out_grad)
    att, qg, okg, ovg, dk, dv = sums(block_ids, *parts)
    return att, qg, dk.reshape(CB_DEV * BLK, DH), dv.reshape(CB_DEV * BLK, DH), okg, ovg


def solution(mesh):
    rows = P(("dp", "ctx"), "head")
    return jax.shard_map(
        on_device,
        mesh=mesh,
        in_specs=(rows,) * 6 + (P("dp", None),),
        out_specs=(rows,) * 6,
        check_vma=False,
    )
```

```python
import math

import jax
import jax.numpy as jnp
from jax import lax
from jax.experimental import pallas as pl
from jax.experimental.pallas import tpu as pltpu
from jax.sharding import PartitionSpec as P

N = 16
BLK = 128
DH = 128
HEADS = 4
ROWS = HEADS * 128
KEYS = 2 * BLK
SLOTS = 24
CB_DEV = 16
EMPTY = 2 * N
SCALE = 1.0 / math.sqrt(DH)
HIDDEN = -1e30
FLOOR = -1e25
WIDE = 2
FAR = 8
F32 = jnp.float32
BF16 = jnp.bfloat16
NT = (((1,), (1,)), ((), ()))
NN = (((1,), (0,)), ((), ()))


def dot(a, b, dims=NN):
    return lax.dot_general(a, b, dims, preferred_element_type=F32)


def wrap(x):
    return lax.rem(x + 2 * N, N)


def head(h):
    return slice(h * 128, (h + 1) * 128)


def is_int(x):
    return isinstance(x, int)


def ring_kernel(
    ids_ref, q_ref, k_ref, v_ref, ok_ref, ov_ref, g_ref,
    att_ref, qg_ref, okg_ref, ovg_ref, dk_ref, dv_ref,
    q_all, g_all, nk, nv, lw, dp, ou, qu,
    own_lw, own_dp, own_ou, own_qu, own_st, own_del,
    st_out, st_in, del_out, del_in, lse_all, delta_all,
    ds_t, p_t, tr, dks, dvs, sel, sb, rb, sf, rf,
    g_send, g_recv, c_send, c_recv, st_s, st_r, de_s, de_r, ls_s, ls_r, dl_s, dl_r,
):
    me = lax.axis_index("ctx")
    low = me * CB_DEV
    nbr = (wrap(me + 1), wrap(me - 1))

    barrier = pltpu.get_barrier_semaphore()

    def loop(lo, hi, fn):
        def body(t, _):
            fn(t)
            return 0

        lax.fori_loop(lo, hi, body, 0)

    def each_peer(fn):
        loop(1, N, fn)

    each_peer(lambda p: pl.semaphore_signal(barrier, inc=1, device_id={"ctx": wrap(me + p)}))
    for h in range(HEADS):
        q_all[me, h] = q_ref[:, head(h)]
        g_all[me, h] = g_ref[:, head(h)]
    pl.semaphore_wait(barrier, N - 1)

    def gather_copy(stream, D, t, h, c):
        part = (q_all, g_all)[stream].at[c, h]
        return pltpu.make_async_remote_copy(
            src_ref=part, dst_ref=part,
            send_sem=g_send.at[stream, D, t - 1, h], recv_sem=g_recv.at[stream, D, t - 1, h],
            device_id={"ctx": nbr[D]},
        )

    def toward(D, d):
        return wrap(me + d) if D == 0 else wrap(me - d)

    def from_behind(D, t):
        return toward(1 - D, t)

    def gather_step(stream, t, work):
        for h in range(HEADS):
            for D in range(2):
                steps = 8 if D == stream else 7
                if is_int(t) and t > steps:
                    continue
                c = from_behind(D, t)
                gather_copy(stream, D, t, h, c).wait_recv()
                if not is_int(t) or t < steps:
                    gather_copy(stream, D, t + 1, h, c).start()
            work(h)

    def gather_first(stream):
        for h in range(HEADS):
            for D in range(2):
                gather_copy(stream, D, 1, h, me).start()

    def gather_sent(stream, t):
        for h in range(HEADS):
            for D in range(2):
                if is_int(t) and t > (8 if D == stream else 7):
                    continue
                gather_copy(stream, D, t, h, me).wait_send()

    def to_candidate(src, dst, send, recv, c, slot):
        return pltpu.make_async_remote_copy(
            src_ref=src.at[c], dst_ref=dst.at[slot], send_sem=send.at[c], recv_sem=recv.at[slot],
            device_id={"ctx": c},
        )

    def to_holder(buf, send, recv, slot, p):
        return pltpu.make_async_remote_copy(
            src_ref=buf.at[slot], dst_ref=buf.at[slot], send_sem=send.at[p], recv_sem=recv.at[slot],
            device_id={"ctx": wrap(me + p)},
        )

    def stage(c, D):
        first = jnp.int32(CB_DEV)
        last = jnp.int32(-1)
        count = jnp.int32(0)
        for j in range(SLOTS):
            b = ids_ref[c, j] - low
            inside = (b >= 0) & (b < CB_DEV)
            first = jnp.where(inside, jnp.minimum(first, b), first)
            last = jnp.where(inside, jnp.maximum(last, b), last)
            count = count + jnp.where(inside, 1, 0)
        sel[c, 0] = jnp.where(count >= 1, first, -1)
        sel[c, 1] = jnp.where(count >= 2, last, -1)
        first = jnp.minimum(first, CB_DEV - 1)
        last = jnp.maximum(last, 0)
        nk[c, :BLK, :] = k_ref[first]
        nk[c, BLK:, :] = k_ref[last]
        nv[c, :BLK, :] = v_ref[first]
        nv[c, BLK:, :] = v_ref[last]
        tr[D] = nv[c].T
        bias0 = jnp.where(count >= 1, 0.0, HIDDEN).astype(F32)
        bias1 = jnp.where(count >= 2, 0.0, HIDDEN).astype(F32)
        return bias0, bias1

    def scores(c, D, h, bias):
        s = dot(nk[c], q_all[c, h], NT) * SCALE
        s0 = s[:BLK] + bias[0]
        s1 = s[BLK:] + bias[1]
        m = jnp.max(jnp.maximum(s0, s1), axis=0, keepdims=True)
        m = jnp.maximum(m, FLOOR)
        e = jnp.exp(jnp.concatenate([s0, s1], axis=0) - m)
        lw[c, h] = e
        st_out[c, h : h + 1, :] = m
        st_out[c, HEADS + h : HEADS + h + 1, :] = jnp.sum(e, axis=0, keepdims=True)
        ou[c, h] = dot(tr[D], e.astype(BF16))

    def weights_grad(c, h):
        d = dot(nv[c], g_all[c, h], NT)
        dp[c, h] = d
        e = lw[c, h].astype(BF16).astype(F32)
        del_out[c, h : h + 1, :] = jnp.sum(e * d, axis=0, keepdims=True)

    def factor(c, h):
        return jnp.exp(st_out[c, h : h + 1, :] - lse_all[c, h : h + 1, :])

    def grads(c, D, h):
        if h == 0:
            tr[D] = nk[c].T
        w = lw[c, h] * factor(c, h)
        p_t[D, :, head(h)] = w.astype(BF16)
        ds = (w * (dp[c, h] - delta_all[c, h : h + 1, :])).astype(BF16)
        ds_t[D, :, head(h)] = ds
        qu[c, h] = dot(tr[D], ds)
        if h % 2 == 1:
            pair = slice((h - 1) * 128, (h + 1) * 128)
            a = dot(ds_t[D, :, pair], q_all[c, h - 1 : h + 1].reshape(256, DH))
            b = dot(p_t[D, :, pair], g_all[c, h - 1 : h + 1].reshape(256, DH))
            for slot in range(2):
                rows = slice(slot * BLK, (slot + 1) * BLK)
                if h == 1:
                    dks[2 * c + slot] = a[rows]
                    dvs[2 * c + slot] = b[rows]
                else:
                    dks[2 * c + slot] += a[rows]
                    dvs[2 * c + slot] += b[rows]

    def own_scores():
        keys = ok_ref[...]
        vt = ov_ref[...].T
        seen = lax.broadcasted_iota(jnp.int32, (BLK, 128), 0) <= lax.broadcasted_iota(jnp.int32, (BLK, 128), 1)
        for h in range(HEADS):
            s = jnp.where(seen, dot(keys, q_all[me, h], NT) * SCALE, HIDDEN)
            m = jnp.max(s, axis=0, keepdims=True)
            e = jnp.exp(s - m)
            own_lw[h] = e
            own_st[h : h + 1, :] = m
            own_st[HEADS + h : HEADS + h + 1, :] = jnp.sum(e, axis=0, keepdims=True)
            own_ou[h] = dot(vt, e.astype(BF16))

    def own_weights_grad(h):
        d = dot(ov_ref[...], g_all[me, h], NT)
        own_dp[h] = d
        e = own_lw[h].astype(BF16).astype(F32)
        own_del[h : h + 1, :] = jnp.sum(e * d, axis=0, keepdims=True)

    def own_factor(h):
        return jnp.exp(own_st[h : h + 1, :] - lse_all[me, h : h + 1, :])

    def own_grads(h):
        w = own_lw[h] * own_factor(h)
        p_t[2, :BLK, head(h)] = w.astype(BF16)
        ds = (w * (own_dp[h] - delta_all[me, h : h + 1, :])).astype(BF16)
        ds_t[2, :BLK, head(h)] = ds
        own_qu[h] = dot(ok_ref[...].T, ds)
        if h == HEADS - 1:
            okg_ref[...] = (dot(ds_t[2, :BLK, :], q_all[me].reshape(ROWS, DH)) * SCALE).astype(BF16)
            ovg_ref[...] = dot(p_t[2, :BLK, :], g_all[me].reshape(ROWS, DH)).astype(BF16)

    def combine_logsum():
        st_in[me] = st_out[me]
        each_peer(lambda p: to_candidate(st_out, st_in, st_s, st_r, wrap(me + p), wrap(me + p)).wait_recv())
        maxima = st_in[:, :HEADS, :]
        totals = st_in[:, HEADS:, :]
        own_max = own_st[:HEADS, :]
        top = jnp.maximum(jnp.max(maxima, axis=0), own_max)
        total = own_st[HEADS:, :] * jnp.exp(own_max - top) + jnp.sum(totals * jnp.exp(maxima - top[None]), axis=0)
        lse_all[me, :HEADS, :] = top + jnp.log(total)
        each_peer(lambda p: to_holder(lse_all, ls_s, ls_r, me, p).start())

    def combine_deltas():
        del_in[me] = del_out[me]
        each_peer(lambda p: to_candidate(del_out, del_in, de_s, de_r, wrap(me + p), wrap(me + p)).wait_recv())
        logsum = lse_all[me, :HEADS, :]
        total = own_del[:HEADS, :] * jnp.exp(own_st[:HEADS, :] - logsum)
        total = total + jnp.sum(del_in[:, :HEADS, :] * jnp.exp(st_in[:, :HEADS, :] - logsum[None]), axis=0)
        delta_all[me, :HEADS, :] = total
        each_peer(lambda p: to_holder(delta_all, dl_s, dl_r, me, p).start())

    def buffers(chain, D, d):
        if is_int(d) and d <= WIDE:
            return sf.at[chain, D, d - 1], rf.at[chain, D, d - 1]
        return sb.at[chain, D, d - 1 - WIDE], rb.at[chain, D, d - 1 - WIDE]

    def chain_copy(chain, D, d, h):
        src, dst = buffers(chain, D, d)
        return pltpu.make_async_remote_copy(
            src_ref=src.at[h], dst_ref=dst.at[h],
            send_sem=c_send.at[chain, D, d - 1, h], recv_sem=c_recv.at[chain, D, d - 1, h],
            device_id={"ctx": nbr[D]},
        )

    def dists(chain, i):
        for D in range(2):
            d = (8 if D == chain else 7) - i
            if not is_int(d) or d >= 1:
                yield D, d

    def chain_head(chain, i, h):
        for D, d in dists(chain, i):
            c = toward(D, d)
            x = ou[c, h] * factor(c, h) if chain == 0 else qu[c, h]
            if not is_int(i) or i > 0:
                chain_copy(chain, D, d + 1, h).wait_recv()
                x = x + buffers(chain, D, d + 1)[1][h].astype(F32)
            out = buffers(chain, D, d)[0]
            out[h] = x.astype(out.dtype)
            chain_copy(chain, D, d, h).start()

    def chain_step(chain, i, work=lambda h: None):
        for h in range(HEADS):
            chain_head(chain, i, h)
            work(h)

    def chain_sent(chain, i):
        for h in range(HEADS):
            for D, d in dists(chain, i):
                chain_copy(chain, D, d, h).wait_send()

    def chain_grads(i, h):
        for D, d in dists(1, i):
            grads(toward(D, d), D, h)

    def block_sum(b):
        a = jnp.zeros((BLK, DH), F32)
        g = jnp.zeros((BLK, DH), F32)
        for c in range(N):
            at = jnp.where(sel[c, 0] == b, 2 * c, jnp.where(sel[c, 1] == b, 2 * c + 1, EMPTY))
            a = a + dks[at]
            g = g + dvs[at]
        dk_ref[b] = (a * SCALE).astype(BF16)
        dv_ref[b] = g.astype(BF16)

    gather_first(0)
    own_scores()
    bias_me = stage(me, 0)
    for h in range(HEADS):
        scores(me, 0, h, bias_me)

    def query_step(t):
        bias = {}

        def work(h):
            for D in range(2):
                if is_int(t) and D == 1 and t > 7:
                    continue
                c = from_behind(D, t)
                if h == 0:
                    bias[D] = stage(c, D)
                scores(c, D, h, bias[D])
                if h == HEADS - 1:
                    to_candidate(st_out, st_in, st_s, st_r, c, me).start()

        gather_step(0, t, work)

    loop(1, 7, query_step)
    query_step(7)
    gather_first(1)
    query_step(8)

    def grad_step(t, then=lambda h: None):
        def work(h):
            for D in range(2):
                if is_int(t) and D == 0 and t > 7:
                    continue
                c = from_behind(D, t)
                weights_grad(c, h)
                if h == HEADS - 1:
                    to_candidate(del_out, del_in, de_s, de_r, c, me).start()
            then(h)

        gather_step(1, t, work)
        if not is_int(t):
            gather_sent(0, t)

    loop(1, 4, grad_step)
    combine_logsum()
    dks[EMPTY] = jnp.zeros((BLK, DH), F32)
    dvs[EMPTY] = jnp.zeros((BLK, DH), F32)

    def own_too(h):
        weights_grad(me, h)
        own_weights_grad(h)

    loop(4, 6, grad_step)
    grad_step(6, own_too)
    each_peer(lambda p: to_holder(lse_all, ls_s, ls_r, wrap(me + p), p).wait_recv())
    grad_step(7, lambda h: chain_head(0, 0, h))
    grad_step(8)

    def output_step(i):
        chain_step(0, i)
        gather_sent(1, i)

    loop(1, 3, output_step)
    combine_deltas()
    loop(3, 5, output_step)
    each_peer(lambda p: to_candidate(st_out, st_in, st_s, st_r, wrap(me + p), me).wait_send())
    each_peer(lambda p: to_holder(lse_all, ls_s, ls_r, me, p).wait_send())
    each_peer(lambda p: to_holder(delta_all, dl_s, dl_r, wrap(me + p), p).wait_recv())
    chain_step(0, 5, lambda h: chain_grads(0, h))

    def both(h):
        chain_head(1, 0, h)
        chain_grads(1, h)

    chain_step(0, 6, both)
    chain_step(0, 7, lambda h: chain_grads(2, h))

    def return_step(i):
        chain_step(1, i, lambda h: chain_grads(i + 2, h))

    loop(1, 5, return_step)

    def finish_output(h):
        x = own_ou[h] * own_factor(h) + ou[me, h] * factor(me, h)
        for D in range(2):
            chain_copy(0, D, 1, h).wait_recv()
            x = x + rf[0, D, 0, h]
        att_ref[:, head(h)] = x.T.astype(BF16)

    def step5(h):
        chain_grads(7, h)
        grads(me, 0, h)
        own_grads(h)
        finish_output(h)

    chain_step(1, 5, step5)

    def step6(h):
        block_sum(2 * h)
        block_sum(2 * h + 1)

    chain_step(1, 6, step6)

    def step7(h):
        block_sum(8 + 2 * h)
        block_sum(9 + 2 * h)

    chain_step(1, 7, step7)
    for t in range(6, 9):
        gather_sent(0, t)
    for t in range(5, 9):
        gather_sent(1, t)
    for i in range(8):
        chain_sent(0, i)
    each_peer(lambda p: to_candidate(del_out, del_in, de_s, de_r, wrap(me + p), me).wait_send())
    each_peer(lambda p: to_holder(delta_all, dl_s, dl_r, me, p).wait_send())
    for i in range(6):
        chain_sent(1, i)
    for h in range(HEADS):
        x = own_qu[h] + qu[me, h]
        for D in range(2):
            chain_copy(1, D, 1, h).wait_recv()
            x = x + rf[1, D, 0, h]
        qg_ref[:, head(h)] = (x * SCALE).T.astype(BF16)
    for i in range(6, 8):
        chain_sent(1, i)


def ring(ids, q, k, v, ok, ov, g):
    vm = pl.BlockSpec(memory_space=pltpu.VMEM)
    shape = jax.ShapeDtypeStruct
    V = pltpu.VMEM
    D = pltpu.SemaphoreType.DMA
    stats = V((N, 8, 128), F32)
    tile = (HEADS, 128, 128)
    return pl.pallas_call(
        ring_kernel,
        in_specs=[pl.BlockSpec(memory_space=pltpu.SMEM)] + [vm] * 6,
        out_specs=[vm] * 6,
        out_shape=[
            shape((128, ROWS), BF16), shape((128, ROWS), BF16),
            shape((BLK, DH), BF16), shape((BLK, DH), BF16),
            shape((CB_DEV, BLK, DH), BF16), shape((CB_DEV, BLK, DH), BF16),
        ],
        scratch_shapes=[
            V((N,) + tile, BF16), V((N,) + tile, BF16),
            V((N, KEYS, DH), BF16), V((N, KEYS, DH), BF16),
            V((N, HEADS, KEYS, 128), F32), V((N, HEADS, KEYS, 128), F32),
            V((N,) + tile, F32), V((N,) + tile, F32),
            V(tile, F32), V(tile, F32), V(tile, F32), V(tile, F32),
            V((8, 128), F32), V((8, 128), F32),
            stats, stats, stats, stats, stats, stats,
            V((3, KEYS, ROWS), BF16), V((3, KEYS, ROWS), BF16), V((2, DH, KEYS), BF16),
            V((2 * N + 1, BLK, DH), F32), V((2 * N + 1, BLK, DH), F32),
            pltpu.SMEM((N, 2), jnp.int32),
            V((2, 2, FAR - WIDE) + tile, BF16), V((2, 2, FAR - WIDE) + tile, BF16),
            V((2, 2, WIDE) + tile, F32), V((2, 2, WIDE) + tile, F32),
            D((2, 2, 8, HEADS)), D((2, 2, 8, HEADS)), D((2, 2, 8, HEADS)), D((2, 2, 8, HEADS)),
            D((N,)), D((N,)), D((N,)), D((N,)), D((N,)), D((N,)), D((N,)), D((N,)),
        ],
        compiler_params=pltpu.CompilerParams(
            collective_id=0, has_side_effects=True, vmem_limit_bytes=60 * 1024 * 1024
        ),
        name="ring_attention",
    )(ids, q, k, v, ok, ov, g)


def hand_on_kernel(*refs):
    n = len(refs) // 2
    copies = [pltpu.make_async_copy(refs[j], refs[n + j], refs[2 * n].at[j]) for j in range(n)]
    for copy in copies:
        copy.start()
    for copy in copies:
        copy.wait()


def hand_on(parts):
    hbm = pl.BlockSpec(memory_space=pl.ANY)
    return pl.pallas_call(
        hand_on_kernel,
        in_specs=[hbm] * len(parts),
        out_specs=[hbm] * len(parts),
        out_shape=[jax.ShapeDtypeStruct(x.shape, x.dtype) for x in parts],
        scratch_shapes=[pltpu.SemaphoreType.DMA((len(parts),))],
        compiler_params=pltpu.CompilerParams(vmem_limit_bytes=60 * 1024 * 1024),
        name="hand_on",
    )(*parts)


def on_device(queries, context_keys, context_values, own_keys, own_values, out_grad, block_ids):
    k = context_keys.reshape(CB_DEV, BLK, DH)
    v = context_values.reshape(CB_DEV, BLK, DH)
    parts = ring(block_ids, queries, k, v, own_keys, own_values, out_grad)
    att, qg, okg, ovg, dk, dv = hand_on(parts)
    return att, qg, dk.reshape(CB_DEV * BLK, DH), dv.reshape(CB_DEV * BLK, DH), okg, ovg


def solution(mesh):
    rows = P(("dp", "ctx"), "head")
    return jax.shard_map(
        on_device,
        mesh=mesh,
        in_specs=(rows,) * 6 + (P("dp", None),),
        out_specs=(rows,) * 6,
        check_vma=False,
    )
```

```python
import math

import jax
import jax.numpy as jnp
from jax import lax
from jax.experimental import pallas as pl
from jax.experimental.pallas import tpu as pltpu
from jax.sharding import PartitionSpec as P

N = 16
BLK = 128
DH = 128
HEADS = 4
ROWS = HEADS * 128
KEYS = 2 * BLK
SLOTS = 24
CB_DEV = 16
EMPTY = 2 * N
SCALE = 1.0 / math.sqrt(DH)
HIDDEN = -1e30
FLOOR = -1e25
WIDE = 2
FAR = 8
LAG = 2
F32 = jnp.float32
BF16 = jnp.bfloat16
NT = (((1,), (1,)), ((), ()))
NN = (((1,), (0,)), ((), ()))


def dot(a, b, dims=NN):
    return lax.dot_general(a, b, dims, preferred_element_type=F32)


def wrap(x):
    return lax.rem(x + 2 * N, N)


def head(h):
    return slice(h * 128, (h + 1) * 128)


def is_int(x):
    return isinstance(x, int)


def ring_kernel(
    ids_ref, q_ref, k_ref, v_ref, ok_ref, ov_ref, g_ref,
    att_ref, qg_ref, okg_ref, ovg_ref, dk_ref, dv_ref,
    q_all, g_all, nk, nv, lw, dp, ou, qu,
    own_lw, own_dp, own_ou, own_qu, own_st, own_del,
    st_out, st_in, del_out, del_in, lse_all, delta_all,
    ds_t, p_t, tr, dks, dvs, sel, sb, rb, sf, rf,
    g_send, g_recv, c_send, c_recv, st_s, st_r, de_s, de_r, ls_s, ls_r, dl_s, dl_r,
):
    me = lax.axis_index("ctx")
    low = me * CB_DEV
    nbr = (wrap(me + 1), wrap(me - 1))

    barrier = pltpu.get_barrier_semaphore()

    def loop(lo, hi, fn):
        def body(t, _):
            fn(t)
            return 0

        lax.fori_loop(lo, hi, body, 0)

    def each_peer(fn):
        loop(1, N, fn)

    each_peer(lambda p: pl.semaphore_signal(barrier, inc=1, device_id={"ctx": wrap(me + p)}))
    for h in range(HEADS):
        q_all[me, h] = q_ref[:, head(h)]
        g_all[me, h] = g_ref[:, head(h)]
    pl.semaphore_wait(barrier, N - 1)

    def gather_copy(stream, D, t, h, c):
        part = (q_all, g_all)[stream].at[c, h]
        return pltpu.make_async_remote_copy(
            src_ref=part, dst_ref=part,
            send_sem=g_send.at[stream, D, t - 1, h], recv_sem=g_recv.at[stream, D, t - 1, h],
            device_id={"ctx": nbr[D]},
        )

    def toward(D, d):
        return wrap(me + d) if D == 0 else wrap(me - d)

    def from_behind(D, t):
        return toward(1 - D, t)

    def gather_head(stream, t, h):
        for D in range(2):
            steps = 8 if D == stream else 7
            if is_int(t) and t > steps:
                continue
            c = from_behind(D, t)
            gather_copy(stream, D, t, h, c).wait_recv()
            if not is_int(t) or t < steps:
                gather_copy(stream, D, t + 1, h, c).start()

    def gather_first(stream, h):
        for D in range(2):
            gather_copy(stream, D, 1, h, me).start()

    def gather_sent(stream, t):
        for h in range(HEADS):
            for D in range(2):
                if is_int(t) and t > (8 if D == stream else 7):
                    continue
                gather_copy(stream, D, t, h, me).wait_send()

    def to_candidate(src, dst, send, recv, c, slot):
        return pltpu.make_async_remote_copy(
            src_ref=src.at[c], dst_ref=dst.at[slot], send_sem=send.at[c], recv_sem=recv.at[slot],
            device_id={"ctx": c},
        )

    def to_holder(buf, send, recv, slot, p):
        return pltpu.make_async_remote_copy(
            src_ref=buf.at[slot], dst_ref=buf.at[slot], send_sem=send.at[p], recv_sem=recv.at[slot],
            device_id={"ctx": wrap(me + p)},
        )

    def stage(c, D):
        first = jnp.int32(CB_DEV)
        last = jnp.int32(-1)
        count = jnp.int32(0)
        for j in range(SLOTS):
            b = ids_ref[c, j] - low
            inside = (b >= 0) & (b < CB_DEV)
            first = jnp.where(inside, jnp.minimum(first, b), first)
            last = jnp.where(inside, jnp.maximum(last, b), last)
            count = count + jnp.where(inside, 1, 0)
        sel[c, 0] = jnp.where(count >= 1, first, -1)
        sel[c, 1] = jnp.where(count >= 2, last, -1)
        first = jnp.minimum(first, CB_DEV - 1)
        last = jnp.maximum(last, 0)
        nk[c, :BLK, :] = k_ref[first]
        nk[c, BLK:, :] = k_ref[last]
        nv[c, :BLK, :] = v_ref[first]
        nv[c, BLK:, :] = v_ref[last]
        tr[D] = nv[c].T
        bias0 = jnp.where(count >= 1, 0.0, HIDDEN).astype(F32)
        bias1 = jnp.where(count >= 2, 0.0, HIDDEN).astype(F32)
        return bias0, bias1

    def scores(c, D, h, bias):
        s = dot(nk[c], q_all[c, h], NT) * SCALE
        s0 = s[:BLK] + bias[0]
        s1 = s[BLK:] + bias[1]
        m = jnp.max(jnp.maximum(s0, s1), axis=0, keepdims=True)
        m = jnp.maximum(m, FLOOR)
        e = jnp.exp(jnp.concatenate([s0, s1], axis=0) - m)
        lw[c, h] = e
        st_out[c, h : h + 1, :] = m
        st_out[c, HEADS + h : HEADS + h + 1, :] = jnp.sum(e, axis=0, keepdims=True)
        ou[c, h] = dot(tr[D], e.astype(BF16))

    def weights_grad(c, h):
        d = dot(nv[c], g_all[c, h], NT)
        dp[c, h] = d
        e = lw[c, h].astype(BF16).astype(F32)
        del_out[c, h : h + 1, :] = jnp.sum(e * d, axis=0, keepdims=True)

    def factor(c, h):
        return jnp.exp(st_out[c, h : h + 1, :] - lse_all[c, h : h + 1, :])

    def grads(c, D, h):
        if h == 0:
            tr[D] = nk[c].T
        w = lw[c, h] * factor(c, h)
        p_t[D, :, head(h)] = w.astype(BF16)
        ds = (w * (dp[c, h] - delta_all[c, h : h + 1, :])).astype(BF16)
        ds_t[D, :, head(h)] = ds
        qu[c, h] = dot(tr[D], ds)
        if h % 2 == 1:
            pair = slice((h - 1) * 128, (h + 1) * 128)
            a = dot(ds_t[D, :, pair], q_all[c, h - 1 : h + 1].reshape(256, DH))
            b = dot(p_t[D, :, pair], g_all[c, h - 1 : h + 1].reshape(256, DH))
            for slot in range(2):
                rows = slice(slot * BLK, (slot + 1) * BLK)
                if h == 1:
                    dks[2 * c + slot] = a[rows]
                    dvs[2 * c + slot] = b[rows]
                else:
                    dks[2 * c + slot] += a[rows]
                    dvs[2 * c + slot] += b[rows]

    def own_scores():
        keys = ok_ref[...]
        vt = ov_ref[...].T
        seen = lax.broadcasted_iota(jnp.int32, (BLK, 128), 0) <= lax.broadcasted_iota(jnp.int32, (BLK, 128), 1)
        for h in range(HEADS):
            s = jnp.where(seen, dot(keys, q_all[me, h], NT) * SCALE, HIDDEN)
            m = jnp.max(s, axis=0, keepdims=True)
            e = jnp.exp(s - m)
            own_lw[h] = e
            own_st[h : h + 1, :] = m
            own_st[HEADS + h : HEADS + h + 1, :] = jnp.sum(e, axis=0, keepdims=True)
            own_ou[h] = dot(vt, e.astype(BF16))

    def own_weights_grad(h):
        d = dot(ov_ref[...], g_all[me, h], NT)
        own_dp[h] = d
        e = own_lw[h].astype(BF16).astype(F32)
        own_del[h : h + 1, :] = jnp.sum(e * d, axis=0, keepdims=True)

    def own_factor(h):
        return jnp.exp(own_st[h : h + 1, :] - lse_all[me, h : h + 1, :])

    def own_grads(h):
        w = own_lw[h] * own_factor(h)
        p_t[2, :BLK, head(h)] = w.astype(BF16)
        ds = (w * (own_dp[h] - delta_all[me, h : h + 1, :])).astype(BF16)
        ds_t[2, :BLK, head(h)] = ds
        own_qu[h] = dot(ok_ref[...].T, ds)
        if h == HEADS - 1:
            okg_ref[...] = (dot(ds_t[2, :BLK, :], q_all[me].reshape(ROWS, DH)) * SCALE).astype(BF16)
            ovg_ref[...] = dot(p_t[2, :BLK, :], g_all[me].reshape(ROWS, DH)).astype(BF16)

    def combine_logsum():
        st_in[me] = st_out[me]
        each_peer(lambda p: to_candidate(st_out, st_in, st_s, st_r, wrap(me + p), wrap(me + p)).wait_recv())
        maxima = st_in[:, :HEADS, :]
        totals = st_in[:, HEADS:, :]
        own_max = own_st[:HEADS, :]
        top = jnp.maximum(jnp.max(maxima, axis=0), own_max)
        total = own_st[HEADS:, :] * jnp.exp(own_max - top) + jnp.sum(totals * jnp.exp(maxima - top[None]), axis=0)
        lse_all[me, :HEADS, :] = top + jnp.log(total)
        each_peer(lambda p: to_holder(lse_all, ls_s, ls_r, me, p).start())

    def combine_deltas():
        del_in[me] = del_out[me]
        each_peer(lambda p: to_candidate(del_out, del_in, de_s, de_r, wrap(me + p), wrap(me + p)).wait_recv())
        logsum = lse_all[me, :HEADS, :]
        total = own_del[:HEADS, :] * jnp.exp(own_st[:HEADS, :] - logsum)
        total = total + jnp.sum(del_in[:, :HEADS, :] * jnp.exp(st_in[:, :HEADS, :] - logsum[None]), axis=0)
        delta_all[me, :HEADS, :] = total
        each_peer(lambda p: to_holder(delta_all, dl_s, dl_r, me, p).start())

    def buffers(chain, D, d):
        if is_int(d) and d <= WIDE:
            return sf.at[chain, D, d - 1], rf.at[chain, D, d - 1]
        return sb.at[chain, D, d - 1 - WIDE], rb.at[chain, D, d - 1 - WIDE]

    def chain_copy(chain, D, d, h):
        src, dst = buffers(chain, D, d)
        return pltpu.make_async_remote_copy(
            src_ref=src.at[h], dst_ref=dst.at[h],
            send_sem=c_send.at[chain, D, d - 1, h], recv_sem=c_recv.at[chain, D, d - 1, h],
            device_id={"ctx": nbr[D]},
        )

    def dists(chain, i):
        for D in range(2):
            d = (8 if D == chain else 7) - i
            if not is_int(d) or d >= 1:
                yield D, d

    def chain_head(chain, i, h):
        for D, d in dists(chain, i):
            c = toward(D, d)
            x = ou[c, h] * factor(c, h) if chain == 0 else qu[c, h]
            if not is_int(i) or i > 0:
                chain_copy(chain, D, d + 1, h).wait_recv()
                x = x + buffers(chain, D, d + 1)[1][h].astype(F32)
            out = buffers(chain, D, d)[0]
            out[h] = x.astype(out.dtype)
            chain_copy(chain, D, d, h).start()

    def chain_sent(chain, i):
        for h in range(HEADS):
            for D, d in dists(chain, i):
                chain_copy(chain, D, d, h).wait_send()

    def chain_grads(i, h):
        for D, d in dists(1, i):
            grads(toward(D, d), D, h)

    def block_sum(b):
        a = jnp.zeros((BLK, DH), F32)
        g = jnp.zeros((BLK, DH), F32)
        for c in range(N):
            at = jnp.where(sel[c, 0] == b, 2 * c, jnp.where(sel[c, 1] == b, 2 * c + 1, EMPTY))
            a = a + dks[at]
            g = g + dvs[at]
        dk_ref[b] = (a * SCALE).astype(BF16)
        dv_ref[b] = g.astype(BF16)

    def query_work(t, bias, h):
        for D in range(2):
            if is_int(t) and D == 1 and t > 7:
                continue
            c = from_behind(D, t)
            if h == 0:
                bias[D] = stage(c, D)
            scores(c, D, h, bias[D])
            if h == HEADS - 1:
                to_candidate(st_out, st_in, st_s, st_r, c, me).start()

    def grad_work(t, h):
        for D in range(2):
            if is_int(t) and D == 0 and t > 7:
                continue
            c = from_behind(D, t)
            weights_grad(c, h)
            if h == HEADS - 1:
                to_candidate(del_out, del_in, de_s, de_r, c, me).start()

    def gather_slot(s, extra=lambda h: None):
        bias = {}
        for h in range(HEADS):
            if not is_int(s) or s <= 8:
                gather_head(0, s, h)
            if not is_int(s) or s > LAG:
                gather_head(1, s - LAG, h)
            elif s == LAG:
                gather_first(1, h)
            if not is_int(s) or s <= 8:
                query_work(s, bias, h)
            if not is_int(s) or s > LAG:
                grad_work(s - LAG, h)
            extra(h)

    for h in range(HEADS):
        gather_first(0, h)
    own_scores()
    bias_me = stage(me, 0)
    for h in range(HEADS):
        scores(me, 0, h, bias_me)
    for s in range(1, LAG + 1):
        gather_slot(s)
    loop(LAG + 1, 7, gather_slot)

    def own_too(h):
        weights_grad(me, h)
        own_weights_grad(h)

    dks[EMPTY] = jnp.zeros((BLK, DH), F32)
    dvs[EMPTY] = jnp.zeros((BLK, DH), F32)
    gather_slot(7)
    gather_slot(8)
    for s in range(9, 8 + LAG):
        gather_slot(s, own_too if s == 9 else lambda h: None)
    combine_logsum()
    gather_slot(8 + LAG)
    each_peer(lambda p: to_holder(lse_all, ls_s, ls_r, wrap(me + p), p).wait_recv())

    for h in range(HEADS):
        chain_head(0, 0, h)
    for t in range(1, 5):
        gather_sent(0, t)
    for h in range(HEADS):
        chain_head(0, 1, h)
    for t in range(5, 9):
        gather_sent(0, t)
    combine_deltas()
    for h in range(HEADS):
        chain_head(0, 2, h)
    each_peer(lambda p: to_holder(delta_all, dl_s, dl_r, wrap(me + p), p).wait_recv())
    for h in range(HEADS):
        chain_grads(0, h)
        chain_head(1, 0, h)
    for h in range(HEADS):
        chain_grads(1, h)

    def chain_slot(u):
        for h in range(HEADS):
            if not is_int(u) or u < 8:
                chain_head(0, u, h)
            chain_head(1, u - 2, h)
            chain_grads(u - 1, h)

    loop(3, 5, chain_slot)
    chain_slot(5)
    for t in range(1, 9):
        gather_sent(1, t)
    chain_slot(6)
    each_peer(lambda p: to_candidate(st_out, st_in, st_s, st_r, wrap(me + p), me).wait_send())
    each_peer(lambda p: to_holder(lse_all, ls_s, ls_r, me, p).wait_send())
    chain_slot(7)
    each_peer(lambda p: to_candidate(del_out, del_in, de_s, de_r, wrap(me + p), me).wait_send())
    each_peer(lambda p: to_holder(delta_all, dl_s, dl_r, me, p).wait_send())
    for h in range(HEADS):
        chain_head(1, 6, h)
        chain_grads(7, h)
        grads(me, 0, h)
        own_grads(h)
    for h in range(HEADS):
        x = own_ou[h] * own_factor(h) + ou[me, h] * factor(me, h)
        for D in range(2):
            chain_copy(0, D, 1, h).wait_recv()
            x = x + rf[0, D, 0, h]
        att_ref[:, head(h)] = x.T.astype(BF16)
        chain_head(1, 7, h)
    loop(0, CB_DEV, block_sum)
    for i in range(8):
        chain_sent(0, i)
    for i in range(6):
        chain_sent(1, i)
    for h in range(HEADS):
        x = own_qu[h] + qu[me, h]
        for D in range(2):
            chain_copy(1, D, 1, h).wait_recv()
            x = x + rf[1, D, 0, h]
        qg_ref[:, head(h)] = (x * SCALE).T.astype(BF16)
    for i in range(6, 8):
        chain_sent(1, i)


def ring(ids, q, k, v, ok, ov, g):
    vm = pl.BlockSpec(memory_space=pltpu.VMEM)
    shape = jax.ShapeDtypeStruct
    V = pltpu.VMEM
    D = pltpu.SemaphoreType.DMA
    stats = V((N, 8, 128), F32)
    tile = (HEADS, 128, 128)
    return pl.pallas_call(
        ring_kernel,
        in_specs=[pl.BlockSpec(memory_space=pltpu.SMEM)] + [vm] * 6,
        out_specs=[vm] * 6,
        out_shape=[
            shape((128, ROWS), BF16), shape((128, ROWS), BF16),
            shape((BLK, DH), BF16), shape((BLK, DH), BF16),
            shape((CB_DEV, BLK, DH), BF16), shape((CB_DEV, BLK, DH), BF16),
        ],
        scratch_shapes=[
            V((N,) + tile, BF16), V((N,) + tile, BF16),
            V((N, KEYS, DH), BF16), V((N, KEYS, DH), BF16),
            V((N, HEADS, KEYS, 128), F32), V((N, HEADS, KEYS, 128), F32),
            V((N,) + tile, F32), V((N,) + tile, F32),
            V(tile, F32), V(tile, F32), V(tile, F32), V(tile, F32),
            V((8, 128), F32), V((8, 128), F32),
            stats, stats, stats, stats, stats, stats,
            V((3, KEYS, ROWS), BF16), V((3, KEYS, ROWS), BF16), V((2, DH, KEYS), BF16),
            V((2 * N + 1, BLK, DH), F32), V((2 * N + 1, BLK, DH), F32),
            pltpu.SMEM((N, 2), jnp.int32),
            V((2, 2, FAR - WIDE) + tile, BF16), V((2, 2, FAR - WIDE) + tile, BF16),
            V((2, 2, WIDE) + tile, F32), V((2, 2, WIDE) + tile, F32),
            D((2, 2, 8, HEADS)), D((2, 2, 8, HEADS)), D((2, 2, 8, HEADS)), D((2, 2, 8, HEADS)),
            D((N,)), D((N,)), D((N,)), D((N,)), D((N,)), D((N,)), D((N,)), D((N,)),
        ],
        compiler_params=pltpu.CompilerParams(
            collective_id=0, has_side_effects=True, vmem_limit_bytes=60 * 1024 * 1024
        ),
        name="ring_attention",
    )(ids, q, k, v, ok, ov, g)


def hand_on_kernel(*refs):
    n = len(refs) // 2
    for j in range(n):
        refs[n + j][...] = refs[j][...]


def hand_on(parts):
    vm = pl.BlockSpec(memory_space=pltpu.VMEM)
    return pl.pallas_call(
        hand_on_kernel,
        in_specs=[vm] * len(parts),
        out_specs=[vm] * len(parts),
        out_shape=[jax.ShapeDtypeStruct(x.shape, x.dtype) for x in parts],
        compiler_params=pltpu.CompilerParams(vmem_limit_bytes=60 * 1024 * 1024),
        name="hand_on",
    )(*parts)


def on_device(queries, context_keys, context_values, own_keys, own_values, out_grad, block_ids):
    k = context_keys.reshape(CB_DEV, BLK, DH)
    v = context_values.reshape(CB_DEV, BLK, DH)
    parts = ring(block_ids, queries, k, v, own_keys, own_values, out_grad)
    att, qg, okg, ovg, dk, dv = hand_on(parts)
    return att, qg, dk.reshape(CB_DEV * BLK, DH), dv.reshape(CB_DEV * BLK, DH), okg, ovg


def solution(mesh):
    rows = P(("dp", "ctx"), "head")
    return jax.shard_map(
        on_device,
        mesh=mesh,
        in_specs=(rows,) * 6 + (P("dp", None),),
        out_specs=(rows,) * 6,
        check_vma=False,
    )
```

```python
import math

import jax
import jax.numpy as jnp
from jax import lax
from jax.experimental import pallas as pl
from jax.experimental.pallas import tpu as pltpu
from jax.sharding import PartitionSpec as P

N = 16
BLK = 128
DH = 128
HEADS = 4
ROWS = HEADS * 128
KEYS = 2 * BLK
SLOTS = 24
CB_DEV = 16
EMPTY = 2 * N
SCALE = 1.0 / math.sqrt(DH)
HIDDEN = -1e30
FLOOR = -1e25
WIDE = 2
FAR = 8
LAG = 2
F32 = jnp.float32
BF16 = jnp.bfloat16
NT = (((1,), (1,)), ((), ()))
NN = (((1,), (0,)), ((), ()))


def dot(a, b, dims=NN):
    return lax.dot_general(a, b, dims, preferred_element_type=F32)


def wrap(x):
    return lax.rem(x + 2 * N, N)


def head(h):
    return slice(h * 128, (h + 1) * 128)


def is_int(x):
    return isinstance(x, int)


def ring_kernel(
    ids_ref, q_ref, k_ref, v_ref, ok_ref, ov_ref, g_ref,
    att_ref, qg_ref, okg_ref, ovg_ref, dk_ref, dv_ref,
    q_all, g_all, nk, nv, lw, dp, ou, qu,
    own_lw, own_dp, own_ou, own_qu, own_st, own_del,
    st_out, st_in, del_out, del_in, lse_all, delta_all, fac,
    ds_t, p_t, tr, dks, dvs, sel, sb, rb, sf, rf,
    g_send, g_recv, c_send, c_recv, st_s, st_r, de_s, de_r, ls_s, ls_r, dl_s, dl_r,
):
    me = lax.axis_index("ctx")
    low = me * CB_DEV
    nbr = (wrap(me + 1), wrap(me - 1))

    barrier = pltpu.get_barrier_semaphore()

    def loop(lo, hi, fn):
        def body(t, _):
            fn(t)
            return 0

        lax.fori_loop(lo, hi, body, 0)

    def each_peer(fn):
        loop(1, N, fn)

    each_peer(lambda p: pl.semaphore_signal(barrier, inc=1, device_id={"ctx": wrap(me + p)}))
    for h in range(HEADS):
        q_all[me, h] = q_ref[:, head(h)]
        g_all[me, h] = g_ref[:, head(h)]
    pl.semaphore_wait(barrier, N - 1)

    def gather_copy(stream, D, t, b, c):
        part = (q_all, g_all)[stream].at[c, pl.ds(2 * b, 2)]
        return pltpu.make_async_remote_copy(
            src_ref=part, dst_ref=part,
            send_sem=g_send.at[stream, D, t - 1, b], recv_sem=g_recv.at[stream, D, t - 1, b],
            device_id={"ctx": nbr[D]},
        )

    def toward(D, d):
        return wrap(me + d) if D == 0 else wrap(me - d)

    def from_behind(D, t):
        return toward(1 - D, t)

    def ways(d, b):
        return (b,) if is_int(d) and d == FAR else () if is_int(d) and d > FAR else (0, 1)

    def behind(t):
        if is_int(t) and t == FAR:
            return ((wrap(me + FAR), 0),)
        return ((from_behind(0, t), 0), (from_behind(1, t), 1))

    def gather_step(stream, t):
        for b in range(2):
            for D in ways(t, b):
                gather_copy(stream, D, t, b, from_behind(D, t)).wait_recv()
            for D in ways(t + 1, b):
                gather_copy(stream, D, t + 1, b, from_behind(D, t)).start()

    def gather_first(stream):
        for b in range(2):
            for D in range(2):
                gather_copy(stream, D, 1, b, me).start()

    def gather_sent(stream, t):
        for b in range(2):
            for D in ways(t, b):
                gather_copy(stream, D, t, b, me).wait_send()

    def to_candidate(src, dst, send, recv, c, slot):
        return pltpu.make_async_remote_copy(
            src_ref=src.at[c], dst_ref=dst.at[slot], send_sem=send.at[c], recv_sem=recv.at[slot],
            device_id={"ctx": c},
        )

    def to_holder(buf, send, recv, slot, p):
        return pltpu.make_async_remote_copy(
            src_ref=buf.at[slot], dst_ref=buf.at[slot], send_sem=send.at[p], recv_sem=recv.at[slot],
            device_id={"ctx": wrap(me + p)},
        )

    def stage(c, D):
        first = jnp.int32(CB_DEV)
        last = jnp.int32(-1)
        count = jnp.int32(0)
        for j in range(SLOTS):
            b = ids_ref[c, j] - low
            inside = (b >= 0) & (b < CB_DEV)
            first = jnp.where(inside, jnp.minimum(first, b), first)
            last = jnp.where(inside, jnp.maximum(last, b), last)
            count = count + jnp.where(inside, 1, 0)
        sel[c, 0] = jnp.where(count >= 1, first, -1)
        sel[c, 1] = jnp.where(count >= 2, last, -1)
        first = jnp.minimum(first, CB_DEV - 1)
        last = jnp.maximum(last, 0)
        nk[c, :BLK, :] = k_ref[first]
        nk[c, BLK:, :] = k_ref[last]
        nv[c, :BLK, :] = v_ref[first]
        nv[c, BLK:, :] = v_ref[last]
        tr[D] = nv[c].T
        bias0 = jnp.where(count >= 1, 0.0, HIDDEN).astype(F32)
        bias1 = jnp.where(count >= 2, 0.0, HIDDEN).astype(F32)
        return bias0, bias1

    def scores(c, D, h, bias):
        s = dot(nk[c], q_all[c, h], NT) * SCALE
        s0 = s[:BLK] + bias[0]
        s1 = s[BLK:] + bias[1]
        m = jnp.max(jnp.maximum(s0, s1), axis=0, keepdims=True)
        m = jnp.maximum(m, FLOOR)
        e = jnp.exp(jnp.concatenate([s0, s1], axis=0) - m)
        lw[c, h] = e
        st_out[c, h : h + 1, :] = m
        st_out[c, HEADS + h : HEADS + h + 1, :] = jnp.sum(e, axis=0, keepdims=True)
        ou[c, h] = dot(tr[D], e.astype(BF16))

    def weights_grad(c, h):
        d = dot(nv[c], g_all[c, h], NT)
        dp[c, h] = d
        e = lw[c, h].astype(BF16).astype(F32)
        del_out[c, h : h + 1, :] = jnp.sum(e * d, axis=0, keepdims=True)

    def grads(c, D):
        tr[D] = nk[c].T
        for h in range(HEADS):
            w = lw[c, h] * fac[c, h : h + 1, :]
            p_t[D, :, head(h)] = w.astype(BF16)
            ds = (w * (dp[c, h] - delta_all[c, h : h + 1, :])).astype(BF16)
            ds_t[D, :, head(h)] = ds
            qu[c, h] = dot(tr[D], ds)
        a = dot(ds_t[D], q_all[c].reshape(ROWS, DH))
        b = dot(p_t[D], g_all[c].reshape(ROWS, DH))
        for slot in range(2):
            rows = slice(slot * BLK, (slot + 1) * BLK)
            dks[2 * c + slot] = a[rows]
            dvs[2 * c + slot] = b[rows]

    def own_scores():
        keys = ok_ref[...]
        vt = ov_ref[...].T
        seen = lax.broadcasted_iota(jnp.int32, (BLK, 128), 0) <= lax.broadcasted_iota(jnp.int32, (BLK, 128), 1)
        for h in range(HEADS):
            s = jnp.where(seen, dot(keys, q_all[me, h], NT) * SCALE, HIDDEN)
            m = jnp.max(s, axis=0, keepdims=True)
            e = jnp.exp(s - m)
            own_lw[h] = e
            own_st[h : h + 1, :] = m
            own_st[HEADS + h : HEADS + h + 1, :] = jnp.sum(e, axis=0, keepdims=True)
            own_ou[h] = dot(vt, e.astype(BF16))

    def own_weights_grad(h):
        d = dot(ov_ref[...], g_all[me, h], NT)
        own_dp[h] = d
        e = own_lw[h].astype(BF16).astype(F32)
        own_del[h : h + 1, :] = jnp.sum(e * d, axis=0, keepdims=True)

    def own_factor(h):
        return jnp.exp(own_st[h : h + 1, :] - lse_all[me, h : h + 1, :])

    def own_grads():
        kt = ok_ref[...].T
        for h in range(HEADS):
            w = own_lw[h] * own_factor(h)
            p_t[2, :BLK, head(h)] = w.astype(BF16)
            ds = (w * (own_dp[h] - delta_all[me, h : h + 1, :])).astype(BF16)
            ds_t[2, :BLK, head(h)] = ds
            own_qu[h] = dot(kt, ds)
        okg_ref[...] = (dot(ds_t[2, :BLK, :], q_all[me].reshape(ROWS, DH)) * SCALE).astype(BF16)
        ovg_ref[...] = dot(p_t[2, :BLK, :], g_all[me].reshape(ROWS, DH)).astype(BF16)

    def combine_logsum():
        st_in[me] = st_out[me]
        each_peer(lambda p: to_candidate(st_out, st_in, st_s, st_r, wrap(me + p), wrap(me + p)).wait_recv())
        maxima = st_in[:, :HEADS, :]
        totals = st_in[:, HEADS:, :]
        own_max = own_st[:HEADS, :]
        top = jnp.maximum(jnp.max(maxima, axis=0), own_max)
        total = own_st[HEADS:, :] * jnp.exp(own_max - top) + jnp.sum(totals * jnp.exp(maxima - top[None]), axis=0)
        lse_all[me, :HEADS, :] = top + jnp.log(total)
        each_peer(lambda p: to_holder(lse_all, ls_s, ls_r, me, p).start())

    def combine_deltas():
        del_in[me] = del_out[me]
        each_peer(lambda p: to_candidate(del_out, del_in, de_s, de_r, wrap(me + p), wrap(me + p)).wait_recv())
        logsum = lse_all[me, :HEADS, :]
        total = own_del[:HEADS, :] * jnp.exp(own_st[:HEADS, :] - logsum)
        total = total + jnp.sum(del_in[:, :HEADS, :] * jnp.exp(st_in[:, :HEADS, :] - logsum[None]), axis=0)
        delta_all[me, :HEADS, :] = total
        each_peer(lambda p: to_holder(delta_all, dl_s, dl_r, me, p).start())

    def buffers(chain, D, d):
        if is_int(d) and d <= WIDE:
            return sf.at[chain, D, d - 1], rf.at[chain, D, d - 1]
        return sb.at[chain, D, d - 1 - WIDE], rb.at[chain, D, d - 1 - WIDE]

    def chain_copy(chain, D, d, b):
        src, dst = buffers(chain, D, d)
        return pltpu.make_async_remote_copy(
            src_ref=src.at[pl.ds(2 * b, 2)], dst_ref=dst.at[pl.ds(2 * b, 2)],
            send_sem=c_send.at[chain, D, d - 1, b], recv_sem=c_recv.at[chain, D, d - 1, b],
            device_id={"ctx": nbr[D]},
        )

    def chain_step(chain, i):
        d = FAR - i
        for b in range(2):
            for D in ways(d + 1, b):
                chain_copy(chain, D, d + 1, b).wait_recv()
            for D in ways(d, b):
                c = toward(D, d)
                out = buffers(chain, D, d)[0]
                for h in (2 * b, 2 * b + 1):
                    x = ou[c, h] * fac[c, h : h + 1, :] if chain == 0 else qu[c, h]
                    if D in ways(d + 1, b):
                        x = x + buffers(chain, D, d + 1)[1][h].astype(F32)
                    out[h] = x.astype(out.dtype)
            for D in ways(d, b):
                chain_copy(chain, D, d, b).start()

    def chain_sent(chain, i):
        for b in range(2):
            for D in ways(FAR - i, b):
                chain_copy(chain, D, FAR - i, b).wait_send()

    def chain_grads(i):
        if is_int(i) and i == 0:
            grads(wrap(me + FAR), 0)
        else:
            grads(toward(0, FAR - i), 0)
            grads(toward(1, FAR - i), 1)

    def block_sum(b):
        a = jnp.zeros((BLK, DH), F32)
        g = jnp.zeros((BLK, DH), F32)
        for c in range(N):
            at = jnp.where(sel[c, 0] == b, 2 * c, jnp.where(sel[c, 1] == b, 2 * c + 1, EMPTY))
            a = a + dks[at]
            g = g + dvs[at]
        dk_ref[b] = (a * SCALE).astype(BF16)
        dv_ref[b] = g.astype(BF16)

    def query_step(t):
        gather_step(0, t)
        for c, D in behind(t):
            bias = stage(c, D)
            for h in range(HEADS):
                scores(c, D, h, bias)
        for c, D in behind(t):
            to_candidate(st_out, st_in, st_s, st_r, c, me).start()

    def grad_step(t):
        gather_step(1, t)
        for c, D in behind(t):
            for h in range(HEADS):
                weights_grad(c, h)
        for c, D in behind(t):
            to_candidate(del_out, del_in, de_s, de_r, c, me).start()

    def gather_slot(s):
        query_step(s)
        grad_step(s - LAG)

    gather_first(0)
    own_scores()
    bias_me = stage(me, 0)
    for h in range(HEADS):
        scores(me, 0, h, bias_me)
    query_step(1)
    gather_first(1)
    query_step(2)
    loop(3, 7, gather_slot)
    gather_slot(7)
    gather_slot(8)
    for h in range(HEADS):
        weights_grad(me, h)
        own_weights_grad(h)
    dks[EMPTY] = jnp.zeros((BLK, DH), F32)
    dvs[EMPTY] = jnp.zeros((BLK, DH), F32)
    grad_step(7)
    combine_logsum()
    grad_step(8)
    each_peer(lambda p: to_holder(lse_all, ls_s, ls_r, wrap(me + p), p).wait_recv())
    fac[:, :HEADS, :] = jnp.exp(st_out[:, :HEADS, :] - lse_all[:, :HEADS, :])

    chain_step(0, 0)
    for t in range(1, 9):
        gather_sent(0, t)
    chain_step(0, 1)
    combine_deltas()
    chain_step(0, 2)
    each_peer(lambda p: to_holder(delta_all, dl_s, dl_r, wrap(me + p), p).wait_recv())
    chain_grads(0)
    chain_step(1, 0)
    chain_grads(1)

    def chain_slot(u):
        chain_step(0, u)
        chain_step(1, u - LAG)
        chain_grads(u - 1)

    chain_slot(3)
    grads(me, 0)
    loop(4, 6, chain_slot)
    for t in range(1, 9):
        gather_sent(1, t)
    chain_slot(6)
    own_grads()
    chain_slot(7)
    chain_grads(7)
    chain_step(1, 6)
    for h in range(HEADS):
        x = own_ou[h] * own_factor(h) + ou[me, h] * fac[me, h : h + 1, :]
        for D in range(2):
            if h % 2 == 0:
                chain_copy(0, D, 1, h // 2).wait_recv()
            x = x + rf[0, D, 0, h]
        att_ref[:, head(h)] = x.T.astype(BF16)
    loop(0, CB_DEV // 2, block_sum)
    chain_step(1, 7)
    loop(CB_DEV // 2, CB_DEV, block_sum)
    each_peer(lambda p: to_candidate(st_out, st_in, st_s, st_r, wrap(me + p), me).wait_send())
    each_peer(lambda p: to_holder(lse_all, ls_s, ls_r, me, p).wait_send())
    each_peer(lambda p: to_candidate(del_out, del_in, de_s, de_r, wrap(me + p), me).wait_send())
    each_peer(lambda p: to_holder(delta_all, dl_s, dl_r, me, p).wait_send())
    for i in range(8):
        chain_sent(0, i)
    for i in range(7):
        chain_sent(1, i)
    for h in range(HEADS):
        x = own_qu[h] + qu[me, h]
        for D in range(2):
            if h % 2 == 0:
                chain_copy(1, D, 1, h // 2).wait_recv()
            x = x + rf[1, D, 0, h]
        qg_ref[:, head(h)] = (x * SCALE).T.astype(BF16)
    chain_sent(1, 7)


def ring(ids, q, k, v, ok, ov, g):
    vm = pl.BlockSpec(memory_space=pltpu.VMEM)
    shape = jax.ShapeDtypeStruct
    V = pltpu.VMEM
    D = pltpu.SemaphoreType.DMA
    stats = V((N, 8, 128), F32)
    tile = (HEADS, 128, 128)
    return pl.pallas_call(
        ring_kernel,
        in_specs=[pl.BlockSpec(memory_space=pltpu.SMEM)] + [vm] * 6,
        out_specs=[vm] * 6,
        out_shape=[
            shape((128, ROWS), BF16), shape((128, ROWS), BF16),
            shape((BLK, DH), BF16), shape((BLK, DH), BF16),
            shape((CB_DEV, BLK, DH), BF16), shape((CB_DEV, BLK, DH), BF16),
        ],
        scratch_shapes=[
            V((N,) + tile, BF16), V((N,) + tile, BF16),
            V((N, KEYS, DH), BF16), V((N, KEYS, DH), BF16),
            V((N, HEADS, KEYS, 128), F32), V((N, HEADS, KEYS, 128), F32),
            V((N,) + tile, F32), V((N,) + tile, F32),
            V(tile, F32), V(tile, F32), V(tile, F32), V(tile, F32),
            V((8, 128), F32), V((8, 128), F32),
            stats, stats, stats, stats, stats, stats, stats,
            V((3, KEYS, ROWS), BF16), V((3, KEYS, ROWS), BF16), V((2, DH, KEYS), BF16),
            V((2 * N + 1, BLK, DH), F32), V((2 * N + 1, BLK, DH), F32),
            pltpu.SMEM((N, 2), jnp.int32),
            V((2, 2, FAR - WIDE) + tile, BF16), V((2, 2, FAR - WIDE) + tile, BF16),
            V((2, 2, WIDE) + tile, F32), V((2, 2, WIDE) + tile, F32),
            D((2, 2, FAR, 2)), D((2, 2, FAR, 2)), D((2, 2, FAR, 2)), D((2, 2, FAR, 2)),
            D((N,)), D((N,)), D((N,)), D((N,)), D((N,)), D((N,)), D((N,)), D((N,)),
        ],
        compiler_params=pltpu.CompilerParams(
            collective_id=0, has_side_effects=True, vmem_limit_bytes=60 * 1024 * 1024
        ),
        name="ring_attention",
    )(ids, q, k, v, ok, ov, g)


def hand_on_kernel(*refs):
    n = len(refs) // 2
    for j in range(n):
        refs[n + j][...] = refs[j][...]


def hand_on(parts):
    vm = pl.BlockSpec(memory_space=pltpu.VMEM)
    return pl.pallas_call(
        hand_on_kernel,
        in_specs=[vm] * len(parts),
        out_specs=[vm] * len(parts),
        out_shape=[jax.ShapeDtypeStruct(x.shape, x.dtype) for x in parts],
        compiler_params=pltpu.CompilerParams(vmem_limit_bytes=60 * 1024 * 1024),
        name="hand_on",
    )(*parts)


def on_device(queries, context_keys, context_values, own_keys, own_values, out_grad, block_ids):
    k = context_keys.reshape(CB_DEV, BLK, DH)
    v = context_values.reshape(CB_DEV, BLK, DH)
    parts = ring(block_ids, queries, k, v, own_keys, own_values, out_grad)
    att, qg, okg, ovg, dk, dv = hand_on(parts)
    return att, qg, dk.reshape(CB_DEV * BLK, DH), dv.reshape(CB_DEV * BLK, DH), okg, ovg


def solution(mesh):
    rows = P(("dp", "ctx"), "head")
    return jax.shard_map(
        on_device,
        mesh=mesh,
        in_specs=(rows,) * 6 + (P("dp", None),),
        out_specs=(rows,) * 6,
        check_vma=False,
    )
```

```python
import math

import jax
import jax.numpy as jnp
from jax import lax
from jax.experimental import pallas as pl
from jax.experimental.pallas import tpu as pltpu
from jax.sharding import PartitionSpec as P

N = 16
BLK = 128
DH = 128
HEADS = 4
ROWS = HEADS * 128
KEYS = 2 * BLK
SLOTS = 24
CB_DEV = 16
EMPTY = 2 * N
SCALE = 1.0 / math.sqrt(DH)
HIDDEN = -1e30
FLOOR = -(2.0**83)
WIDE = 2
FAR = 8
MARK = 256
F32 = jnp.float32
BF16 = jnp.bfloat16
NT = (((1,), (1,)), ((), ()))
NN = (((1,), (0,)), ((), ()))


def dot(a, b, dims=NN):
    return lax.dot_general(a, b, dims, preferred_element_type=F32)


def wrap(x):
    return lax.rem(x + 2 * N, N)


def head(h):
    return slice(h * 128, (h + 1) * 128)


def is_int(x):
    return isinstance(x, int)


def ring_kernel(
    ids_ref, q_ref, k_ref, v_ref, ok_ref, ov_ref, g_ref,
    att_ref, qg_ref, okg_ref, ovg_ref, dk_ref, dv_ref,
    q_all, g_all, nk, nv, lw, dp, ou, qu,
    own_lw, own_dp, own_ou, own_qu, own_st, own_del,
    st_out, st_in, lse_all, fac,
    ds_t, p_t, tr, dks, dvs, sel, sb, rb, sf, rf,
    g_send, g_recv, c_send, c_recv, st_s, st_r, ls_s, ls_r,
):
    me = lax.axis_index("ctx")
    low = me * CB_DEV
    nbr = (wrap(me + 1), wrap(me - 1))

    barrier = pltpu.get_barrier_semaphore()

    def loop(lo, hi, fn):
        def body(t, _):
            fn(t)
            return 0

        lax.fori_loop(lo, hi, body, 0)

    def each_peer(fn):
        loop(1, N, fn)

    each_peer(lambda p: pl.semaphore_signal(barrier, inc=1, device_id={"ctx": wrap(me + p)}))
    for h in range(HEADS):
        q_all[me, h] = q_ref[:, head(h)]
        g_all[me, h] = g_ref[:, head(h)]
    pl.semaphore_wait(barrier, N - 1)

    def gather_copy(stream, D, t, b, c):
        part = (q_all, g_all)[stream].at[c, pl.ds(2 * b, 2)]
        return pltpu.make_async_remote_copy(
            src_ref=part, dst_ref=part,
            send_sem=g_send.at[stream, D, t - 1, b], recv_sem=g_recv.at[stream, D, t - 1, b],
            device_id={"ctx": nbr[D]},
        )

    def toward(D, d):
        return wrap(me + d) if D == 0 else wrap(me - d)

    def from_behind(D, t):
        return toward(1 - D, t)

    def ways(d, b):
        return (b,) if is_int(d) and d == FAR else () if is_int(d) and d > FAR else (0, 1)

    def behind(t):
        if is_int(t) and t == FAR:
            return ((wrap(me + FAR), 0),)
        return ((from_behind(0, t), 0), (from_behind(1, t), 1))

    def gather_step(stream, t):
        for b in range(2):
            for D in ways(t, b):
                gather_copy(stream, D, t, b, from_behind(D, t)).wait_recv()
            for D in ways(t + 1, b):
                gather_copy(stream, D, t + 1, b, from_behind(D, t)).start()

    def gather_first(stream):
        for b in range(2):
            for D in range(2):
                gather_copy(stream, D, 1, b, me).start()

    def gather_sent(stream, t):
        for b in range(2):
            for D in ways(t, b):
                gather_copy(stream, D, t, b, me).wait_send()

    def to_candidate(src, dst, send, recv, c, slot):
        return pltpu.make_async_remote_copy(
            src_ref=src.at[c], dst_ref=dst.at[slot], send_sem=send.at[c], recv_sem=recv.at[slot],
            device_id={"ctx": c},
        )

    def to_holder(buf, send, recv, slot, p):
        return pltpu.make_async_remote_copy(
            src_ref=buf.at[slot], dst_ref=buf.at[slot], send_sem=send.at[p], recv_sem=recv.at[slot],
            device_id={"ctx": wrap(me + p)},
        )

    def stage(c, D):
        first = jnp.int32(CB_DEV)
        last = jnp.int32(-1)
        count = jnp.int32(0)
        for j in range(SLOTS):
            b = ids_ref[c, j] - low
            inside = (b >= 0) & (b < CB_DEV)
            first = jnp.where(inside, jnp.minimum(first, b), first)
            last = jnp.where(inside, jnp.maximum(last, b), last)
            count = count + jnp.where(inside, 1, 0)
        sel[c, 0] = jnp.where(count >= 1, first, -1)
        sel[c, 1] = jnp.where(count >= 2, last, -1)
        first = jnp.minimum(first, CB_DEV - 1)
        last = jnp.maximum(last, 0)
        nk[c, :BLK, :] = k_ref[first]
        nk[c, BLK:, :] = k_ref[last]
        nv[c, :BLK, :] = v_ref[first]
        nv[c, BLK:, :] = v_ref[last]
        tr[D] = nv[c].T
        bias0 = jnp.where(count >= 1, 0.0, HIDDEN).astype(F32)
        bias1 = jnp.where(count >= 2, 0.0, HIDDEN).astype(F32)
        return bias0, bias1

    def scores(c, D, h, bias):
        s = dot(nk[c], q_all[c, h], NT) * SCALE
        s0 = s[:BLK] + bias[0]
        s1 = s[BLK:] + bias[1]
        m = jnp.max(jnp.maximum(s0, s1), axis=0, keepdims=True)
        m = jnp.maximum(m, FLOOR)
        e = jnp.exp(jnp.concatenate([s0, s1], axis=0) - m)
        lw[c, h] = e
        st_out[c, h : h + 1, :] = m
        st_out[c, HEADS + h : HEADS + h + 1, :] = jnp.sum(e, axis=0, keepdims=True)
        ou[c, h] = dot(tr[D], e.astype(BF16))

    def weights_grad(c, h):
        d = dot(nv[c], g_all[c, h], NT)
        dp[c, h] = d
        e = lw[c, h].astype(BF16).astype(F32)
        st_out[c, 2 * HEADS + h : 2 * HEADS + h + 1, :] = jnp.sum(e * d, axis=0, keepdims=True)

    def grads(c, D):
        tr[D] = nk[c].T
        for h in range(HEADS):
            w = lw[c, h] * fac[c, h : h + 1, :]
            p_t[D, :, head(h)] = w.astype(BF16)
            ds = (w * (dp[c, h] - lse_all[c, HEADS + h : HEADS + h + 1, :])).astype(BF16)
            ds_t[D, :, head(h)] = ds
            qu[c, h] = dot(tr[D], ds)
        a = dot(ds_t[D], q_all[c].reshape(ROWS, DH))
        b = dot(p_t[D], g_all[c].reshape(ROWS, DH))
        for slot in range(2):
            rows = slice(slot * BLK, (slot + 1) * BLK)
            dks[2 * c + slot] = a[rows]
            dvs[2 * c + slot] = b[rows]

    def own_scores():
        keys = ok_ref[...]
        vt = ov_ref[...].T
        seen = lax.broadcasted_iota(jnp.int32, (BLK, 128), 0) <= lax.broadcasted_iota(jnp.int32, (BLK, 128), 1)
        for h in range(HEADS):
            s = jnp.where(seen, dot(keys, q_all[me, h], NT) * SCALE, HIDDEN)
            m = jnp.max(s, axis=0, keepdims=True)
            e = jnp.exp(s - m)
            own_lw[h] = e
            own_st[h : h + 1, :] = m
            own_st[HEADS + h : HEADS + h + 1, :] = jnp.sum(e, axis=0, keepdims=True)
            own_ou[h] = dot(vt, e.astype(BF16))

    def own_weights_grad(h):
        d = dot(ov_ref[...], g_all[me, h], NT)
        own_dp[h] = d
        e = own_lw[h].astype(BF16).astype(F32)
        own_del[h : h + 1, :] = jnp.sum(e * d, axis=0, keepdims=True)

    def own_factor(h):
        return jnp.exp(own_st[h : h + 1, :] - lse_all[me, h : h + 1, :])

    def own_grads():
        kt = ok_ref[...].T
        for h in range(HEADS):
            w = own_lw[h] * own_factor(h)
            p_t[2, :BLK, head(h)] = w.astype(BF16)
            ds = (w * (own_dp[h] - lse_all[me, HEADS + h : HEADS + h + 1, :])).astype(BF16)
            ds_t[2, :BLK, head(h)] = ds
            own_qu[h] = dot(kt, ds)
        okg_ref[...] = (dot(ds_t[2, :BLK, :], q_all[me].reshape(ROWS, DH)) * SCALE).astype(BF16)
        ovg_ref[...] = dot(p_t[2, :BLK, :], g_all[me].reshape(ROWS, DH)).astype(BF16)

    def combine():
        st_in[me] = st_out[me]
        each_peer(lambda p: to_candidate(st_out, st_in, st_s, st_r, wrap(me + p), wrap(me + p)).wait_recv())
        maxima = st_in[:, :HEADS, :]
        totals = st_in[:, HEADS : 2 * HEADS, :]
        parts = st_in[:, 2 * HEADS : 3 * HEADS, :]
        own_max = own_st[:HEADS, :]
        top = jnp.maximum(jnp.max(maxima, axis=0), own_max)
        lift = jnp.exp(maxima - top[None])
        own_lift = jnp.exp(own_max - top)
        total = own_st[HEADS:, :] * own_lift + jnp.sum(totals * lift, axis=0)
        lse_all[me, :HEADS, :] = top + jnp.log(total)
        lse_all[me, HEADS:, :] = (own_del[:HEADS, :] * own_lift + jnp.sum(parts * lift, axis=0)) / total
        each_peer(lambda p: to_holder(lse_all, ls_s, ls_r, me, p).start())

    def buffers(chain, D, d):
        if is_int(d) and d <= WIDE:
            return sf.at[chain, D, d - 1], rf.at[chain, D, d - 1]
        return sb.at[chain, D, d - 1 - WIDE], rb.at[chain, D, d - 1 - WIDE]

    def chain_copy(chain, D, d, b):
        src, dst = buffers(chain, D, d)
        rows = pl.ds(0, MARK + 16 if chain == 0 else MARK)
        return pltpu.make_async_remote_copy(
            src_ref=src.at[b, rows], dst_ref=dst.at[b, rows],
            send_sem=c_send.at[chain, D, d - 1, b], recv_sem=c_recv.at[chain, D, d - 1, b],
            device_id={"ctx": nbr[D]},
        )

    def chain_step(chain, i):
        d = FAR - i
        for b in range(2):
            for D in ways(d + 1, b):
                chain_copy(chain, D, d + 1, b).wait_recv()
            for D in ways(d, b):
                c = toward(D, d)
                out = buffers(chain, D, d)[0]
                came = D in ways(d + 1, b)
                arrived = buffers(chain, D, d + 1)[1] if came else None
                if chain == 0 and came:
                    old = arrived[b, MARK:, :].astype(F32)
                marks = []
                for j in range(2):
                    h = 2 * b + j
                    if chain == 0:
                        m = st_out[c, h : h + 1, :]
                        r = jnp.ceil(m * 0.25) * 4.0
                        if came:
                            r = jnp.maximum(r, old[8 * j : 8 * j + 1])
                        x = ou[c, h] * jnp.exp(m - r)
                        if came:
                            x = x + arrived[b, head(j), :].astype(F32) * jnp.exp(old[8 * j : 8 * j + 1] - r)
                        marks.append(jnp.broadcast_to(r, (8, 128)))
                    else:
                        x = qu[c, h]
                        if came:
                            x = x + arrived[b, head(j), :].astype(F32)
                    out[b, head(j), :] = x.astype(out.dtype)
                if chain == 0:
                    out[b, MARK:, :] = jnp.concatenate(marks, axis=0).astype(out.dtype)
            for D in ways(d, b):
                chain_copy(chain, D, d, b).start()

    def chain_sent(chain, i):
        for b in range(2):
            for D in ways(FAR - i, b):
                chain_copy(chain, D, FAR - i, b).wait_send()

    def chain_grads(i):
        if is_int(i) and i == 0:
            grads(wrap(me + FAR), 0)
        else:
            grads(toward(0, FAR - i), 0)
            grads(toward(1, FAR - i), 1)

    def block_sum(b):
        a = jnp.zeros((BLK, DH), F32)
        g = jnp.zeros((BLK, DH), F32)
        for c in range(N):
            at = jnp.where(sel[c, 0] == b, 2 * c, jnp.where(sel[c, 1] == b, 2 * c + 1, EMPTY))
            a = a + dks[at]
            g = g + dvs[at]
        dk_ref[b] = (a * SCALE).astype(BF16)
        dv_ref[b] = g.astype(BF16)

    def query_step(t):
        gather_step(0, t)
        for c, D in behind(t):
            bias = stage(c, D)
            for h in range(HEADS):
                scores(c, D, h, bias)

    def grad_step(t):
        gather_step(1, t)
        for c, D in behind(t):
            for h in range(HEADS):
                weights_grad(c, h)
        for c, D in behind(t):
            to_candidate(st_out, st_in, st_s, st_r, c, me).start()

    def gather_slot(s):
        query_step(s)
        grad_step(s - 1)

    gather_first(0)
    gather_first(1)
    own_scores()
    bias_me = stage(me, 0)
    for h in range(HEADS):
        scores(me, 0, h, bias_me)
    query_step(1)
    loop(2, 7, gather_slot)
    gather_slot(7)
    gather_slot(8)

    chain_step(0, 0)
    grad_step(8)
    for h in range(HEADS):
        weights_grad(me, h)
        own_weights_grad(h)
    dks[EMPTY] = jnp.zeros((BLK, DH), F32)
    dvs[EMPTY] = jnp.zeros((BLK, DH), F32)
    chain_step(0, 1)
    for t in range(1, 9):
        gather_sent(0, t)
    chain_step(0, 2)
    combine()
    chain_step(0, 3)
    for t in range(1, 9):
        gather_sent(1, t)
    chain_step(0, 4)
    each_peer(lambda p: to_holder(lse_all, ls_s, ls_r, wrap(me + p), p).wait_recv())
    fac[:, :HEADS, :] = jnp.exp(st_out[:, :HEADS, :] - lse_all[:, :HEADS, :])

    chain_grads(0)
    chain_step(1, 0)
    chain_grads(1)
    for i in range(1, 4):
        chain_step(0, i + 4)
        chain_step(1, i)
        chain_grads(i + 1)
    grads(me, 0)
    chain_step(1, 4)
    chain_grads(5)
    own_grads()
    for h in range(HEADS):
        x = own_ou[h] * own_factor(h) + ou[me, h] * fac[me, h : h + 1, :]
        for D in range(2):
            b, j = h // 2, h % 2
            if j == 0:
                chain_copy(0, D, 1, b).wait_recv()
            lift = jnp.exp(rf[0, D, 0, b, MARK + 8 * j : MARK + 8 * j + 1, :] - lse_all[me, h : h + 1, :])
            x = x + rf[0, D, 0, b, head(j), :] * lift
        att_ref[:, head(h)] = x.T.astype(BF16)
    chain_step(1, 5)
    chain_grads(6)
    chain_grads(7)
    chain_step(1, 6)
    loop(0, CB_DEV // 2, block_sum)
    chain_step(1, 7)
    loop(CB_DEV // 2, CB_DEV, block_sum)
    each_peer(lambda p: to_candidate(st_out, st_in, st_s, st_r, wrap(me + p), me).wait_send())
    each_peer(lambda p: to_holder(lse_all, ls_s, ls_r, me, p).wait_send())
    for i in range(8):
        chain_sent(0, i)
    for i in range(7):
        chain_sent(1, i)
    for h in range(HEADS):
        x = own_qu[h] + qu[me, h]
        for D in range(2):
            b, j = h // 2, h % 2
            if j == 0:
                chain_copy(1, D, 1, b).wait_recv()
            x = x + rf[1, D, 0, b, head(j), :]
        qg_ref[:, head(h)] = (x * SCALE).T.astype(BF16)
    chain_sent(1, 7)


def ring(ids, q, k, v, ok, ov, g):
    vm = pl.BlockSpec(memory_space=pltpu.VMEM)
    shape = jax.ShapeDtypeStruct
    V = pltpu.VMEM
    D = pltpu.SemaphoreType.DMA
    message = (2, MARK + 16, 128)
    tile = (HEADS, 128, 128)
    return pl.pallas_call(
        ring_kernel,
        in_specs=[pl.BlockSpec(memory_space=pltpu.SMEM)] + [vm] * 6,
        out_specs=[vm] * 6,
        out_shape=[
            shape((128, ROWS), BF16), shape((128, ROWS), BF16),
            shape((BLK, DH), BF16), shape((BLK, DH), BF16),
            shape((CB_DEV, BLK, DH), BF16), shape((CB_DEV, BLK, DH), BF16),
        ],
        scratch_shapes=[
            V((N,) + tile, BF16), V((N,) + tile, BF16),
            V((N, KEYS, DH), BF16), V((N, KEYS, DH), BF16),
            V((N, HEADS, KEYS, 128), F32), V((N, HEADS, KEYS, 128), F32),
            V((N,) + tile, F32), V((N,) + tile, F32),
            V(tile, F32), V(tile, F32), V(tile, F32), V(tile, F32),
            V((8, 128), F32), V((8, 128), F32),
            V((N, 16, 128), F32), V((N, 16, 128), F32), V((N, 8, 128), F32), V((N, 8, 128), F32),
            V((3, KEYS, ROWS), BF16), V((3, KEYS, ROWS), BF16), V((2, DH, KEYS), BF16),
            V((2 * N + 1, BLK, DH), F32), V((2 * N + 1, BLK, DH), F32),
            pltpu.SMEM((N, 2), jnp.int32),
            V((2, 2, FAR - WIDE) + message, BF16), V((2, 2, FAR - WIDE) + message, BF16),
            V((2, 2, WIDE) + message, F32), V((2, 2, WIDE) + message, F32),
            D((2, 2, FAR, 2)), D((2, 2, FAR, 2)), D((2, 2, FAR, 2)), D((2, 2, FAR, 2)),
            D((N,)), D((N,)), D((N,)), D((N,)),
        ],
        compiler_params=pltpu.CompilerParams(
            collective_id=0, has_side_effects=True, vmem_limit_bytes=60 * 1024 * 1024
        ),
        name="ring_attention",
    )(ids, q, k, v, ok, ov, g)


def hand_on_kernel(*refs):
    n = len(refs) // 2
    for j in range(n):
        refs[n + j][...] = refs[j][...]


def hand_on(parts):
    vm = pl.BlockSpec(memory_space=pltpu.VMEM)
    return pl.pallas_call(
        hand_on_kernel,
        in_specs=[vm] * len(parts),
        out_specs=[vm] * len(parts),
        out_shape=[jax.ShapeDtypeStruct(x.shape, x.dtype) for x in parts],
        compiler_params=pltpu.CompilerParams(vmem_limit_bytes=60 * 1024 * 1024),
        name="hand_on",
    )(*parts)


def on_device(queries, context_keys, context_values, own_keys, own_values, out_grad, block_ids):
    k = context_keys.reshape(CB_DEV, BLK, DH)
    v = context_values.reshape(CB_DEV, BLK, DH)
    parts = ring(block_ids, queries, k, v, own_keys, own_values, out_grad)
    att, qg, okg, ovg, dk, dv = hand_on(parts)
    return att, qg, dk.reshape(CB_DEV * BLK, DH), dv.reshape(CB_DEV * BLK, DH), okg, ovg


def solution(mesh):
    rows = P(("dp", "ctx"), "head")
    return jax.shard_map(
        on_device,
        mesh=mesh,
        in_specs=(rows,) * 6 + (P("dp", None),),
        out_specs=(rows,) * 6,
        check_vma=False,
    )
```

```python
import math

import jax
import jax.numpy as jnp
from jax import lax
from jax.experimental import pallas as pl
from jax.experimental.pallas import tpu as pltpu
from jax.sharding import PartitionSpec as P

N = 16
BLK = 128
DH = 128
HEADS = 4
ROWS = HEADS * 128
KEYS = 2 * BLK
SLOTS = 24
CB_DEV = 16
EMPTY = 2 * N
SCALE = 1.0 / math.sqrt(DH)
HIDDEN = -1e30
FLOOR = -(2.0**83)
NEAR = 2
FAR = 8
MARK = 256
F32 = jnp.float32
BF16 = jnp.bfloat16
NT = (((1,), (1,)), ((), ()))
NN = (((1,), (0,)), ((), ()))


def dot(a, b, dims=NN):
    return lax.dot_general(a, b, dims, preferred_element_type=F32)


def wrap(x):
    return lax.rem(x + 2 * N, N)


def head(h):
    return slice(h * 128, (h + 1) * 128)


def is_int(x):
    return isinstance(x, int)


def ring_kernel(
    ids_ref, q_ref, k_ref, v_ref, ok_ref, ov_ref, g_ref,
    att_ref, qg_ref, okg_ref, ovg_ref, dk_ref, dv_ref,
    q_all, g_all, nk, nv, lw, dp, ou, qu,
    own_lw, own_dp, own_ou, own_qu, own_st, own_del,
    st_out, st_in, lse_all, fac,
    ds_t, p_t, tr, dks, dvs, sel, sb, rb,
    fk, fv, f_lw, f_dp, f_ou, f_max,
    g_send, g_recv, c_send, c_recv, st_s, st_r, ls_s, ls_r, f_send, f_recv,
):
    me = lax.axis_index("ctx")
    low = me * CB_DEV
    nbr = (wrap(me + 1), wrap(me - 1))

    barrier = pltpu.get_barrier_semaphore()

    def loop(lo, hi, fn):
        def body(t, _):
            fn(t)
            return 0

        lax.fori_loop(lo, hi, body, 0)

    def each_peer(fn):
        loop(1, N, fn)

    each_peer(lambda p: pl.semaphore_signal(barrier, inc=1, device_id={"ctx": wrap(me + p)}))
    for h in range(HEADS):
        q_all[me, h] = q_ref[:, head(h)]
        g_all[me, h] = g_ref[:, head(h)]
    pl.semaphore_wait(barrier, N - 1)

    def gather_copy(stream, D, t, b, c):
        part = (q_all, g_all)[stream].at[c, pl.ds(2 * b, 2)]
        return pltpu.make_async_remote_copy(
            src_ref=part, dst_ref=part,
            send_sem=g_send.at[stream, D, t - 1, b], recv_sem=g_recv.at[stream, D, t - 1, b],
            device_id={"ctx": nbr[D]},
        )

    def toward(D, d):
        return wrap(me + d) if D == 0 else wrap(me - d)

    def from_behind(D, t):
        return toward(1 - D, t)

    def ways(d, b):
        return (b,) if is_int(d) and d == FAR else () if is_int(d) and d > FAR else (0, 1)

    def behind(t):
        if is_int(t) and t == FAR:
            return ((wrap(me + FAR), 0),)
        return ((from_behind(0, t), 0), (from_behind(1, t), 1))

    def gather_step(stream, t):
        for b in range(2):
            for D in ways(t, b):
                gather_copy(stream, D, t, b, from_behind(D, t)).wait_recv()
            for D in ways(t + 1, b):
                gather_copy(stream, D, t + 1, b, from_behind(D, t)).start()

    def gather_first(stream):
        for b in range(2):
            for D in range(2):
                gather_copy(stream, D, 1, b, me).start()

    def gather_sent(stream, t):
        for b in range(2):
            for D in ways(t, b):
                gather_copy(stream, D, t, b, me).wait_send()

    def to_candidate(src, dst, send, recv, c, slot):
        return pltpu.make_async_remote_copy(
            src_ref=src.at[c], dst_ref=dst.at[slot], send_sem=send.at[c], recv_sem=recv.at[slot],
            device_id={"ctx": c},
        )

    def to_holder(buf, send, recv, slot, p):
        return pltpu.make_async_remote_copy(
            src_ref=buf.at[slot], dst_ref=buf.at[slot], send_sem=send.at[p], recv_sem=recv.at[slot],
            device_id={"ctx": wrap(me + p)},
        )

    def biases(count):
        return (
            jnp.where(count >= 1, 0.0, HIDDEN).astype(F32),
            jnp.where(count >= 2, 0.0, HIDDEN).astype(F32),
        )

    def pick(c, low):
        first = jnp.int32(CB_DEV)
        last = jnp.int32(-1)
        count = jnp.int32(0)
        for j in range(SLOTS):
            b = ids_ref[c, j] - low
            inside = (b >= 0) & (b < CB_DEV)
            first = jnp.where(inside, jnp.minimum(first, b), first)
            last = jnp.where(inside, jnp.maximum(last, b), last)
            count = count + jnp.where(inside, 1, 0)
        return first, last, count

    def stage(c):
        first, last, count = pick(c, low)
        sel[c, 0] = jnp.where(count >= 1, first, -1)
        sel[c, 1] = jnp.where(count >= 2, last, -1)
        first = jnp.minimum(first, CB_DEV - 1)
        last = jnp.maximum(last, 0)
        nk[c, :BLK, :] = k_ref[first]
        nk[c, BLK:, :] = k_ref[last]
        nv[c, :BLK, :] = v_ref[first]
        nv[c, BLK:, :] = v_ref[last]

    def score_bias(c, D):
        tr[D] = nv[c].T
        return (
            jnp.where(sel[c, 0] >= 0, 0.0, HIDDEN).astype(F32),
            jnp.where(sel[c, 1] >= 0, 0.0, HIDDEN).astype(F32),
        )

    def local_scores(keys, q, bias):
        s = dot(keys, q, NT) * SCALE
        s0 = s[:BLK] + bias[0]
        s1 = s[BLK:] + bias[1]
        m = jnp.max(jnp.maximum(s0, s1), axis=0, keepdims=True)
        m = jnp.maximum(m, FLOOR)
        return m, jnp.exp(jnp.concatenate([s0, s1], axis=0) - m)

    def scores(c, D, h, bias):
        m, e = local_scores(nk[c], q_all[c, h], bias)
        lw[c, h] = e
        st_out[c, h : h + 1, :] = m
        st_out[c, HEADS + h : HEADS + h + 1, :] = jnp.sum(e, axis=0, keepdims=True)
        ou[c, h] = dot(tr[D], e.astype(BF16))

    def weights_grad(c, h):
        d = dot(nv[c], g_all[c, h], NT)
        dp[c, h] = d
        e = lw[c, h].astype(BF16).astype(F32)
        st_out[c, 2 * HEADS + h : 2 * HEADS + h + 1, :] = jnp.sum(e * d, axis=0, keepdims=True)

    def grads(c, D, back=True):
        if back:
            tr[D] = nk[c].T
        for h in range(HEADS):
            w = lw[c, h] * fac[c, h : h + 1, :]
            p_t[D, :, head(h)] = w.astype(BF16)
            ds = (w * (dp[c, h] - lse_all[c, HEADS + h : HEADS + h + 1, :])).astype(BF16)
            ds_t[D, :, head(h)] = ds
            if back:
                qu[c, h] = dot(tr[D], ds)
        a = dot(ds_t[D], q_all[c].reshape(ROWS, DH))
        b = dot(p_t[D], g_all[c].reshape(ROWS, DH))
        for slot in range(2):
            rows = slice(slot * BLK, (slot + 1) * BLK)
            dks[2 * c + slot] = a[rows]
            dvs[2 * c + slot] = b[rows]

    def own_scores():
        keys = ok_ref[...]
        vt = ov_ref[...].T
        seen = lax.broadcasted_iota(jnp.int32, (BLK, 128), 0) <= lax.broadcasted_iota(jnp.int32, (BLK, 128), 1)
        for h in range(HEADS):
            s = jnp.where(seen, dot(keys, q_all[me, h], NT) * SCALE, HIDDEN)
            m = jnp.max(s, axis=0, keepdims=True)
            e = jnp.exp(s - m)
            own_lw[h] = e
            own_st[h : h + 1, :] = m
            own_st[HEADS + h : HEADS + h + 1, :] = jnp.sum(e, axis=0, keepdims=True)
            own_ou[h] = dot(vt, e.astype(BF16))

    def own_weights_grad(h):
        d = dot(ov_ref[...], g_all[me, h], NT)
        own_dp[h] = d
        e = own_lw[h].astype(BF16).astype(F32)
        own_del[h : h + 1, :] = jnp.sum(e * d, axis=0, keepdims=True)

    def own_factor(h):
        return jnp.exp(own_st[h : h + 1, :] - lse_all[me, h : h + 1, :])

    def own_grads():
        kt = ok_ref[...].T
        for h in range(HEADS):
            w = own_lw[h] * own_factor(h)
            p_t[2, :BLK, head(h)] = w.astype(BF16)
            ds = (w * (own_dp[h] - lse_all[me, HEADS + h : HEADS + h + 1, :])).astype(BF16)
            ds_t[2, :BLK, head(h)] = ds
            own_qu[h] = dot(kt, ds)
        okg_ref[...] = (dot(ds_t[2, :BLK, :], q_all[me].reshape(ROWS, DH)) * SCALE).astype(BF16)
        ovg_ref[...] = dot(p_t[2, :BLK, :], g_all[me].reshape(ROWS, DH)).astype(BF16)

    def near_copy(D, d, w):
        return pltpu.make_async_remote_copy(
            src_ref=(nk, nv)[w].at[toward(D, d)], dst_ref=(fk, fv)[w].at[2 * D + d - 1],
            send_sem=f_send.at[D, d - 1, w], recv_sem=f_recv.at[D, d - 1, w],
            device_id={"ctx": toward(D, d)},
        )

    def near_scores(D, d):
        n = 2 * D + d - 1
        for w in range(2):
            near_copy(D, d, w).wait_recv()
        count = pick(me, from_behind(D, d) * CB_DEV)[2]
        bias = biases(count)
        tr[D] = fv[n].T
        for h in range(HEADS):
            m, e = local_scores(fk[n], q_all[me, h], bias)
            f_lw[n, h] = e
            f_max[n, h : h + 1, :] = m
            f_ou[n, h] = dot(tr[D], e.astype(BF16))
            f_dp[n, h] = dot(fv[n], g_all[me, h], NT)

    def near_grads(D, d):
        n = 2 * D + d - 1
        tr[D] = fk[n].T
        for h in range(HEADS):
            w = f_lw[n, h] * jnp.exp(f_max[n, h : h + 1, :] - lse_all[me, h : h + 1, :])
            ds = (w * (f_dp[n, h] - lse_all[me, HEADS + h : HEADS + h + 1, :])).astype(BF16)
            own_qu[h] += dot(tr[D], ds)

    def combine():
        st_in[me] = st_out[me]
        each_peer(lambda p: to_candidate(st_out, st_in, st_s, st_r, wrap(me + p), wrap(me + p)).wait_recv())
        maxima = st_in[:, :HEADS, :]
        totals = st_in[:, HEADS : 2 * HEADS, :]
        parts = st_in[:, 2 * HEADS : 3 * HEADS, :]
        own_max = own_st[:HEADS, :]
        top = jnp.maximum(jnp.max(maxima, axis=0), own_max)
        lift = jnp.exp(maxima - top[None])
        own_lift = jnp.exp(own_max - top)
        total = own_st[HEADS:, :] * own_lift + jnp.sum(totals * lift, axis=0)
        lse_all[me, :HEADS, :] = top + jnp.log(total)
        lse_all[me, HEADS:, :] = (own_del[:HEADS, :] * own_lift + jnp.sum(parts * lift, axis=0)) / total
        each_peer(lambda p: to_holder(lse_all, ls_s, ls_r, me, p).start())

    def buffers(chain, D, d):
        return sb.at[chain, D, d - 1 - NEAR], rb.at[chain, D, d - 1 - NEAR]

    def chain_copy(chain, D, d, b):
        src, dst = buffers(chain, D, d)
        rows = pl.ds(0, MARK + 16 if chain == 0 else MARK)
        return pltpu.make_async_remote_copy(
            src_ref=src.at[b, rows], dst_ref=dst.at[b, rows],
            send_sem=c_send.at[chain, D, d - 1, b], recv_sem=c_recv.at[chain, D, d - 1, b],
            device_id={"ctx": toward(D, NEAR + 1) if d == NEAR + 1 else nbr[D]},
        )

    def chain_step(chain, i):
        d = FAR - i
        for b in range(2):
            for D in ways(d + 1, b):
                chain_copy(chain, D, d + 1, b).wait_recv()
            for D in ways(d, b):
                c = toward(D, d)
                out = buffers(chain, D, d)[0]
                came = D in ways(d + 1, b)
                arrived = buffers(chain, D, d + 1)[1] if came else None
                if chain == 0 and came:
                    old = arrived[b, MARK:, :].astype(F32)
                marks = []
                for j in range(2):
                    h = 2 * b + j
                    if chain == 0:
                        m = st_out[c, h : h + 1, :]
                        r = jnp.ceil(m * 0.25) * 4.0
                        if came:
                            r = jnp.maximum(r, old[8 * j : 8 * j + 1])
                        x = ou[c, h] * jnp.exp(m - r)
                        if came:
                            x = x + arrived[b, head(j), :].astype(F32) * jnp.exp(old[8 * j : 8 * j + 1] - r)
                        marks.append(jnp.broadcast_to(r, (8, 128)))
                    else:
                        x = qu[c, h]
                        if came:
                            x = x + arrived[b, head(j), :].astype(F32)
                    out[b, head(j), :] = x.astype(out.dtype)
                if chain == 0:
                    out[b, MARK:, :] = jnp.concatenate(marks, axis=0).astype(out.dtype)
            for D in ways(d, b):
                chain_copy(chain, D, d, b).start()

    def chain_sent(chain, i):
        for b in range(2):
            for D in ways(FAR - i, b):
                chain_copy(chain, D, FAR - i, b).wait_send()

    def chain_grads(i):
        if is_int(i) and i == 0:
            grads(wrap(me + FAR), 0)
        else:
            grads(toward(0, FAR - i), 0)
            grads(toward(1, FAR - i), 1)

    def block_sum(b):
        a = jnp.zeros((BLK, DH), F32)
        g = jnp.zeros((BLK, DH), F32)
        for c in range(N):
            at = jnp.where(sel[c, 0] == b, 2 * c, jnp.where(sel[c, 1] == b, 2 * c + 1, EMPTY))
            a = a + dks[at]
            g = g + dvs[at]
        dk_ref[b] = (a * SCALE).astype(BF16)
        dv_ref[b] = g.astype(BF16)

    def query_step(t):
        gather_step(0, t)
        for c, D in behind(t):
            if not is_int(t) or t > NEAR:
                stage(c)
            bias = score_bias(c, D)
            for h in range(HEADS):
                scores(c, D, h, bias)

    def grad_step(t):
        gather_step(1, t)
        for c, D in behind(t):
            for h in range(HEADS):
                weights_grad(c, h)
        for c, D in behind(t):
            to_candidate(st_out, st_in, st_s, st_r, c, me).start()

    def gather_slot(s):
        query_step(s)
        grad_step(s - 1)

    gather_first(0)
    gather_first(1)
    for d in range(1, NEAR + 1):
        for D in range(2):
            stage(toward(D, d))
            for w in range(2):
                near_copy(D, d, w).start()
    own_scores()
    stage(me)
    bias_me = score_bias(me, 0)
    for h in range(HEADS):
        scores(me, 0, h, bias_me)
    query_step(1)
    gather_slot(2)
    loop(3, 7, gather_slot)
    gather_slot(7)
    gather_slot(8)

    chain_step(0, 0)
    grad_step(8)
    for h in range(HEADS):
        weights_grad(me, h)
        own_weights_grad(h)
    dks[EMPTY] = jnp.zeros((BLK, DH), F32)
    dvs[EMPTY] = jnp.zeros((BLK, DH), F32)
    chain_step(0, 1)
    near_scores(0, 1)
    near_scores(1, 1)
    for t in range(1, 9):
        gather_sent(0, t)
    chain_step(0, 2)
    combine()
    chain_step(0, 3)
    near_scores(0, 2)
    near_scores(1, 2)
    for t in range(1, 9):
        gather_sent(1, t)
    chain_step(0, 4)
    each_peer(lambda p: to_holder(lse_all, ls_s, ls_r, wrap(me + p), p).wait_recv())
    fac[:, :HEADS, :] = jnp.exp(st_out[:, :HEADS, :] - lse_all[:, :HEADS, :])

    chain_grads(0)
    chain_step(1, 0)
    chain_grads(1)
    chain_step(0, 5)
    chain_step(1, 1)
    chain_grads(2)
    for D in range(2):
        grads(toward(D, 2), D, False)
    chain_step(1, 2)
    chain_grads(3)
    for D in range(2):
        grads(toward(D, 1), D, False)
    chain_step(1, 3)
    chain_grads(4)
    own_grads()
    near_grads(0, 1)
    near_grads(1, 1)
    chain_step(1, 4)
    chain_grads(5)
    chain_step(1, 5)
    grads(me, 0)
    near_grads(0, 2)
    near_grads(1, 2)
    last = NEAR + 1
    for h in range(HEADS):
        b, j = h // 2, h % 2
        x = own_ou[h] * own_factor(h) + ou[me, h] * fac[me, h : h + 1, :]
        for n in range(2 * NEAR):
            x = x + f_ou[n, h] * jnp.exp(f_max[n, h : h + 1, :] - lse_all[me, h : h + 1, :])
        for D in range(2):
            if j == 0:
                chain_copy(0, D, last, b).wait_recv()
            came = buffers(0, D, last)[1]
            r = came[b, MARK:, :].astype(F32)[8 * j : 8 * j + 1]
            x = x + came[b, head(j), :].astype(F32) * jnp.exp(r - lse_all[me, h : h + 1, :])
        att_ref[:, head(h)] = x.T.astype(BF16)
    loop(0, CB_DEV, block_sum)
    each_peer(lambda p: to_candidate(st_out, st_in, st_s, st_r, wrap(me + p), me).wait_send())
    each_peer(lambda p: to_holder(lse_all, ls_s, ls_r, me, p).wait_send())
    for d in range(1, NEAR + 1):
        for D in range(2):
            for w in range(2):
                near_copy(D, d, w).wait_send()
    for i in range(6):
        chain_sent(0, i)
    for i in range(5):
        chain_sent(1, i)
    for h in range(HEADS):
        b, j = h // 2, h % 2
        x = own_qu[h] + qu[me, h]
        for D in range(2):
            if j == 0:
                chain_copy(1, D, last, b).wait_recv()
            x = x + buffers(1, D, last)[1][b, head(j), :].astype(F32)
        qg_ref[:, head(h)] = (x * SCALE).T.astype(BF16)
    chain_sent(1, 5)


def ring(ids, q, k, v, ok, ov, g):
    vm = pl.BlockSpec(memory_space=pltpu.VMEM)
    shape = jax.ShapeDtypeStruct
    V = pltpu.VMEM
    D = pltpu.SemaphoreType.DMA
    message = (2, MARK + 16, 128)
    tile = (HEADS, 128, 128)
    return pl.pallas_call(
        ring_kernel,
        in_specs=[pl.BlockSpec(memory_space=pltpu.SMEM)] + [vm] * 6,
        out_specs=[vm] * 6,
        out_shape=[
            shape((128, ROWS), BF16), shape((128, ROWS), BF16),
            shape((BLK, DH), BF16), shape((BLK, DH), BF16),
            shape((CB_DEV, BLK, DH), BF16), shape((CB_DEV, BLK, DH), BF16),
        ],
        scratch_shapes=[
            V((N,) + tile, BF16), V((N,) + tile, BF16),
            V((N, KEYS, DH), BF16), V((N, KEYS, DH), BF16),
            V((N, HEADS, KEYS, 128), F32), V((N, HEADS, KEYS, 128), F32),
            V((N,) + tile, F32), V((N,) + tile, F32),
            V(tile, F32), V(tile, F32), V(tile, F32), V(tile, F32),
            V((8, 128), F32), V((8, 128), F32),
            V((N, 16, 128), F32), V((N, 16, 128), F32), V((N, 8, 128), F32), V((N, 8, 128), F32),
            V((3, KEYS, ROWS), BF16), V((3, KEYS, ROWS), BF16), V((2, DH, KEYS), BF16),
            V((2 * N + 1, BLK, DH), F32), V((2 * N + 1, BLK, DH), F32),
            pltpu.SMEM((N, 2), jnp.int32),
            V((2, 2, FAR - NEAR) + message, BF16), V((2, 2, FAR - NEAR) + message, BF16),
            V((2 * NEAR, KEYS, DH), BF16), V((2 * NEAR, KEYS, DH), BF16),
            V((2 * NEAR, HEADS, KEYS, 128), F32), V((2 * NEAR, HEADS, KEYS, 128), F32),
            V((2 * NEAR,) + tile, F32), V((2 * NEAR, 8, 128), F32),
            D((2, 2, FAR, 2)), D((2, 2, FAR, 2)), D((2, 2, FAR, 2)), D((2, 2, FAR, 2)),
            D((N,)), D((N,)), D((N,)), D((N,)), D((2, NEAR, 2)), D((2, NEAR, 2)),
        ],
        compiler_params=pltpu.CompilerParams(
            collective_id=0, has_side_effects=True, vmem_limit_bytes=60 * 1024 * 1024
        ),
        name="ring_attention",
    )(ids, q, k, v, ok, ov, g)


def hand_on_kernel(*refs):
    n = len(refs) // 2
    for j in range(n):
        refs[n + j][...] = refs[j][...]


def hand_on(parts):
    vm = pl.BlockSpec(memory_space=pltpu.VMEM)
    return pl.pallas_call(
        hand_on_kernel,
        in_specs=[vm] * len(parts),
        out_specs=[vm] * len(parts),
        out_shape=[jax.ShapeDtypeStruct(x.shape, x.dtype) for x in parts],
        compiler_params=pltpu.CompilerParams(vmem_limit_bytes=60 * 1024 * 1024),
        name="hand_on",
    )(*parts)


def on_device(queries, context_keys, context_values, own_keys, own_values, out_grad, block_ids):
    k = context_keys.reshape(CB_DEV, BLK, DH)
    v = context_values.reshape(CB_DEV, BLK, DH)
    parts = ring(block_ids, queries, k, v, own_keys, own_values, out_grad)
    att, qg, okg, ovg, dk, dv = hand_on(parts)
    return att, qg, dk.reshape(CB_DEV * BLK, DH), dv.reshape(CB_DEV * BLK, DH), okg, ovg


def solution(mesh):
    rows = P(("dp", "ctx"), "head")
    return jax.shard_map(
        on_device,
        mesh=mesh,
        in_specs=(rows,) * 6 + (P("dp", None),),
        out_specs=(rows,) * 6,
        check_vma=False,
    )
```

```python
import math

import jax
import jax.numpy as jnp
from jax import lax
from jax.experimental import pallas as pl
from jax.experimental.pallas import tpu as pltpu
from jax.sharding import PartitionSpec as P

N = 16
BLK = 128
DH = 128
HEADS = 4
ROWS = HEADS * 128
KEYS = 2 * BLK
SLOTS = 24
CB_DEV = 16
EMPTY = 2 * N
SCALE = 1.0 / math.sqrt(DH)
HIDDEN = -1e30
FLOOR = -(2.0**83)
NEAR = 2
FAR = 8
MARK = 256
F32 = jnp.float32
BF16 = jnp.bfloat16
NT = (((1,), (1,)), ((), ()))
NN = (((1,), (0,)), ((), ()))


def dot(a, b, dims=NN):
    return lax.dot_general(a, b, dims, preferred_element_type=F32)


def wrap(x):
    return lax.rem(x + 2 * N, N)


def head(h):
    return slice(h * 128, (h + 1) * 128)


def is_int(x):
    return isinstance(x, int)


def ring_kernel(
    ids_ref, q_ref, k_ref, v_ref, ok_ref, ov_ref, g_ref,
    att_ref, qg_ref, okg_ref, ovg_ref, dk_ref, dv_ref,
    q_all, g_all, nk, nv, lw, dp, ou, qu,
    own_lw, own_dp, own_ou, own_qu, own_st, own_del,
    st_out, st_in, lse_all, fac,
    ds_t, p_t, tr, dks, dvs, sel, sb, rb,
    fk, fv, f_lw, f_dp, f_ou, f_max,
    g_send, g_recv, c_send, c_recv, st_s, st_r, ls_s, ls_r, f_send, f_recv, pace_sem,
):
    me = lax.axis_index("ctx")
    low = me * CB_DEV
    nbr = (wrap(me + 1), wrap(me - 1))

    barrier = pltpu.get_barrier_semaphore()

    def loop(lo, hi, fn):
        def body(t, _):
            fn(t)
            return 0

        lax.fori_loop(lo, hi, body, 0)

    def each_peer(fn):
        loop(1, N, fn)

    paired = lax.axis_size("head") % 2 == 0
    side = lax.axis_index("head")
    other = side + 1 - 2 * lax.rem(side, 2)

    def pace(wait=True):
        if paired:
            pl.semaphore_signal(pace_sem, inc=1, device_id={"head": other})
            if wait:
                pl.semaphore_wait(pace_sem, 1)

    each_peer(lambda p: pl.semaphore_signal(barrier, inc=1, device_id={"ctx": wrap(me + p)}))
    if paired:
        pl.semaphore_signal(barrier, inc=1, device_id={"head": other})
    for h in range(HEADS):
        q_all[me, h] = q_ref[:, head(h)]
        g_all[me, h] = g_ref[:, head(h)]
    pl.semaphore_wait(barrier, N if paired else N - 1)

    def gather_copy(stream, D, t, b, c):
        part = (q_all, g_all)[stream].at[c, pl.ds(2 * b, 2)]
        return pltpu.make_async_remote_copy(
            src_ref=part, dst_ref=part,
            send_sem=g_send.at[stream, D, t - 1, b], recv_sem=g_recv.at[stream, D, t - 1, b],
            device_id={"ctx": nbr[D]},
        )

    def toward(D, d):
        return wrap(me + d) if D == 0 else wrap(me - d)

    def from_behind(D, t):
        return toward(1 - D, t)

    def ways(d, b):
        return (b,) if is_int(d) and d == FAR else () if is_int(d) and d > FAR else (0, 1)

    def behind(t):
        if is_int(t) and t == FAR:
            return ((wrap(me + FAR), 0),)
        return ((from_behind(0, t), 0), (from_behind(1, t), 1))

    def gather_step(stream, t):
        for b in range(2):
            for D in ways(t, b):
                gather_copy(stream, D, t, b, from_behind(D, t)).wait_recv()
            for D in ways(t + 1, b):
                gather_copy(stream, D, t + 1, b, from_behind(D, t)).start()

    def gather_first(stream):
        for b in range(2):
            for D in range(2):
                gather_copy(stream, D, 1, b, me).start()

    def gather_sent(stream, t):
        for b in range(2):
            for D in ways(t, b):
                gather_copy(stream, D, t, b, me).wait_send()

    def to_candidate(src, dst, send, recv, c, slot):
        return pltpu.make_async_remote_copy(
            src_ref=src.at[c], dst_ref=dst.at[slot], send_sem=send.at[c], recv_sem=recv.at[slot],
            device_id={"ctx": c},
        )

    def to_holder(buf, send, recv, slot, p):
        return pltpu.make_async_remote_copy(
            src_ref=buf.at[slot], dst_ref=buf.at[slot], send_sem=send.at[p], recv_sem=recv.at[slot],
            device_id={"ctx": wrap(me + p)},
        )

    def biases(count):
        return (
            jnp.where(count >= 1, 0.0, HIDDEN).astype(F32),
            jnp.where(count >= 2, 0.0, HIDDEN).astype(F32),
        )

    def pick(c, low):
        first = jnp.int32(CB_DEV)
        last = jnp.int32(-1)
        count = jnp.int32(0)
        for j in range(SLOTS):
            b = ids_ref[c, j] - low
            inside = (b >= 0) & (b < CB_DEV)
            first = jnp.where(inside, jnp.minimum(first, b), first)
            last = jnp.where(inside, jnp.maximum(last, b), last)
            count = count + jnp.where(inside, 1, 0)
        return first, last, count

    def stage(c):
        first, last, count = pick(c, low)
        sel[c, 0] = jnp.where(count >= 1, first, -1)
        sel[c, 1] = jnp.where(count >= 2, last, -1)
        first = jnp.minimum(first, CB_DEV - 1)
        last = jnp.maximum(last, 0)
        nk[c, :BLK, :] = k_ref[first]
        nk[c, BLK:, :] = k_ref[last]
        nv[c, :BLK, :] = v_ref[first]
        nv[c, BLK:, :] = v_ref[last]

    def score_bias(c, D):
        tr[D] = nv[c].T
        return (
            jnp.where(sel[c, 0] >= 0, 0.0, HIDDEN).astype(F32),
            jnp.where(sel[c, 1] >= 0, 0.0, HIDDEN).astype(F32),
        )

    def local_scores(keys, q, bias):
        s = dot(keys, q, NT) * SCALE
        s0 = s[:BLK] + bias[0]
        s1 = s[BLK:] + bias[1]
        m = jnp.max(jnp.maximum(s0, s1), axis=0, keepdims=True)
        m = jnp.maximum(m, FLOOR)
        return m, jnp.exp(jnp.concatenate([s0, s1], axis=0) - m)

    def scores(c, D, h, bias):
        m, e = local_scores(nk[c], q_all[c, h], bias)
        lw[c, h] = e
        st_out[c, h : h + 1, :] = m
        st_out[c, HEADS + h : HEADS + h + 1, :] = jnp.sum(e, axis=0, keepdims=True)
        ou[c, h] = dot(tr[D], e.astype(BF16))

    def weights_grad(c, h):
        d = dot(nv[c], g_all[c, h], NT)
        dp[c, h] = d
        e = lw[c, h].astype(BF16).astype(F32)
        st_out[c, 2 * HEADS + h : 2 * HEADS + h + 1, :] = jnp.sum(e * d, axis=0, keepdims=True)

    def grads(c, D, back=True):
        if back:
            tr[D] = nk[c].T
        for h in range(HEADS):
            w = lw[c, h] * fac[c, h : h + 1, :]
            p_t[D, :, head(h)] = w.astype(BF16)
            ds = (w * (dp[c, h] - lse_all[c, HEADS + h : HEADS + h + 1, :])).astype(BF16)
            ds_t[D, :, head(h)] = ds
            if back:
                qu[c, h] = dot(tr[D], ds)
        a = dot(ds_t[D], q_all[c].reshape(ROWS, DH))
        b = dot(p_t[D], g_all[c].reshape(ROWS, DH))
        for slot in range(2):
            rows = slice(slot * BLK, (slot + 1) * BLK)
            dks[2 * c + slot] = a[rows]
            dvs[2 * c + slot] = b[rows]

    def own_scores():
        keys = ok_ref[...]
        vt = ov_ref[...].T
        seen = lax.broadcasted_iota(jnp.int32, (BLK, 128), 0) <= lax.broadcasted_iota(jnp.int32, (BLK, 128), 1)
        for h in range(HEADS):
            s = jnp.where(seen, dot(keys, q_all[me, h], NT) * SCALE, HIDDEN)
            m = jnp.max(s, axis=0, keepdims=True)
            e = jnp.exp(s - m)
            own_lw[h] = e
            own_st[h : h + 1, :] = m
            own_st[HEADS + h : HEADS + h + 1, :] = jnp.sum(e, axis=0, keepdims=True)
            own_ou[h] = dot(vt, e.astype(BF16))

    def own_weights_grad(h):
        d = dot(ov_ref[...], g_all[me, h], NT)
        own_dp[h] = d
        e = own_lw[h].astype(BF16).astype(F32)
        own_del[h : h + 1, :] = jnp.sum(e * d, axis=0, keepdims=True)

    def own_factor(h):
        return jnp.exp(own_st[h : h + 1, :] - lse_all[me, h : h + 1, :])

    def own_grads():
        kt = ok_ref[...].T
        for h in range(HEADS):
            w = own_lw[h] * own_factor(h)
            p_t[2, :BLK, head(h)] = w.astype(BF16)
            ds = (w * (own_dp[h] - lse_all[me, HEADS + h : HEADS + h + 1, :])).astype(BF16)
            ds_t[2, :BLK, head(h)] = ds
            own_qu[h] = dot(kt, ds)
        okg_ref[...] = (dot(ds_t[2, :BLK, :], q_all[me].reshape(ROWS, DH)) * SCALE).astype(BF16)
        ovg_ref[...] = dot(p_t[2, :BLK, :], g_all[me].reshape(ROWS, DH)).astype(BF16)

    def near_copy(D, d, w):
        return pltpu.make_async_remote_copy(
            src_ref=(nk, nv)[w].at[toward(D, d)], dst_ref=(fk, fv)[w].at[2 * D + d - 1],
            send_sem=f_send.at[D, d - 1, w], recv_sem=f_recv.at[D, d - 1, w],
            device_id={"ctx": toward(D, d)},
        )

    def near_scores(D, d):
        n = 2 * D + d - 1
        for w in range(2):
            near_copy(D, d, w).wait_recv()
        count = pick(me, from_behind(D, d) * CB_DEV)[2]
        bias = biases(count)
        tr[D] = fv[n].T
        for h in range(HEADS):
            m, e = local_scores(fk[n], q_all[me, h], bias)
            f_lw[n, h] = e
            f_max[n, h : h + 1, :] = m
            f_ou[n, h] = dot(tr[D], e.astype(BF16))
            f_dp[n, h] = dot(fv[n], g_all[me, h], NT)

    def near_grads(D, d):
        n = 2 * D + d - 1
        tr[D] = fk[n].T
        for h in range(HEADS):
            w = f_lw[n, h] * jnp.exp(f_max[n, h : h + 1, :] - lse_all[me, h : h + 1, :])
            ds = (w * (f_dp[n, h] - lse_all[me, HEADS + h : HEADS + h + 1, :])).astype(BF16)
            own_qu[h] += dot(tr[D], ds)

    def combine():
        st_in[me] = st_out[me]
        each_peer(lambda p: to_candidate(st_out, st_in, st_s, st_r, wrap(me + p), wrap(me + p)).wait_recv())
        maxima = st_in[:, :HEADS, :]
        totals = st_in[:, HEADS : 2 * HEADS, :]
        parts = st_in[:, 2 * HEADS : 3 * HEADS, :]
        own_max = own_st[:HEADS, :]
        top = jnp.maximum(jnp.max(maxima, axis=0), own_max)
        lift = jnp.exp(maxima - top[None])
        own_lift = jnp.exp(own_max - top)
        total = own_st[HEADS:, :] * own_lift + jnp.sum(totals * lift, axis=0)
        lse_all[me, :HEADS, :] = top + jnp.log(total)
        lse_all[me, HEADS:, :] = (own_del[:HEADS, :] * own_lift + jnp.sum(parts * lift, axis=0)) / total
        to_holder(lse_all, ls_s, ls_r, me, FAR).start()

        def both_sides(p):
            to_holder(lse_all, ls_s, ls_r, me, FAR - p).start()
            to_holder(lse_all, ls_s, ls_r, me, FAR + p).start()

        loop(1, FAR, both_sides)

    def buffers(chain, D, d):
        return sb.at[chain, D, d - 1 - NEAR], rb.at[chain, D, d - 1 - NEAR]

    def chain_copy(chain, D, d, b):
        src, dst = buffers(chain, D, d)
        rows = pl.ds(0, MARK + 16 if chain == 0 else MARK)
        return pltpu.make_async_remote_copy(
            src_ref=src.at[b, rows], dst_ref=dst.at[b, rows],
            send_sem=c_send.at[chain, D, d - 1, b], recv_sem=c_recv.at[chain, D, d - 1, b],
            device_id={"ctx": toward(D, NEAR + 1) if d == NEAR + 1 else nbr[D]},
        )

    def chain_step(chain, i):
        d = FAR - i
        for b in range(2):
            for D in ways(d + 1, b):
                chain_copy(chain, D, d + 1, b).wait_recv()
            for D in ways(d, b):
                c = toward(D, d)
                out = buffers(chain, D, d)[0]
                came = D in ways(d + 1, b)
                arrived = buffers(chain, D, d + 1)[1] if came else None
                if chain == 0 and came:
                    old = arrived[b, MARK:, :].astype(F32)
                marks = []
                for j in range(2):
                    h = 2 * b + j
                    if chain == 0:
                        m = st_out[c, h : h + 1, :]
                        r = jnp.ceil(m * 0.25) * 4.0
                        if came:
                            r = jnp.maximum(r, old[8 * j : 8 * j + 1])
                        x = ou[c, h] * jnp.exp(m - r)
                        if came:
                            x = x + arrived[b, head(j), :].astype(F32) * jnp.exp(old[8 * j : 8 * j + 1] - r)
                        marks.append(jnp.broadcast_to(r, (8, 128)))
                    else:
                        x = qu[c, h]
                        if came:
                            x = x + arrived[b, head(j), :].astype(F32)
                    out[b, head(j), :] = x.astype(out.dtype)
                if chain == 0:
                    out[b, MARK:, :] = jnp.concatenate(marks, axis=0).astype(out.dtype)
            for D in ways(d, b):
                chain_copy(chain, D, d, b).start()

    def chain_sent(chain, i):
        for b in range(2):
            for D in ways(FAR - i, b):
                chain_copy(chain, D, FAR - i, b).wait_send()

    def chain_grads(i):
        if is_int(i) and i == 0:
            grads(wrap(me + FAR), 0)
        else:
            grads(toward(0, FAR - i), 0)
            grads(toward(1, FAR - i), 1)

    def block_sum(b):
        a = jnp.zeros((BLK, DH), F32)
        g = jnp.zeros((BLK, DH), F32)
        for c in range(N):
            at = jnp.where(sel[c, 0] == b, 2 * c, jnp.where(sel[c, 1] == b, 2 * c + 1, EMPTY))
            a = a + dks[at]
            g = g + dvs[at]
        dk_ref[b] = (a * SCALE).astype(BF16)
        dv_ref[b] = g.astype(BF16)

    def query_step(t):
        gather_step(0, t)
        for c, D in behind(t):
            if not is_int(t) or t > NEAR:
                stage(c)
            bias = score_bias(c, D)
            for h in range(HEADS):
                scores(c, D, h, bias)

    def grad_step(t):
        gather_step(1, t)
        for c, D in behind(t):
            for h in range(HEADS):
                weights_grad(c, h)
        for c, D in behind(t):
            to_candidate(st_out, st_in, st_s, st_r, c, me).start()

    def gather_slot(s):
        pace()
        query_step(s)
        grad_step(s - 1)

    gather_first(0)
    gather_first(1)
    for d in range(1, NEAR + 1):
        for D in range(2):
            stage(toward(D, d))
            for w in range(2):
                near_copy(D, d, w).start()
    own_scores()
    stage(me)
    bias_me = score_bias(me, 0)
    for h in range(HEADS):
        scores(me, 0, h, bias_me)
    pace(False)
    query_step(1)
    gather_slot(2)
    loop(3, 7, gather_slot)
    gather_slot(7)
    gather_slot(8)

    chain_step(0, 0)
    grad_step(8)
    for h in range(HEADS):
        weights_grad(me, h)
        own_weights_grad(h)
    dks[EMPTY] = jnp.zeros((BLK, DH), F32)
    dvs[EMPTY] = jnp.zeros((BLK, DH), F32)
    pace()
    chain_step(0, 1)
    near_scores(0, 1)
    near_scores(1, 1)
    pace()
    chain_step(0, 2)
    combine()
    pace()
    chain_step(0, 3)
    near_scores(0, 2)
    near_scores(1, 2)
    for t in range(1, 9):
        gather_sent(0, t)
    pace()
    chain_step(0, 4)
    each_peer(lambda p: to_holder(lse_all, ls_s, ls_r, wrap(me + p), p).wait_recv())
    fac[:, :HEADS, :] = jnp.exp(st_out[:, :HEADS, :] - lse_all[:, :HEADS, :])

    chain_grads(0)
    chain_step(1, 0)
    chain_grads(1)
    pace()
    chain_step(0, 5)
    chain_step(1, 1)
    chain_grads(2)
    for D in range(2):
        grads(toward(D, 2), D, False)
    own_grads()
    pace()
    chain_step(1, 2)
    chain_grads(3)
    for D in range(2):
        grads(toward(D, 1), D, False)
    near_grads(0, 1)
    near_grads(1, 1)
    pace()
    chain_step(1, 3)
    chain_grads(4)
    grads(me, 0)
    last = NEAR + 1
    for h in range(HEADS):
        b, j = h // 2, h % 2
        x = own_ou[h] * own_factor(h) + ou[me, h] * fac[me, h : h + 1, :]
        for n in range(2 * NEAR):
            x = x + f_ou[n, h] * jnp.exp(f_max[n, h : h + 1, :] - lse_all[me, h : h + 1, :])
        for D in range(2):
            if j == 0:
                chain_copy(0, D, last, b).wait_recv()
            came = buffers(0, D, last)[1]
            r = came[b, MARK:, :].astype(F32)[8 * j : 8 * j + 1]
            x = x + came[b, head(j), :].astype(F32) * jnp.exp(r - lse_all[me, h : h + 1, :])
        att_ref[:, head(h)] = x.T.astype(BF16)
    pace()
    chain_step(1, 4)
    chain_grads(5)
    near_grads(0, 2)
    near_grads(1, 2)
    for t in range(1, 9):
        gather_sent(1, t)
    pace()
    chain_step(1, 5)
    loop(0, CB_DEV, block_sum)
    each_peer(lambda p: to_candidate(st_out, st_in, st_s, st_r, wrap(me + p), me).wait_send())
    each_peer(lambda p: to_holder(lse_all, ls_s, ls_r, me, p).wait_send())
    for d in range(1, NEAR + 1):
        for D in range(2):
            for w in range(2):
                near_copy(D, d, w).wait_send()
    for i in range(6):
        chain_sent(0, i)
    for i in range(5):
        chain_sent(1, i)
    if paired:
        pl.semaphore_wait(pace_sem, 1)
    for h in range(HEADS):
        b, j = h // 2, h % 2
        x = own_qu[h] + qu[me, h]
        for D in range(2):
            if j == 0:
                chain_copy(1, D, last, b).wait_recv()
            x = x + buffers(1, D, last)[1][b, head(j), :].astype(F32)
        qg_ref[:, head(h)] = (x * SCALE).T.astype(BF16)
    chain_sent(1, 5)


def ring(ids, q, k, v, ok, ov, g):
    vm = pl.BlockSpec(memory_space=pltpu.VMEM)
    shape = jax.ShapeDtypeStruct
    V = pltpu.VMEM
    D = pltpu.SemaphoreType.DMA
    message = (2, MARK + 16, 128)
    tile = (HEADS, 128, 128)
    return pl.pallas_call(
        ring_kernel,
        in_specs=[pl.BlockSpec(memory_space=pltpu.SMEM)] + [vm] * 6,
        out_specs=[vm] * 6,
        out_shape=[
            shape((128, ROWS), BF16), shape((128, ROWS), BF16),
            shape((BLK, DH), BF16), shape((BLK, DH), BF16),
            shape((CB_DEV, BLK, DH), BF16), shape((CB_DEV, BLK, DH), BF16),
        ],
        scratch_shapes=[
            V((N,) + tile, BF16), V((N,) + tile, BF16),
            V((N, KEYS, DH), BF16), V((N, KEYS, DH), BF16),
            V((N, HEADS, KEYS, 128), F32), V((N, HEADS, KEYS, 128), F32),
            V((N,) + tile, F32), V((N,) + tile, F32),
            V(tile, F32), V(tile, F32), V(tile, F32), V(tile, F32),
            V((8, 128), F32), V((8, 128), F32),
            V((N, 16, 128), F32), V((N, 16, 128), F32), V((N, 8, 128), F32), V((N, 8, 128), F32),
            V((3, KEYS, ROWS), BF16), V((3, KEYS, ROWS), BF16), V((2, DH, KEYS), BF16),
            V((2 * N + 1, BLK, DH), F32), V((2 * N + 1, BLK, DH), F32),
            pltpu.SMEM((N, 2), jnp.int32),
            V((2, 2, FAR - NEAR) + message, BF16), V((2, 2, FAR - NEAR) + message, BF16),
            V((2 * NEAR, KEYS, DH), BF16), V((2 * NEAR, KEYS, DH), BF16),
            V((2 * NEAR, HEADS, KEYS, 128), F32), V((2 * NEAR, HEADS, KEYS, 128), F32),
            V((2 * NEAR,) + tile, F32), V((2 * NEAR, 8, 128), F32),
            D((2, 2, FAR, 2)), D((2, 2, FAR, 2)), D((2, 2, FAR, 2)), D((2, 2, FAR, 2)),
            D((N,)), D((N,)), D((N,)), D((N,)), D((2, NEAR, 2)), D((2, NEAR, 2)),
            pltpu.SemaphoreType.REGULAR,
        ],
        compiler_params=pltpu.CompilerParams(
            collective_id=0, has_side_effects=True, vmem_limit_bytes=60 * 1024 * 1024
        ),
        name="ring_attention",
    )(ids, q, k, v, ok, ov, g)


def hand_on_kernel(*refs):
    n = len(refs) // 2
    for j in range(n):
        refs[n + j][...] = refs[j][...]


def hand_on(parts):
    vm = pl.BlockSpec(memory_space=pltpu.VMEM)
    return pl.pallas_call(
        hand_on_kernel,
        in_specs=[vm] * len(parts),
        out_specs=[vm] * len(parts),
        out_shape=[jax.ShapeDtypeStruct(x.shape, x.dtype) for x in parts],
        compiler_params=pltpu.CompilerParams(vmem_limit_bytes=60 * 1024 * 1024),
        name="hand_on",
    )(*parts)


def on_device(queries, context_keys, context_values, own_keys, own_values, out_grad, block_ids):
    k = context_keys.reshape(CB_DEV, BLK, DH)
    v = context_values.reshape(CB_DEV, BLK, DH)
    parts = ring(block_ids, queries, k, v, own_keys, own_values, out_grad)
    att, qg, okg, ovg, dk, dv = hand_on(parts)
    return att, qg, dk.reshape(CB_DEV * BLK, DH), dv.reshape(CB_DEV * BLK, DH), okg, ovg


def solution(mesh):
    rows = P(("dp", "ctx"), "head")
    return jax.shard_map(
        on_device,
        mesh=mesh,
        in_specs=(rows,) * 6 + (P("dp", None),),
        out_specs=(rows,) * 6,
        check_vma=False,
    )
```

```python
import math

import jax
import jax.numpy as jnp
from jax import lax
from jax.experimental import pallas as pl
from jax.experimental.pallas import tpu as pltpu
from jax.sharding import PartitionSpec as P

N = 16
BLK = 128
DH = 128
HEADS = 4
ROWS = HEADS * 128
KEYS = 2 * BLK
SLOTS = 24
CB_DEV = 16
EMPTY = 2 * N
SCALE = 1.0 / math.sqrt(DH)
HIDDEN = -1e30
FLOOR = -(2.0**83)
NEAR = 2
FAR = 8
MARK = 256
F32 = jnp.float32
BF16 = jnp.bfloat16
NT = (((1,), (1,)), ((), ()))
NN = (((1,), (0,)), ((), ()))


def dot(a, b, dims=NN):
    return lax.dot_general(a, b, dims, preferred_element_type=F32)


def wrap(x):
    return lax.rem(x + 2 * N, N)


def head(h):
    return slice(h * 128, (h + 1) * 128)


def is_int(x):
    return isinstance(x, int)


def ring_kernel(
    ids_ref, q_ref, k_ref, v_ref, ok_ref, ov_ref, g_ref,
    att_ref, qg_ref, okg_ref, ovg_ref, dk_ref, dv_ref,
    q_all, g_all, nk, nv, lw, dp, ou, qu,
    own_lw, own_dp, own_ou, own_qu, own_st, own_del,
    st_out, st_in, lse_all, fac,
    ds_t, p_t, tr, dks, dvs, sel, sb, rb,
    fk, fv, f_lw, f_dp, f_ou, f_max,
    g_send, g_recv, c_send, c_recv, st_s, st_r, ls_s, ls_r, f_send, f_recv, pace_sem,
):
    me = lax.axis_index("ctx")
    low = me * CB_DEV
    nbr = (wrap(me + 1), wrap(me - 1))

    barrier = pltpu.get_barrier_semaphore()

    def loop(lo, hi, fn):
        def body(t, _):
            fn(t)
            return 0

        lax.fori_loop(lo, hi, body, 0)

    def each_peer(fn):
        loop(1, N, fn)

    paired = lax.axis_size("head") % 2 == 0
    side = lax.axis_index("head")
    other = side + 1 - 2 * lax.rem(side, 2)

    def pace(wait=True):
        if paired:
            pl.semaphore_signal(pace_sem, inc=1, device_id={"head": other})
            if wait:
                pl.semaphore_wait(pace_sem, 1)

    each_peer(lambda p: pl.semaphore_signal(barrier, inc=1, device_id={"ctx": wrap(me + p)}))
    if paired:
        pl.semaphore_signal(barrier, inc=1, device_id={"head": other})
    for h in range(HEADS):
        q_all[me, h] = q_ref[:, head(h)]
        g_all[me, h] = g_ref[:, head(h)]
    pl.semaphore_wait(barrier, N if paired else N - 1)

    def gather_copy(stream, D, t, b, c):
        part = (q_all, g_all)[stream].at[c, pl.ds(2 * b, 2)]
        return pltpu.make_async_remote_copy(
            src_ref=part, dst_ref=part,
            send_sem=g_send.at[stream, D, t - 1, b], recv_sem=g_recv.at[stream, D, t - 1, b],
            device_id={"ctx": nbr[D]},
        )

    def toward(D, d):
        return wrap(me + d) if D == 0 else wrap(me - d)

    def from_behind(D, t):
        return toward(1 - D, t)

    def ways(d, b):
        return (b,) if is_int(d) and d == FAR else () if is_int(d) and d > FAR else (0, 1)

    def behind(t):
        if is_int(t) and t == FAR:
            return ((wrap(me + FAR), 0),)
        return ((from_behind(0, t), 0), (from_behind(1, t), 1))

    def gather_step(stream, t):
        for b in range(2):
            for D in ways(t, b):
                gather_copy(stream, D, t, b, from_behind(D, t)).wait_recv()
            for D in ways(t + 1, b):
                gather_copy(stream, D, t + 1, b, from_behind(D, t)).start()

    def gather_first(stream):
        for b in range(2):
            for D in range(2):
                gather_copy(stream, D, 1, b, me).start()

    def gather_sent(stream, t):
        for b in range(2):
            for D in ways(t, b):
                gather_copy(stream, D, t, b, me).wait_send()

    def to_candidate(src, dst, send, recv, c, slot):
        return pltpu.make_async_remote_copy(
            src_ref=src.at[c], dst_ref=dst.at[slot], send_sem=send.at[c], recv_sem=recv.at[slot],
            device_id={"ctx": c},
        )

    def to_holder(buf, send, recv, slot, p):
        return pltpu.make_async_remote_copy(
            src_ref=buf.at[slot], dst_ref=buf.at[slot], send_sem=send.at[p], recv_sem=recv.at[slot],
            device_id={"ctx": wrap(me + p)},
        )

    def biases(count):
        return (
            jnp.where(count >= 1, 0.0, HIDDEN).astype(F32),
            jnp.where(count >= 2, 0.0, HIDDEN).astype(F32),
        )

    def pick(c, low):
        first = jnp.int32(CB_DEV)
        last = jnp.int32(-1)
        count = jnp.int32(0)
        for j in range(SLOTS):
            b = ids_ref[c, j] - low
            inside = (b >= 0) & (b < CB_DEV)
            first = jnp.where(inside, jnp.minimum(first, b), first)
            last = jnp.where(inside, jnp.maximum(last, b), last)
            count = count + jnp.where(inside, 1, 0)
        return first, last, count

    def stage(c):
        first, last, count = pick(c, low)
        sel[c, 0] = jnp.where(count >= 1, first, -1)
        sel[c, 1] = jnp.where(count >= 2, last, -1)
        first = jnp.minimum(first, CB_DEV - 1)
        last = jnp.maximum(last, 0)
        nk[c, :BLK, :] = k_ref[first]
        nk[c, BLK:, :] = k_ref[last]
        nv[c, :BLK, :] = v_ref[first]
        nv[c, BLK:, :] = v_ref[last]

    def score_bias(c, D):
        tr[D] = nv[c].T
        return (
            jnp.where(sel[c, 0] >= 0, 0.0, HIDDEN).astype(F32),
            jnp.where(sel[c, 1] >= 0, 0.0, HIDDEN).astype(F32),
        )

    def local_scores(keys, q, bias):
        s = dot(keys, q, NT) * SCALE
        s0 = s[:BLK] + bias[0]
        s1 = s[BLK:] + bias[1]
        m = jnp.max(jnp.maximum(s0, s1), axis=0, keepdims=True)
        m = jnp.maximum(m, FLOOR)
        return m, jnp.exp(jnp.concatenate([s0, s1], axis=0) - m)

    def scores(c, D, h, bias):
        m, e = local_scores(nk[c], q_all[c, h], bias)
        lw[c, h] = e
        st_out[c, h : h + 1, :] = m
        st_out[c, HEADS + h : HEADS + h + 1, :] = jnp.sum(e, axis=0, keepdims=True)
        ou[c, h] = dot(tr[D], e.astype(BF16))

    def weights_grad(c, h):
        d = dot(nv[c], g_all[c, h], NT)
        dp[c, h] = d
        e = lw[c, h].astype(BF16).astype(F32)
        st_out[c, 2 * HEADS + h : 2 * HEADS + h + 1, :] = jnp.sum(e * d, axis=0, keepdims=True)

    def grads(c, D, back=True):
        if back:
            tr[D] = nk[c].T
        for h in range(HEADS):
            w = lw[c, h] * fac[c, h : h + 1, :]
            p_t[D, :, head(h)] = w.astype(BF16)
            ds = (w * (dp[c, h] - lse_all[c, HEADS + h : HEADS + h + 1, :])).astype(BF16)
            ds_t[D, :, head(h)] = ds
            if back:
                qu[c, h] = dot(tr[D], ds)
        a = dot(ds_t[D], q_all[c].reshape(ROWS, DH))
        b = dot(p_t[D], g_all[c].reshape(ROWS, DH))
        for slot in range(2):
            rows = slice(slot * BLK, (slot + 1) * BLK)
            dks[2 * c + slot] = a[rows]
            dvs[2 * c + slot] = b[rows]

    def own_scores():
        keys = ok_ref[...]
        vt = ov_ref[...].T
        seen = lax.broadcasted_iota(jnp.int32, (BLK, 128), 0) <= lax.broadcasted_iota(jnp.int32, (BLK, 128), 1)
        for h in range(HEADS):
            s = jnp.where(seen, dot(keys, q_all[me, h], NT) * SCALE, HIDDEN)
            m = jnp.max(s, axis=0, keepdims=True)
            e = jnp.exp(s - m)
            own_lw[h] = e
            own_st[h : h + 1, :] = m
            own_st[HEADS + h : HEADS + h + 1, :] = jnp.sum(e, axis=0, keepdims=True)
            own_ou[h] = dot(vt, e.astype(BF16))

    def own_weights_grad(h):
        d = dot(ov_ref[...], g_all[me, h], NT)
        own_dp[h] = d
        e = own_lw[h].astype(BF16).astype(F32)
        own_del[h : h + 1, :] = jnp.sum(e * d, axis=0, keepdims=True)

    def own_factor(h):
        return jnp.exp(own_st[h : h + 1, :] - lse_all[me, h : h + 1, :])

    def own_grads():
        kt = ok_ref[...].T
        for h in range(HEADS):
            w = own_lw[h] * own_factor(h)
            p_t[2, :BLK, head(h)] = w.astype(BF16)
            ds = (w * (own_dp[h] - lse_all[me, HEADS + h : HEADS + h + 1, :])).astype(BF16)
            ds_t[2, :BLK, head(h)] = ds
            own_qu[h] = dot(kt, ds)
        okg_ref[...] = (dot(ds_t[2, :BLK, :], q_all[me].reshape(ROWS, DH)) * SCALE).astype(BF16)
        ovg_ref[...] = dot(p_t[2, :BLK, :], g_all[me].reshape(ROWS, DH)).astype(BF16)

    def near_copy(D, d, w):
        return pltpu.make_async_remote_copy(
            src_ref=(nk, nv)[w].at[toward(D, d)], dst_ref=(fk, fv)[w].at[2 * D + d - 1],
            send_sem=f_send.at[D, d - 1, w], recv_sem=f_recv.at[D, d - 1, w],
            device_id={"ctx": toward(D, d)},
        )

    def near_send(d):
        for w in range(2):
            for D in range(2):
                near_copy(D, d, w).start()

    def near_scores(D, d):
        n = 2 * D + d - 1
        for w in range(2):
            near_copy(D, d, w).wait_recv()
        count = pick(me, from_behind(D, d) * CB_DEV)[2]
        bias = biases(count)
        tr[D] = fv[n].T
        for h in range(HEADS):
            m, e = local_scores(fk[n], q_all[me, h], bias)
            f_lw[n, h] = e
            f_max[n, h : h + 1, :] = m
            f_ou[n, h] = dot(tr[D], e.astype(BF16))
            f_dp[n, h] = dot(fv[n], g_all[me, h], NT)

    def near_grads(D, d):
        n = 2 * D + d - 1
        tr[D] = fk[n].T
        for h in range(HEADS):
            w = f_lw[n, h] * jnp.exp(f_max[n, h : h + 1, :] - lse_all[me, h : h + 1, :])
            ds = (w * (f_dp[n, h] - lse_all[me, HEADS + h : HEADS + h + 1, :])).astype(BF16)
            own_qu[h] += dot(tr[D], ds)

    def combine():
        st_in[me] = st_out[me]
        each_peer(lambda p: to_candidate(st_out, st_in, st_s, st_r, wrap(me + p), wrap(me + p)).wait_recv())
        maxima = st_in[:, :HEADS, :]
        totals = st_in[:, HEADS : 2 * HEADS, :]
        parts = st_in[:, 2 * HEADS : 3 * HEADS, :]
        own_max = own_st[:HEADS, :]
        top = jnp.maximum(jnp.max(maxima, axis=0), own_max)
        lift = jnp.exp(maxima - top[None])
        own_lift = jnp.exp(own_max - top)
        total = own_st[HEADS:, :] * own_lift + jnp.sum(totals * lift, axis=0)
        lse_all[me, :HEADS, :] = top + jnp.log(total)
        lse_all[me, HEADS:, :] = (own_del[:HEADS, :] * own_lift + jnp.sum(parts * lift, axis=0)) / total
        to_holder(lse_all, ls_s, ls_r, me, FAR).start()

        def both_sides(p):
            to_holder(lse_all, ls_s, ls_r, me, FAR - p).start()
            to_holder(lse_all, ls_s, ls_r, me, FAR + p).start()

        loop(1, FAR, both_sides)

    def buffers(chain, D, d):
        return sb.at[chain, D, d - 1 - NEAR], rb.at[chain, D, d - 1 - NEAR]

    PARTS = (((0, 1), (2, 3)), ((0,), (1,), (2,), (3,)))

    def chain_copy(chain, D, d, heads):
        src, dst = buffers(chain, D, d)
        b, j = heads[0] // 2, heads[0] % 2
        rows = pl.ds(0, MARK + 16) if chain == 0 else pl.ds(j * 128, 128)
        return pltpu.make_async_remote_copy(
            src_ref=src.at[b, rows], dst_ref=dst.at[b, rows],
            send_sem=c_send.at[chain, D, d - 1, heads[0]], recv_sem=c_recv.at[chain, D, d - 1, heads[0]],
            device_id={"ctx": toward(D, NEAR + 1) if d == NEAR + 1 else nbr[D]},
        )

    def chain_step(chain, i):
        d = FAR - i
        for heads in PARTS[chain]:
            b = heads[0] // 2
            for D in ways(d + 1, b):
                chain_copy(chain, D, d + 1, heads).wait_recv()
            for D in ways(d, b):
                c = toward(D, d)
                out = buffers(chain, D, d)[0]
                came = D in ways(d + 1, b)
                arrived = buffers(chain, D, d + 1)[1] if came else None
                if chain == 0 and came:
                    old = arrived[b, MARK:, :].astype(F32)
                marks = []
                for h in heads:
                    j = h % 2
                    if chain == 0:
                        m = st_out[c, h : h + 1, :]
                        r = jnp.ceil(m * 0.25) * 4.0
                        if came:
                            r = jnp.maximum(r, old[8 * j : 8 * j + 1])
                        x = ou[c, h] * jnp.exp(m - r)
                        if came:
                            x = x + arrived[b, head(j), :].astype(F32) * jnp.exp(old[8 * j : 8 * j + 1] - r)
                        marks.append(jnp.broadcast_to(r, (8, 128)))
                    else:
                        x = qu[c, h]
                        if came:
                            x = x + arrived[b, head(j), :].astype(F32)
                    out[b, head(j), :] = x.astype(out.dtype)
                if chain == 0:
                    out[b, MARK:, :] = jnp.concatenate(marks, axis=0).astype(out.dtype)
            for D in ways(d, b):
                chain_copy(chain, D, d, heads).start()

    def chain_sent(chain, i):
        for heads in PARTS[chain]:
            for D in ways(FAR - i, heads[0] // 2):
                chain_copy(chain, D, FAR - i, heads).wait_send()

    def chain_grads(i):
        if is_int(i) and i == 0:
            grads(wrap(me + FAR), 0)
        else:
            grads(toward(0, FAR - i), 0)
            grads(toward(1, FAR - i), 1)

    def block_sum(b):
        a = jnp.zeros((BLK, DH), F32)
        g = jnp.zeros((BLK, DH), F32)
        for c in range(N):
            at = jnp.where(sel[c, 0] == b, 2 * c, jnp.where(sel[c, 1] == b, 2 * c + 1, EMPTY))
            a = a + dks[at]
            g = g + dvs[at]
        dk_ref[b] = (a * SCALE).astype(BF16)
        dv_ref[b] = g.astype(BF16)

    def query_step(t):
        gather_step(0, t)
        for c, D in behind(t):
            if not is_int(t) or t > NEAR:
                stage(c)
            bias = score_bias(c, D)
            for h in range(HEADS):
                scores(c, D, h, bias)

    def grad_step(t):
        gather_step(1, t)
        for c, D in behind(t):
            for h in range(HEADS):
                weights_grad(c, h)
        for c, D in behind(t):
            to_candidate(st_out, st_in, st_s, st_r, c, me).start()

    def gather_slot(s):
        pace()
        query_step(s)
        grad_step(s - 1)

    gather_first(0)
    gather_first(1)
    for d in range(1, NEAR + 1):
        for D in range(2):
            stage(toward(D, d))
    own_scores()
    stage(me)
    bias_me = score_bias(me, 0)
    for h in range(HEADS):
        scores(me, 0, h, bias_me)
    pace(False)
    query_step(1)
    gather_slot(2)
    loop(3, 7, gather_slot)
    gather_slot(7)
    gather_slot(8)

    chain_step(0, 0)
    grad_step(8)
    for h in range(HEADS):
        weights_grad(me, h)
        own_weights_grad(h)
    dks[EMPTY] = jnp.zeros((BLK, DH), F32)
    dvs[EMPTY] = jnp.zeros((BLK, DH), F32)
    near_send(1)
    pace()
    chain_step(0, 1)
    near_send(2)
    pace()
    chain_step(0, 2)
    combine()
    pace()
    chain_step(0, 3)
    near_scores(0, 1)
    near_scores(1, 1)
    for t in range(1, 9):
        gather_sent(0, t)
    pace()
    chain_step(0, 4)
    each_peer(lambda p: to_holder(lse_all, ls_s, ls_r, wrap(me + p), p).wait_recv())
    fac[:, :HEADS, :] = jnp.exp(st_out[:, :HEADS, :] - lse_all[:, :HEADS, :])

    chain_grads(0)
    chain_step(1, 0)
    chain_grads(1)
    pace()
    chain_step(0, 5)
    chain_step(1, 1)
    chain_grads(2)
    for D in range(2):
        grads(toward(D, 2), D, False)
    own_grads()
    pace()
    chain_step(1, 2)
    chain_grads(3)
    near_scores(0, 2)
    near_scores(1, 2)
    for D in range(2):
        grads(toward(D, 1), D, False)
    pace()
    chain_step(1, 3)
    chain_grads(4)
    grads(me, 0)
    last = NEAR + 1
    for h in range(HEADS):
        b, j = h // 2, h % 2
        x = own_ou[h] * own_factor(h) + ou[me, h] * fac[me, h : h + 1, :]
        for n in range(2 * NEAR):
            x = x + f_ou[n, h] * jnp.exp(f_max[n, h : h + 1, :] - lse_all[me, h : h + 1, :])
        for D in range(2):
            if j == 0:
                chain_copy(0, D, last, (h, h + 1)).wait_recv()
            came = buffers(0, D, last)[1]
            r = came[b, MARK:, :].astype(F32)[8 * j : 8 * j + 1]
            x = x + came[b, head(j), :].astype(F32) * jnp.exp(r - lse_all[me, h : h + 1, :])
        att_ref[:, head(h)] = x.T.astype(BF16)
    pace()
    chain_step(1, 4)
    chain_grads(5)
    near_grads(0, 1)
    near_grads(1, 1)
    near_grads(0, 2)
    near_grads(1, 2)
    for t in range(1, 9):
        gather_sent(1, t)
    pace()
    chain_step(1, 5)
    loop(0, CB_DEV, block_sum)
    each_peer(lambda p: to_candidate(st_out, st_in, st_s, st_r, wrap(me + p), me).wait_send())
    each_peer(lambda p: to_holder(lse_all, ls_s, ls_r, me, p).wait_send())
    for d in range(1, NEAR + 1):
        for D in range(2):
            for w in range(2):
                near_copy(D, d, w).wait_send()
    for i in range(6):
        chain_sent(0, i)
    for i in range(5):
        chain_sent(1, i)
    if paired:
        pl.semaphore_wait(pace_sem, 1)
    for h in range(HEADS):
        b, j = h // 2, h % 2
        x = own_qu[h] + qu[me, h]
        for D in range(2):
            chain_copy(1, D, last, (h,)).wait_recv()
            x = x + buffers(1, D, last)[1][b, head(j), :].astype(F32)
        qg_ref[:, head(h)] = (x * SCALE).T.astype(BF16)
    chain_sent(1, 5)


def ring(ids, q, k, v, ok, ov, g):
    vm = pl.BlockSpec(memory_space=pltpu.VMEM)
    shape = jax.ShapeDtypeStruct
    V = pltpu.VMEM
    D = pltpu.SemaphoreType.DMA
    message = (2, MARK + 16, 128)
    tile = (HEADS, 128, 128)
    return pl.pallas_call(
        ring_kernel,
        in_specs=[pl.BlockSpec(memory_space=pltpu.SMEM)] + [vm] * 6,
        out_specs=[vm] * 6,
        out_shape=[
            shape((128, ROWS), BF16), shape((128, ROWS), BF16),
            shape((BLK, DH), BF16), shape((BLK, DH), BF16),
            shape((CB_DEV, BLK, DH), BF16), shape((CB_DEV, BLK, DH), BF16),
        ],
        scratch_shapes=[
            V((N,) + tile, BF16), V((N,) + tile, BF16),
            V((N, KEYS, DH), BF16), V((N, KEYS, DH), BF16),
            V((N, HEADS, KEYS, 128), F32), V((N, HEADS, KEYS, 128), F32),
            V((N,) + tile, F32), V((N,) + tile, F32),
            V(tile, F32), V(tile, F32), V(tile, F32), V(tile, F32),
            V((8, 128), F32), V((8, 128), F32),
            V((N, 16, 128), F32), V((N, 16, 128), F32), V((N, 8, 128), F32), V((N, 8, 128), F32),
            V((3, KEYS, ROWS), BF16), V((3, KEYS, ROWS), BF16), V((2, DH, KEYS), BF16),
            V((2 * N + 1, BLK, DH), F32), V((2 * N + 1, BLK, DH), F32),
            pltpu.SMEM((N, 2), jnp.int32),
            V((2, 2, FAR - NEAR) + message, BF16), V((2, 2, FAR - NEAR) + message, BF16),
            V((2 * NEAR, KEYS, DH), BF16), V((2 * NEAR, KEYS, DH), BF16),
            V((2 * NEAR, HEADS, KEYS, 128), F32), V((2 * NEAR, HEADS, KEYS, 128), F32),
            V((2 * NEAR,) + tile, F32), V((2 * NEAR, 8, 128), F32),
            D((2, 2, FAR, 2)), D((2, 2, FAR, 2)), D((2, 2, FAR, HEADS)), D((2, 2, FAR, HEADS)),
            D((N,)), D((N,)), D((N,)), D((N,)), D((2, NEAR, 2)), D((2, NEAR, 2)),
            pltpu.SemaphoreType.REGULAR,
        ],
        compiler_params=pltpu.CompilerParams(
            collective_id=0, has_side_effects=True, vmem_limit_bytes=60 * 1024 * 1024
        ),
        name="ring_attention",
    )(ids, q, k, v, ok, ov, g)


def hand_on_kernel(*refs):
    n = len(refs) // 2
    for j in range(n):
        refs[n + j][...] = refs[j][...]


def hand_on(parts):
    vm = pl.BlockSpec(memory_space=pltpu.VMEM)
    return pl.pallas_call(
        hand_on_kernel,
        in_specs=[vm] * len(parts),
        out_specs=[vm] * len(parts),
        out_shape=[jax.ShapeDtypeStruct(x.shape, x.dtype) for x in parts],
        compiler_params=pltpu.CompilerParams(vmem_limit_bytes=60 * 1024 * 1024),
        name="hand_on",
    )(*parts)


def on_device(queries, context_keys, context_values, own_keys, own_values, out_grad, block_ids):
    k = context_keys.reshape(CB_DEV, BLK, DH)
    v = context_values.reshape(CB_DEV, BLK, DH)
    parts = ring(block_ids, queries, k, v, own_keys, own_values, out_grad)
    att, qg, okg, ovg, dk, dv = hand_on(parts)
    return att, qg, dk.reshape(CB_DEV * BLK, DH), dv.reshape(CB_DEV * BLK, DH), okg, ovg


def solution(mesh):
    rows = P(("dp", "ctx"), "head")
    return jax.shard_map(
        on_device,
        mesh=mesh,
        in_specs=(rows,) * 6 + (P("dp", None),),
        out_specs=(rows,) * 6,
        check_vma=False,
    )
```

```python
import math

import jax
import jax.numpy as jnp
from jax import lax
from jax.experimental import pallas as pl
from jax.experimental.pallas import tpu as pltpu
from jax.sharding import PartitionSpec as P

N = 16
BLK = 128
DH = 128
HEADS = 4
ROWS = HEADS * 128
KEYS = 2 * BLK
SLOTS = 24
CB_DEV = 16
EMPTY = 2 * N
SCALE = 1.0 / math.sqrt(DH)
HIDDEN = -1e30
FLOOR = -(2.0**83)
NEAR = 2
FAR = 8
MARK = 256
F32 = jnp.float32
BF16 = jnp.bfloat16
NT = (((1,), (1,)), ((), ()))
NN = (((1,), (0,)), ((), ()))


def dot(a, b, dims=NN):
    return lax.dot_general(a, b, dims, preferred_element_type=F32)


def wrap(x):
    return lax.rem(x + 2 * N, N)


def head(h):
    return slice(h * 128, (h + 1) * 128)


def is_int(x):
    return isinstance(x, int)


def ring_kernel(
    ids_ref, q_ref, k_hbm, v_hbm, ok_ref, ov_ref, g_ref,
    att_ref, qg_ref, okg_ref, ovg_ref, dk_ref, dv_ref,
    q_all, g_all, nk, nv, lw, dp, ou, qu,
    own_lw, own_dp, own_ou, own_qu, own_st, own_del,
    st_out, st_in, lse_all, fac,
    ds_t, p_t, tr, dks, dvs, sel, sb, rb,
    fk, fv, f_lw, f_dp, f_ou, f_max,
    g_send, g_recv, c_send, c_recv, st_s, st_r, ls_s, ls_r, f_send, f_recv, pace_sem, k_ref, v_ref, kv_sem,
):
    me = lax.axis_index("ctx")
    low = me * CB_DEV
    nbr = (wrap(me + 1), wrap(me - 1))

    blocks_in = (
        pltpu.make_async_copy(k_hbm, k_ref, kv_sem.at[0]),
        pltpu.make_async_copy(v_hbm, v_ref, kv_sem.at[1]),
    )
    for copy in blocks_in:
        copy.start()
    barrier = pltpu.get_barrier_semaphore()

    def loop(lo, hi, fn):
        def body(t, _):
            fn(t)
            return 0

        lax.fori_loop(lo, hi, body, 0)

    def each_peer(fn):
        loop(1, N, fn)

    paired = lax.axis_size("head") % 2 == 0
    side = lax.axis_index("head")
    other = side + 1 - 2 * lax.rem(side, 2)

    def pace():
        if paired:
            pl.semaphore_signal(pace_sem, inc=1, device_id={"head": other})
            pl.semaphore_wait(pace_sem, 1)

    each_peer(lambda p: pl.semaphore_signal(barrier, inc=1, device_id={"ctx": wrap(me + p)}))
    if paired:
        pl.semaphore_signal(barrier, inc=1, device_id={"head": other})
    for h in range(HEADS):
        q_all[me, h] = q_ref[:, head(h)]
        g_all[me, h] = g_ref[:, head(h)]
    pl.semaphore_wait(barrier, N if paired else N - 1)

    def gather_copy(stream, D, t, b, c):
        part = (q_all, g_all)[stream].at[c, pl.ds(2 * b, 2)]
        return pltpu.make_async_remote_copy(
            src_ref=part, dst_ref=part,
            send_sem=g_send.at[stream, D, t - 1, b], recv_sem=g_recv.at[stream, D, t - 1, b],
            device_id={"ctx": nbr[D]},
        )

    def toward(D, d):
        return wrap(me + d) if D == 0 else wrap(me - d)

    def from_behind(D, t):
        return toward(1 - D, t)

    def ways(d, b):
        return (b,) if is_int(d) and d == FAR else () if is_int(d) and d > FAR else (0, 1)

    def behind(t):
        if is_int(t) and t == FAR:
            return ((wrap(me + FAR), 0),)
        return ((from_behind(0, t), 0), (from_behind(1, t), 1))

    def gather_step(stream, t):
        for b in range(2):
            for D in ways(t, b):
                gather_copy(stream, D, t, b, from_behind(D, t)).wait_recv()
            for D in ways(t + 1, b):
                gather_copy(stream, D, t + 1, b, from_behind(D, t)).start()

    def gather_first(stream):
        for b in range(2):
            for D in range(2):
                gather_copy(stream, D, 1, b, me).start()

    def gather_sent(stream, t):
        for b in range(2):
            for D in ways(t, b):
                gather_copy(stream, D, t, b, me).wait_send()

    def to_candidate(src, dst, send, recv, c, slot):
        return pltpu.make_async_remote_copy(
            src_ref=src.at[c], dst_ref=dst.at[slot], send_sem=send.at[c], recv_sem=recv.at[slot],
            device_id={"ctx": c},
        )

    def to_holder(buf, send, recv, slot, p):
        return pltpu.make_async_remote_copy(
            src_ref=buf.at[slot], dst_ref=buf.at[slot], send_sem=send.at[p], recv_sem=recv.at[slot],
            device_id={"ctx": wrap(me + p)},
        )

    def biases(count):
        return (
            jnp.where(count >= 1, 0.0, HIDDEN).astype(F32),
            jnp.where(count >= 2, 0.0, HIDDEN).astype(F32),
        )

    def pick(c, low):
        first = jnp.int32(CB_DEV)
        last = jnp.int32(-1)
        count = jnp.int32(0)
        for j in range(SLOTS):
            b = ids_ref[c, j] - low
            inside = (b >= 0) & (b < CB_DEV)
            first = jnp.where(inside, jnp.minimum(first, b), first)
            last = jnp.where(inside, jnp.maximum(last, b), last)
            count = count + jnp.where(inside, 1, 0)
        return first, last, count

    def stage(c):
        first, last, count = pick(c, low)
        sel[c, 0] = jnp.where(count >= 1, first, -1)
        sel[c, 1] = jnp.where(count >= 2, last, -1)
        first = jnp.minimum(first, CB_DEV - 1)
        last = jnp.maximum(last, 0)
        nk[c, :BLK, :] = k_ref[first]
        nk[c, BLK:, :] = k_ref[last]
        nv[c, :BLK, :] = v_ref[first]
        nv[c, BLK:, :] = v_ref[last]

    def score_bias(c, D):
        tr[D] = nv[c].T
        return (
            jnp.where(sel[c, 0] >= 0, 0.0, HIDDEN).astype(F32),
            jnp.where(sel[c, 1] >= 0, 0.0, HIDDEN).astype(F32),
        )

    def local_scores(keys, q, bias):
        s = dot(keys, q, NT) * SCALE
        s0 = s[:BLK] + bias[0]
        s1 = s[BLK:] + bias[1]
        m = jnp.max(jnp.maximum(s0, s1), axis=0, keepdims=True)
        m = jnp.maximum(m, FLOOR)
        return m, jnp.exp(jnp.concatenate([s0, s1], axis=0) - m)

    def scores(c, D, h, bias):
        m, e = local_scores(nk[c], q_all[c, h], bias)
        lw[c, h] = e
        st_out[c, h : h + 1, :] = m
        st_out[c, HEADS + h : HEADS + h + 1, :] = jnp.sum(e, axis=0, keepdims=True)
        ou[c, h] = dot(tr[D], e.astype(BF16))

    def weights_grad(c, h):
        d = dot(nv[c], g_all[c, h], NT)
        dp[c, h] = d
        e = lw[c, h].astype(BF16).astype(F32)
        st_out[c, 2 * HEADS + h : 2 * HEADS + h + 1, :] = jnp.sum(e * d, axis=0, keepdims=True)

    def grads(c, D, back=True):
        if back:
            tr[D] = nk[c].T
        for h in range(HEADS):
            w = lw[c, h] * fac[c, h : h + 1, :]
            p_t[D, :, head(h)] = w.astype(BF16)
            ds = (w * (dp[c, h] - lse_all[c, HEADS + h : HEADS + h + 1, :])).astype(BF16)
            ds_t[D, :, head(h)] = ds
            if back:
                qu[c, h] = dot(tr[D], ds)
        a = dot(ds_t[D], q_all[c].reshape(ROWS, DH))
        b = dot(p_t[D], g_all[c].reshape(ROWS, DH))
        for slot in range(2):
            rows = slice(slot * BLK, (slot + 1) * BLK)
            dks[2 * c + slot] = a[rows]
            dvs[2 * c + slot] = b[rows]

    def own_scores():
        keys = ok_ref[...]
        vt = ov_ref[...].T
        seen = lax.broadcasted_iota(jnp.int32, (BLK, 128), 0) <= lax.broadcasted_iota(jnp.int32, (BLK, 128), 1)
        for h in range(HEADS):
            s = jnp.where(seen, dot(keys, q_all[me, h], NT) * SCALE, HIDDEN)
            m = jnp.max(s, axis=0, keepdims=True)
            e = jnp.exp(s - m)
            own_lw[h] = e
            own_st[h : h + 1, :] = m
            own_st[HEADS + h : HEADS + h + 1, :] = jnp.sum(e, axis=0, keepdims=True)
            own_ou[h] = dot(vt, e.astype(BF16))

    def own_weights_grad(h):
        d = dot(ov_ref[...], g_all[me, h], NT)
        own_dp[h] = d
        e = own_lw[h].astype(BF16).astype(F32)
        own_del[h : h + 1, :] = jnp.sum(e * d, axis=0, keepdims=True)

    def own_factor(h):
        return jnp.exp(own_st[h : h + 1, :] - lse_all[me, h : h + 1, :])

    def own_grads():
        kt = ok_ref[...].T
        for h in range(HEADS):
            w = own_lw[h] * own_factor(h)
            p_t[2, :BLK, head(h)] = w.astype(BF16)
            ds = (w * (own_dp[h] - lse_all[me, HEADS + h : HEADS + h + 1, :])).astype(BF16)
            ds_t[2, :BLK, head(h)] = ds
            own_qu[h] = dot(kt, ds)
        okg_ref[...] = (dot(ds_t[2, :BLK, :], q_all[me].reshape(ROWS, DH)) * SCALE).astype(BF16)
        ovg_ref[...] = dot(p_t[2, :BLK, :], g_all[me].reshape(ROWS, DH)).astype(BF16)

    def near_copy(D, d, w):
        return pltpu.make_async_remote_copy(
            src_ref=(nk, nv)[w].at[toward(D, d)], dst_ref=(fk, fv)[w].at[2 * D + d - 1],
            send_sem=f_send.at[D, d - 1, w], recv_sem=f_recv.at[D, d - 1, w],
            device_id={"ctx": toward(D, d)},
        )

    def near_send(d):
        for w in range(2):
            for D in range(2):
                near_copy(D, d, w).start()

    def near_scores(D, d):
        n = 2 * D + d - 1
        for w in range(2):
            near_copy(D, d, w).wait_recv()
        count = pick(me, from_behind(D, d) * CB_DEV)[2]
        bias = biases(count)
        tr[D] = fv[n].T
        for h in range(HEADS):
            m, e = local_scores(fk[n], q_all[me, h], bias)
            f_lw[n, h] = e
            f_max[n, h : h + 1, :] = m
            f_ou[n, h] = dot(tr[D], e.astype(BF16))
            f_dp[n, h] = dot(fv[n], g_all[me, h], NT)

    def near_grads(D, d):
        n = 2 * D + d - 1
        tr[D] = fk[n].T
        for h in range(HEADS):
            w = f_lw[n, h] * jnp.exp(f_max[n, h : h + 1, :] - lse_all[me, h : h + 1, :])
            ds = (w * (f_dp[n, h] - lse_all[me, HEADS + h : HEADS + h + 1, :])).astype(BF16)
            own_qu[h] += dot(tr[D], ds)

    def combine():
        st_in[me] = st_out[me]
        each_peer(lambda p: to_candidate(st_out, st_in, st_s, st_r, wrap(me + p), wrap(me + p)).wait_recv())
        maxima = st_in[:, :HEADS, :]
        totals = st_in[:, HEADS : 2 * HEADS, :]
        parts = st_in[:, 2 * HEADS : 3 * HEADS, :]
        own_max = own_st[:HEADS, :]
        top = jnp.maximum(jnp.max(maxima, axis=0), own_max)
        lift = jnp.exp(maxima - top[None])
        own_lift = jnp.exp(own_max - top)
        total = own_st[HEADS:, :] * own_lift + jnp.sum(totals * lift, axis=0)
        lse_all[me, :HEADS, :] = top + jnp.log(total)
        lse_all[me, HEADS:, :] = (own_del[:HEADS, :] * own_lift + jnp.sum(parts * lift, axis=0)) / total
        to_holder(lse_all, ls_s, ls_r, me, FAR).start()

        def both_sides(p):
            to_holder(lse_all, ls_s, ls_r, me, FAR - p).start()
            to_holder(lse_all, ls_s, ls_r, me, FAR + p).start()

        loop(1, FAR, both_sides)

    def buffers(chain, D, d):
        return sb.at[chain, D, d - 1 - NEAR], rb.at[chain, D, d - 1 - NEAR]

    PARTS = (((0, 1), (2, 3)), ((0,), (1,), (2,), (3,)))

    def chain_copy(chain, D, d, heads):
        src, dst = buffers(chain, D, d)
        b, j = heads[0] // 2, heads[0] % 2
        rows = pl.ds(0, MARK + 16) if chain == 0 else pl.ds(j * 128, 128)
        return pltpu.make_async_remote_copy(
            src_ref=src.at[b, rows], dst_ref=dst.at[b, rows],
            send_sem=c_send.at[chain, D, d - 1, heads[0]], recv_sem=c_recv.at[chain, D, d - 1, heads[0]],
            device_id={"ctx": toward(D, NEAR + 1) if d == NEAR + 1 else nbr[D]},
        )

    def chain_step(chain, i):
        d = FAR - i
        for heads in PARTS[chain]:
            b = heads[0] // 2
            for D in ways(d + 1, b):
                chain_copy(chain, D, d + 1, heads).wait_recv()
            for D in ways(d, b):
                c = toward(D, d)
                out = buffers(chain, D, d)[0]
                came = D in ways(d + 1, b)
                arrived = buffers(chain, D, d + 1)[1] if came else None
                if chain == 0 and came:
                    old = arrived[b, MARK:, :].astype(F32)
                marks = []
                for h in heads:
                    j = h % 2
                    if chain == 0:
                        m = st_out[c, h : h + 1, :]
                        r = jnp.ceil(m * 0.25) * 4.0
                        if came:
                            r = jnp.maximum(r, old[8 * j : 8 * j + 1])
                        x = ou[c, h] * jnp.exp(m - r)
                        if came:
                            x = x + arrived[b, head(j), :].astype(F32) * jnp.exp(old[8 * j : 8 * j + 1] - r)
                        marks.append(jnp.broadcast_to(r, (8, 128)))
                    else:
                        x = qu[c, h]
                        if came:
                            x = x + arrived[b, head(j), :].astype(F32)
                    out[b, head(j), :] = x.astype(out.dtype)
                if chain == 0:
                    out[b, MARK:, :] = jnp.concatenate(marks, axis=0).astype(out.dtype)
            for D in ways(d, b):
                chain_copy(chain, D, d, heads).start()

    def chain_sent(chain, i):
        for heads in PARTS[chain]:
            for D in ways(FAR - i, heads[0] // 2):
                chain_copy(chain, D, FAR - i, heads).wait_send()

    def chain_grads(i):
        if is_int(i) and i == 0:
            grads(wrap(me + FAR), 0)
        else:
            grads(toward(0, FAR - i), 0)
            grads(toward(1, FAR - i), 1)

    def block_sum(b):
        a = jnp.zeros((BLK, DH), F32)
        g = jnp.zeros((BLK, DH), F32)
        for c in range(N):
            at = jnp.where(sel[c, 0] == b, 2 * c, jnp.where(sel[c, 1] == b, 2 * c + 1, EMPTY))
            a = a + dks[at]
            g = g + dvs[at]
        dk_ref[b] = (a * SCALE).astype(BF16)
        dv_ref[b] = g.astype(BF16)

    def query_step(t):
        gather_step(0, t)
        for c, D in behind(t):
            if not is_int(t) or t > NEAR:
                stage(c)
            bias = score_bias(c, D)
            for h in range(HEADS):
                scores(c, D, h, bias)

    def grad_step(t):
        gather_step(1, t)
        for c, D in behind(t):
            for h in range(HEADS):
                weights_grad(c, h)
        for c, D in behind(t):
            to_candidate(st_out, st_in, st_s, st_r, c, me).start()

    def gather_slot(s):
        pace()
        query_step(s)
        grad_step(s - 1)

    gather_first(0)
    gather_first(1)
    for copy in blocks_in:
        copy.wait()
    for d in range(1, NEAR + 1):
        for D in range(2):
            stage(toward(D, d))
    own_scores()
    stage(me)
    bias_me = score_bias(me, 0)
    for h in range(HEADS):
        scores(me, 0, h, bias_me)
    pace()
    query_step(1)
    gather_slot(2)
    loop(3, 7, gather_slot)
    gather_slot(7)
    gather_slot(8)

    chain_step(0, 0)
    grad_step(8)
    for h in range(HEADS):
        weights_grad(me, h)
        own_weights_grad(h)
    dks[EMPTY] = jnp.zeros((BLK, DH), F32)
    dvs[EMPTY] = jnp.zeros((BLK, DH), F32)
    near_send(1)
    pace()
    chain_step(0, 1)
    near_send(2)
    pace()
    chain_step(0, 2)
    combine()
    pace()
    chain_step(0, 3)
    near_scores(0, 1)
    near_scores(1, 1)
    for t in range(1, 9):
        gather_sent(0, t)
    pace()
    chain_step(0, 4)
    near_scores(0, 2)
    near_scores(1, 2)
    each_peer(lambda p: to_holder(lse_all, ls_s, ls_r, wrap(me + p), p).wait_recv())
    fac[:, :HEADS, :] = jnp.exp(st_out[:, :HEADS, :] - lse_all[:, :HEADS, :])

    chain_grads(0)
    chain_step(1, 0)
    chain_grads(1)
    pace()
    chain_step(0, 5)
    chain_step(1, 1)
    chain_grads(2)
    for D in range(2):
        grads(toward(D, 2), D, False)
    own_grads()
    pace()
    chain_step(1, 2)
    chain_grads(3)
    for D in range(2):
        grads(toward(D, 1), D, False)
    pace()
    chain_step(1, 3)
    chain_grads(4)
    grads(me, 0)
    last = NEAR + 1
    for h in range(HEADS):
        b, j = h // 2, h % 2
        x = own_ou[h] * own_factor(h) + ou[me, h] * fac[me, h : h + 1, :]
        for n in range(2 * NEAR):
            x = x + f_ou[n, h] * jnp.exp(f_max[n, h : h + 1, :] - lse_all[me, h : h + 1, :])
        for D in range(2):
            if j == 0:
                chain_copy(0, D, last, (h, h + 1)).wait_recv()
            came = buffers(0, D, last)[1]
            r = came[b, MARK:, :].astype(F32)[8 * j : 8 * j + 1]
            x = x + came[b, head(j), :].astype(F32) * jnp.exp(r - lse_all[me, h : h + 1, :])
        att_ref[:, head(h)] = x.T.astype(BF16)
    pace()
    chain_step(1, 4)
    chain_grads(5)
    near_grads(0, 1)
    near_grads(1, 1)
    near_grads(0, 2)
    near_grads(1, 2)
    for t in range(1, 9):
        gather_sent(1, t)
    pace()
    chain_step(1, 5)
    loop(0, CB_DEV, block_sum)
    each_peer(lambda p: to_candidate(st_out, st_in, st_s, st_r, wrap(me + p), me).wait_send())
    each_peer(lambda p: to_holder(lse_all, ls_s, ls_r, me, p).wait_send())
    for d in range(1, NEAR + 1):
        for D in range(2):
            for w in range(2):
                near_copy(D, d, w).wait_send()
    for i in range(6):
        chain_sent(0, i)
    for i in range(5):
        chain_sent(1, i)
    for h in range(HEADS):
        b, j = h // 2, h % 2
        x = own_qu[h] + qu[me, h]
        for D in range(2):
            chain_copy(1, D, last, (h,)).wait_recv()
            x = x + buffers(1, D, last)[1][b, head(j), :].astype(F32)
        qg_ref[:, head(h)] = (x * SCALE).T.astype(BF16)
    chain_sent(1, 5)


def ring(ids, q, k, v, ok, ov, g):
    vm = pl.BlockSpec(memory_space=pltpu.VMEM)
    hbm = pl.BlockSpec(memory_space=pl.ANY)
    shape = jax.ShapeDtypeStruct
    V = pltpu.VMEM
    D = pltpu.SemaphoreType.DMA
    message = (2, MARK + 16, 128)
    tile = (HEADS, 128, 128)
    return pl.pallas_call(
        ring_kernel,
        in_specs=[pl.BlockSpec(memory_space=pltpu.SMEM), vm, hbm, hbm, vm, vm, vm],
        out_specs=[vm] * 6,
        out_shape=[
            shape((128, ROWS), BF16), shape((128, ROWS), BF16),
            shape((BLK, DH), BF16), shape((BLK, DH), BF16),
            shape((CB_DEV, BLK, DH), BF16), shape((CB_DEV, BLK, DH), BF16),
        ],
        scratch_shapes=[
            V((N,) + tile, BF16), V((N,) + tile, BF16),
            V((N, KEYS, DH), BF16), V((N, KEYS, DH), BF16),
            V((N, HEADS, KEYS, 128), F32), V((N, HEADS, KEYS, 128), F32),
            V((N,) + tile, F32), V((N,) + tile, F32),
            V(tile, F32), V(tile, F32), V(tile, F32), V(tile, F32),
            V((8, 128), F32), V((8, 128), F32),
            V((N, 16, 128), F32), V((N, 16, 128), F32), V((N, 8, 128), F32), V((N, 8, 128), F32),
            V((3, KEYS, ROWS), BF16), V((3, KEYS, ROWS), BF16), V((2, DH, KEYS), BF16),
            V((2 * N + 1, BLK, DH), F32), V((2 * N + 1, BLK, DH), F32),
            pltpu.SMEM((N, 2), jnp.int32),
            V((2, 2, FAR - NEAR) + message, BF16), V((2, 2, FAR - NEAR) + message, BF16),
            V((2 * NEAR, KEYS, DH), BF16), V((2 * NEAR, KEYS, DH), BF16),
            V((2 * NEAR, HEADS, KEYS, 128), F32), V((2 * NEAR, HEADS, KEYS, 128), F32),
            V((2 * NEAR,) + tile, F32), V((2 * NEAR, 8, 128), F32),
            D((2, 2, FAR, 2)), D((2, 2, FAR, 2)), D((2, 2, FAR, HEADS)), D((2, 2, FAR, HEADS)),
            D((N,)), D((N,)), D((N,)), D((N,)), D((2, NEAR, 2)), D((2, NEAR, 2)),
            pltpu.SemaphoreType.REGULAR,
            V((CB_DEV, BLK, DH), BF16), V((CB_DEV, BLK, DH), BF16), D((2,)),
        ],
        compiler_params=pltpu.CompilerParams(
            collective_id=0, has_side_effects=True, vmem_limit_bytes=60 * 1024 * 1024
        ),
        name="ring_attention",
    )(ids, q, k, v, ok, ov, g)


def hand_on_kernel(*refs):
    n = (len(refs) - 2) // 3
    held = refs[2 * n : 3 * n]
    into = [pltpu.make_async_copy(refs[j], held[j], refs[3 * n].at[j]) for j in range(n)]
    out = [pltpu.make_async_copy(held[j], refs[n + j], refs[3 * n + 1].at[j]) for j in range(n)]
    for copy in into:
        copy.start()
    for j in range(n):
        into[j].wait()
        out[j].start()
    for copy in out:
        copy.wait()


def hand_on(parts):
    hbm = pl.BlockSpec(memory_space=pl.ANY)
    n = len(parts)
    return pl.pallas_call(
        hand_on_kernel,
        in_specs=[hbm] * n,
        out_specs=[hbm] * n,
        out_shape=[jax.ShapeDtypeStruct(x.shape, x.dtype) for x in parts],
        scratch_shapes=[pltpu.VMEM(x.shape, x.dtype) for x in parts]
        + [pltpu.SemaphoreType.DMA((n,)), pltpu.SemaphoreType.DMA((n,))],
        compiler_params=pltpu.CompilerParams(vmem_limit_bytes=60 * 1024 * 1024),
        name="hand_on",
    )(*parts)


def on_device(queries, context_keys, context_values, own_keys, own_values, out_grad, block_ids):
    k = context_keys.reshape(CB_DEV, BLK, DH)
    v = context_values.reshape(CB_DEV, BLK, DH)
    parts = ring(block_ids, queries, k, v, own_keys, own_values, out_grad)
    att, qg, okg, ovg, dk, dv = hand_on(parts)
    return att, qg, dk.reshape(CB_DEV * BLK, DH), dv.reshape(CB_DEV * BLK, DH), okg, ovg


def solution(mesh):
    rows = P(("dp", "ctx"), "head")
    return jax.shard_map(
        on_device,
        mesh=mesh,
        in_specs=(rows,) * 6 + (P("dp", None),),
        out_specs=(rows,) * 6,
        check_vma=False,
    )
```

```python
import math

import jax
import jax.numpy as jnp
from jax import lax
from jax.experimental import pallas as pl
from jax.experimental.pallas import tpu as pltpu
from jax.sharding import PartitionSpec as P

N = 16
BLK = 128
DH = 128
HEADS = 4
ROWS = HEADS * 128
KEYS = 2 * BLK
SLOTS = 24
CB_DEV = 16
EMPTY = 2 * N
SCALE = 1.0 / math.sqrt(DH)
HIDDEN = -1e30
FLOOR = -(2.0**83)
NEAR = 2
FAR = 8
MARK = 256
F32 = jnp.float32
BF16 = jnp.bfloat16
NT = (((1,), (1,)), ((), ()))
NN = (((1,), (0,)), ((), ()))


def dot(a, b, dims=NN):
    return lax.dot_general(a, b, dims, preferred_element_type=F32)


def wrap(x):
    return lax.rem(x + 2 * N, N)


def head(h):
    return slice(h * 128, (h + 1) * 128)


def is_int(x):
    return isinstance(x, int)


def ring_kernel(
    ids_ref, q_ref, k_hbm, v_hbm, ok_ref, ov_ref, g_ref,
    att_ref, qg_ref, okg_ref, ovg_ref, dk_ref, dv_ref,
    q_all, g_all, nk, nv, lw, dp, ou, qu,
    own_lw, own_dp, own_ou, own_qu, own_st, own_del,
    st_out, st_in, lse_all, fac,
    ds_t, p_t, tr, dks, dvs, sel, sb, rb,
    fk, fv, f_lw, f_dp, f_ou, f_max,
    g_send, g_recv, c_send, c_recv, st_s, st_r, ls_s, ls_r, f_send, f_recv, pace_sem, k_ref, v_ref, kv_sem,
):
    me = lax.axis_index("ctx")
    low = me * CB_DEV
    nbr = (wrap(me + 1), wrap(me - 1))

    blocks_in = (
        pltpu.make_async_copy(k_hbm, k_ref, kv_sem.at[0]),
        pltpu.make_async_copy(v_hbm, v_ref, kv_sem.at[1]),
    )
    for copy in blocks_in:
        copy.start()
    barrier = pltpu.get_barrier_semaphore()

    def loop(lo, hi, fn):
        def body(t, _):
            fn(t)
            return 0

        lax.fori_loop(lo, hi, body, 0)

    def each_peer(fn):
        loop(1, N, fn)

    paired = lax.axis_size("head") % 2 == 0
    side = lax.axis_index("head")
    other = side + 1 - 2 * lax.rem(side, 2)

    def pace(wait=True):
        if paired:
            pl.semaphore_signal(pace_sem, inc=1, device_id={"head": other})
            if wait:
                pl.semaphore_wait(pace_sem, 1)

    each_peer(lambda p: pl.semaphore_signal(barrier, inc=1, device_id={"ctx": wrap(me + p)}))
    if paired:
        pl.semaphore_signal(barrier, inc=1, device_id={"head": other})
    for h in range(HEADS):
        q_all[me, h] = q_ref[:, head(h)]
        g_all[me, h] = g_ref[:, head(h)]
    pl.semaphore_wait(barrier, N if paired else N - 1)

    def gather_copy(stream, D, t, b, c):
        part = (q_all, g_all)[stream].at[c, pl.ds(2 * b, 2)]
        return pltpu.make_async_remote_copy(
            src_ref=part, dst_ref=part,
            send_sem=g_send.at[stream, D, t - 1, b], recv_sem=g_recv.at[stream, D, t - 1, b],
            device_id={"ctx": nbr[D]},
        )

    def toward(D, d):
        return wrap(me + d) if D == 0 else wrap(me - d)

    def from_behind(D, t):
        return toward(1 - D, t)

    def ways(d, b):
        return (b,) if is_int(d) and d == FAR else () if is_int(d) and d > FAR else (0, 1)

    def behind(t):
        if is_int(t) and t == FAR:
            return ((wrap(me + FAR), 0),)
        return ((from_behind(0, t), 0), (from_behind(1, t), 1))

    def gather_step(stream, t):
        for b in range(2):
            for D in ways(t, b):
                gather_copy(stream, D, t, b, from_behind(D, t)).wait_recv()
            for D in ways(t + 1, b):
                gather_copy(stream, D, t + 1, b, from_behind(D, t)).start()

    def gather_first(stream):
        for b in range(2):
            for D in range(2):
                gather_copy(stream, D, 1, b, me).start()

    def gather_sent(stream, t):
        for b in range(2):
            for D in ways(t, b):
                gather_copy(stream, D, t, b, me).wait_send()

    def to_candidate(src, dst, send, recv, c, slot):
        return pltpu.make_async_remote_copy(
            src_ref=src.at[c], dst_ref=dst.at[slot], send_sem=send.at[c], recv_sem=recv.at[slot],
            device_id={"ctx": c},
        )

    def to_holder(buf, send, recv, slot, p):
        return pltpu.make_async_remote_copy(
            src_ref=buf.at[slot], dst_ref=buf.at[slot], send_sem=send.at[p], recv_sem=recv.at[slot],
            device_id={"ctx": wrap(me + p)},
        )

    def biases(count):
        return (
            jnp.where(count >= 1, 0.0, HIDDEN).astype(F32),
            jnp.where(count >= 2, 0.0, HIDDEN).astype(F32),
        )

    def pick(c, low):
        first = jnp.int32(CB_DEV)
        last = jnp.int32(-1)
        count = jnp.int32(0)
        for j in range(SLOTS):
            b = ids_ref[c, j] - low
            inside = (b >= 0) & (b < CB_DEV)
            first = jnp.where(inside, jnp.minimum(first, b), first)
            last = jnp.where(inside, jnp.maximum(last, b), last)
            count = count + jnp.where(inside, 1, 0)
        return first, last, count

    def stage(c):
        first, last, count = pick(c, low)
        sel[c, 0] = jnp.where(count >= 1, first, -1)
        sel[c, 1] = jnp.where(count >= 2, last, -1)
        first = jnp.minimum(first, CB_DEV - 1)
        last = jnp.maximum(last, 0)
        nk[c, :BLK, :] = k_ref[first]
        nk[c, BLK:, :] = k_ref[last]
        nv[c, :BLK, :] = v_ref[first]
        nv[c, BLK:, :] = v_ref[last]

    def score_bias(c, D):
        tr[D] = nv[c].T
        return (
            jnp.where(sel[c, 0] >= 0, 0.0, HIDDEN).astype(F32),
            jnp.where(sel[c, 1] >= 0, 0.0, HIDDEN).astype(F32),
        )

    def local_scores(keys, q, bias):
        s = dot(keys, q, NT) * SCALE
        s0 = s[:BLK] + bias[0]
        s1 = s[BLK:] + bias[1]
        m = jnp.max(jnp.maximum(s0, s1), axis=0, keepdims=True)
        m = jnp.maximum(m, FLOOR)
        return m, jnp.exp(jnp.concatenate([s0, s1], axis=0) - m)

    def scores(c, D, h, bias):
        m, e = local_scores(nk[c], q_all[c, h], bias)
        lw[c, h] = e
        st_out[c, h : h + 1, :] = m
        st_out[c, HEADS + h : HEADS + h + 1, :] = jnp.sum(e, axis=0, keepdims=True)
        ou[c, h] = dot(tr[D], e.astype(BF16))

    def weights_grad(c, h):
        d = dot(nv[c], g_all[c, h], NT)
        dp[c, h] = d
        e = lw[c, h].astype(BF16).astype(F32)
        st_out[c, 2 * HEADS + h : 2 * HEADS + h + 1, :] = jnp.sum(e * d, axis=0, keepdims=True)

    def grads(c, D, back=True):
        if back:
            tr[D] = nk[c].T
        for h in range(HEADS):
            w = lw[c, h] * fac[c, h : h + 1, :]
            p_t[D, :, head(h)] = w.astype(BF16)
            ds = (w * (dp[c, h] - lse_all[c, HEADS + h : HEADS + h + 1, :])).astype(BF16)
            ds_t[D, :, head(h)] = ds
            if back:
                qu[c, h] = dot(tr[D], ds)
        a = dot(ds_t[D], q_all[c].reshape(ROWS, DH))
        b = dot(p_t[D], g_all[c].reshape(ROWS, DH))
        for slot in range(2):
            rows = slice(slot * BLK, (slot + 1) * BLK)
            dks[2 * c + slot] = a[rows]
            dvs[2 * c + slot] = b[rows]

    def own_scores():
        keys = ok_ref[...]
        vt = ov_ref[...].T
        seen = lax.broadcasted_iota(jnp.int32, (BLK, 128), 0) <= lax.broadcasted_iota(jnp.int32, (BLK, 128), 1)
        for h in range(HEADS):
            s = jnp.where(seen, dot(keys, q_all[me, h], NT) * SCALE, HIDDEN)
            m = jnp.max(s, axis=0, keepdims=True)
            e = jnp.exp(s - m)
            own_lw[h] = e
            own_st[h : h + 1, :] = m
            own_st[HEADS + h : HEADS + h + 1, :] = jnp.sum(e, axis=0, keepdims=True)
            own_ou[h] = dot(vt, e.astype(BF16))

    def own_weights_grad(h):
        d = dot(ov_ref[...], g_all[me, h], NT)
        own_dp[h] = d
        e = own_lw[h].astype(BF16).astype(F32)
        own_del[h : h + 1, :] = jnp.sum(e * d, axis=0, keepdims=True)

    def own_factor(h):
        return jnp.exp(own_st[h : h + 1, :] - lse_all[me, h : h + 1, :])

    def own_grads():
        kt = ok_ref[...].T
        for h in range(HEADS):
            w = own_lw[h] * own_factor(h)
            p_t[2, :BLK, head(h)] = w.astype(BF16)
            ds = (w * (own_dp[h] - lse_all[me, HEADS + h : HEADS + h + 1, :])).astype(BF16)
            ds_t[2, :BLK, head(h)] = ds
            own_qu[h] = dot(kt, ds)
        okg_ref[...] = (dot(ds_t[2, :BLK, :], q_all[me].reshape(ROWS, DH)) * SCALE).astype(BF16)
        ovg_ref[...] = dot(p_t[2, :BLK, :], g_all[me].reshape(ROWS, DH)).astype(BF16)

    def near_copy(D, d, w):
        return pltpu.make_async_remote_copy(
            src_ref=(nk, nv)[w].at[toward(D, d)], dst_ref=(fk, fv)[w].at[2 * D + d - 1],
            send_sem=f_send.at[D, d - 1, w], recv_sem=f_recv.at[D, d - 1, w],
            device_id={"ctx": toward(D, d)},
        )

    def near_send(d):
        for w in range(2):
            for D in range(2):
                near_copy(D, d, w).start()

    def near_scores(D, d):
        n = 2 * D + d - 1
        for w in range(2):
            near_copy(D, d, w).wait_recv()
        count = pick(me, from_behind(D, d) * CB_DEV)[2]
        bias = biases(count)
        tr[D] = fv[n].T
        for h in range(HEADS):
            m, e = local_scores(fk[n], q_all[me, h], bias)
            f_lw[n, h] = e
            f_max[n, h : h + 1, :] = m
            f_ou[n, h] = dot(tr[D], e.astype(BF16))
            f_dp[n, h] = dot(fv[n], g_all[me, h], NT)

    def near_grads(D, d):
        n = 2 * D + d - 1
        tr[D] = fk[n].T
        for h in range(HEADS):
            w = f_lw[n, h] * jnp.exp(f_max[n, h : h + 1, :] - lse_all[me, h : h + 1, :])
            ds = (w * (f_dp[n, h] - lse_all[me, HEADS + h : HEADS + h + 1, :])).astype(BF16)
            own_qu[h] += dot(tr[D], ds)

    def combine():
        st_in[me] = st_out[me]
        each_peer(lambda p: to_candidate(st_out, st_in, st_s, st_r, wrap(me + p), wrap(me + p)).wait_recv())
        maxima = st_in[:, :HEADS, :]
        totals = st_in[:, HEADS : 2 * HEADS, :]
        parts = st_in[:, 2 * HEADS : 3 * HEADS, :]
        own_max = own_st[:HEADS, :]
        top = jnp.maximum(jnp.max(maxima, axis=0), own_max)
        lift = jnp.exp(maxima - top[None])
        own_lift = jnp.exp(own_max - top)
        total = own_st[HEADS:, :] * own_lift + jnp.sum(totals * lift, axis=0)
        lse_all[me, :HEADS, :] = top + jnp.log(total)
        lse_all[me, HEADS:, :] = (own_del[:HEADS, :] * own_lift + jnp.sum(parts * lift, axis=0)) / total
        to_holder(lse_all, ls_s, ls_r, me, FAR).start()

        def both_sides(p):
            to_holder(lse_all, ls_s, ls_r, me, FAR - p).start()
            to_holder(lse_all, ls_s, ls_r, me, FAR + p).start()

        loop(1, FAR, both_sides)

    def buffers(chain, D, d):
        return sb.at[chain, D, d - 1 - NEAR], rb.at[chain, D, d - 1 - NEAR]

    PARTS = (((0, 1), (2, 3)), ((0,), (1,), (2,), (3,)))

    def chain_copy(chain, D, d, heads):
        src, dst = buffers(chain, D, d)
        b, j = heads[0] // 2, heads[0] % 2
        rows = pl.ds(0, MARK + 16) if chain == 0 else pl.ds(j * 128, 128)
        return pltpu.make_async_remote_copy(
            src_ref=src.at[b, rows], dst_ref=dst.at[b, rows],
            send_sem=c_send.at[chain, D, d - 1, heads[0]], recv_sem=c_recv.at[chain, D, d - 1, heads[0]],
            device_id={"ctx": toward(D, NEAR + 1) if d == NEAR + 1 else nbr[D]},
        )

    def chain_step(chain, i):
        d = FAR - i
        for heads in PARTS[chain]:
            b = heads[0] // 2
            for D in ways(d + 1, b):
                chain_copy(chain, D, d + 1, heads).wait_recv()
            for D in ways(d, b):
                c = toward(D, d)
                out = buffers(chain, D, d)[0]
                came = D in ways(d + 1, b)
                arrived = buffers(chain, D, d + 1)[1] if came else None
                if chain == 0 and came:
                    old = arrived[b, MARK:, :].astype(F32)
                marks = []
                for h in heads:
                    j = h % 2
                    if chain == 0:
                        m = st_out[c, h : h + 1, :]
                        r = jnp.ceil(m * 0.25) * 4.0
                        if came:
                            r = jnp.maximum(r, old[8 * j : 8 * j + 1])
                        x = ou[c, h] * jnp.exp(m - r)
                        if came:
                            x = x + arrived[b, head(j), :].astype(F32) * jnp.exp(old[8 * j : 8 * j + 1] - r)
                        marks.append(jnp.broadcast_to(r, (8, 128)))
                    else:
                        x = qu[c, h]
                        if came:
                            x = x + arrived[b, head(j), :].astype(F32)
                    out[b, head(j), :] = x.astype(out.dtype)
                if chain == 0:
                    out[b, MARK:, :] = jnp.concatenate(marks, axis=0).astype(out.dtype)
            for D in ways(d, b):
                chain_copy(chain, D, d, heads).start()

    def chain_sent(chain, i):
        for heads in PARTS[chain]:
            for D in ways(FAR - i, heads[0] // 2):
                chain_copy(chain, D, FAR - i, heads).wait_send()

    def chain_grads(i):
        if is_int(i) and i == 0:
            grads(wrap(me + FAR), 0)
        else:
            grads(toward(0, FAR - i), 0)
            grads(toward(1, FAR - i), 1)

    def block_sum(b):
        a = jnp.zeros((BLK, DH), F32)
        g = jnp.zeros((BLK, DH), F32)
        for c in range(N):
            at = jnp.where(sel[c, 0] == b, 2 * c, jnp.where(sel[c, 1] == b, 2 * c + 1, EMPTY))
            a = a + dks[at]
            g = g + dvs[at]
        dk_ref[b] = (a * SCALE).astype(BF16)
        dv_ref[b] = g.astype(BF16)

    def query_step(t):
        gather_step(0, t)
        for c, D in behind(t):
            if not is_int(t) or t > NEAR:
                stage(c)
            bias = score_bias(c, D)
            for h in range(HEADS):
                scores(c, D, h, bias)

    def grad_step(t):
        gather_step(1, t)
        for c, D in behind(t):
            for h in range(HEADS):
                weights_grad(c, h)
        for c, D in behind(t):
            to_candidate(st_out, st_in, st_s, st_r, c, me).start()

    def gather_slot(s):
        pace()
        query_step(s)
        grad_step(s - 1)

    gather_first(0)
    gather_first(1)
    for copy in blocks_in:
        copy.wait()
    for d in range(1, NEAR + 1):
        for D in range(2):
            stage(toward(D, d))
    own_scores()
    stage(me)
    bias_me = score_bias(me, 0)
    for h in range(HEADS):
        scores(me, 0, h, bias_me)
    pace(False)
    query_step(1)
    gather_slot(2)
    loop(3, 7, gather_slot)
    gather_slot(7)
    gather_slot(8)

    chain_step(0, 0)
    grad_step(8)
    for h in range(HEADS):
        weights_grad(me, h)
        own_weights_grad(h)
    dks[EMPTY] = jnp.zeros((BLK, DH), F32)
    dvs[EMPTY] = jnp.zeros((BLK, DH), F32)
    near_send(1)
    pace()
    chain_step(0, 1)
    near_send(2)
    pace()
    chain_step(0, 2)
    combine()
    pace()
    chain_step(0, 3)
    near_scores(0, 1)
    near_scores(1, 1)
    for t in range(1, 9):
        gather_sent(0, t)
    pace()
    chain_step(0, 4)
    near_scores(0, 2)
    near_scores(1, 2)
    each_peer(lambda p: to_holder(lse_all, ls_s, ls_r, wrap(me + p), p).wait_recv())
    fac[:, :HEADS, :] = jnp.exp(st_out[:, :HEADS, :] - lse_all[:, :HEADS, :])

    chain_grads(0)
    chain_step(1, 0)
    chain_grads(1)
    pace()
    chain_step(0, 5)
    chain_step(1, 1)
    chain_grads(2)
    for D in range(2):
        grads(toward(D, 2), D, False)
    own_grads()
    pace()
    chain_step(1, 2)
    chain_grads(3)
    for D in range(2):
        grads(toward(D, 1), D, False)
    pace()
    chain_step(1, 3)
    chain_grads(4)
    grads(me, 0)
    last = NEAR + 1
    for h in range(HEADS):
        b, j = h // 2, h % 2
        x = own_ou[h] * own_factor(h) + ou[me, h] * fac[me, h : h + 1, :]
        for n in range(2 * NEAR):
            x = x + f_ou[n, h] * jnp.exp(f_max[n, h : h + 1, :] - lse_all[me, h : h + 1, :])
        for D in range(2):
            if j == 0:
                chain_copy(0, D, last, (h, h + 1)).wait_recv()
            came = buffers(0, D, last)[1]
            r = came[b, MARK:, :].astype(F32)[8 * j : 8 * j + 1]
            x = x + came[b, head(j), :].astype(F32) * jnp.exp(r - lse_all[me, h : h + 1, :])
        att_ref[:, head(h)] = x.T.astype(BF16)
    pace()
    chain_step(1, 4)
    chain_grads(5)
    near_grads(0, 1)
    near_grads(1, 1)
    near_grads(0, 2)
    near_grads(1, 2)
    for t in range(1, 9):
        gather_sent(1, t)
    pace()
    chain_step(1, 5)
    loop(0, CB_DEV, block_sum)
    each_peer(lambda p: to_candidate(st_out, st_in, st_s, st_r, wrap(me + p), me).wait_send())
    each_peer(lambda p: to_holder(lse_all, ls_s, ls_r, me, p).wait_send())
    for d in range(1, NEAR + 1):
        for D in range(2):
            for w in range(2):
                near_copy(D, d, w).wait_send()
    for i in range(6):
        chain_sent(0, i)
    for i in range(5):
        chain_sent(1, i)
    if paired:
        pl.semaphore_wait(pace_sem, 1)
    for h in range(HEADS):
        b, j = h // 2, h % 2
        x = own_qu[h] + qu[me, h]
        for D in range(2):
            chain_copy(1, D, last, (h,)).wait_recv()
            x = x + buffers(1, D, last)[1][b, head(j), :].astype(F32)
        qg_ref[:, head(h)] = (x * SCALE).T.astype(BF16)
    chain_sent(1, 5)


def ring(ids, q, k, v, ok, ov, g):
    vm = pl.BlockSpec(memory_space=pltpu.VMEM)
    hbm = pl.BlockSpec(memory_space=pl.ANY)
    shape = jax.ShapeDtypeStruct
    V = pltpu.VMEM
    D = pltpu.SemaphoreType.DMA
    message = (2, MARK + 16, 128)
    tile = (HEADS, 128, 128)
    return pl.pallas_call(
        ring_kernel,
        in_specs=[pl.BlockSpec(memory_space=pltpu.SMEM), vm, hbm, hbm, vm, vm, vm],
        out_specs=[vm] * 6,
        out_shape=[
            shape((128, ROWS), BF16), shape((128, ROWS), BF16),
            shape((BLK, DH), BF16), shape((BLK, DH), BF16),
            shape((CB_DEV, BLK, DH), BF16), shape((CB_DEV, BLK, DH), BF16),
        ],
        scratch_shapes=[
            V((N,) + tile, BF16), V((N,) + tile, BF16),
            V((N, KEYS, DH), BF16), V((N, KEYS, DH), BF16),
            V((N, HEADS, KEYS, 128), F32), V((N, HEADS, KEYS, 128), F32),
            V((N,) + tile, F32), V((N,) + tile, F32),
            V(tile, F32), V(tile, F32), V(tile, F32), V(tile, F32),
            V((8, 128), F32), V((8, 128), F32),
            V((N, 16, 128), F32), V((N, 16, 128), F32), V((N, 8, 128), F32), V((N, 8, 128), F32),
            V((3, KEYS, ROWS), BF16), V((3, KEYS, ROWS), BF16), V((2, DH, KEYS), BF16),
            V((2 * N + 1, BLK, DH), F32), V((2 * N + 1, BLK, DH), F32),
            pltpu.SMEM((N, 2), jnp.int32),
            V((2, 2, FAR - NEAR) + message, BF16), V((2, 2, FAR - NEAR) + message, BF16),
            V((2 * NEAR, KEYS, DH), BF16), V((2 * NEAR, KEYS, DH), BF16),
            V((2 * NEAR, HEADS, KEYS, 128), F32), V((2 * NEAR, HEADS, KEYS, 128), F32),
            V((2 * NEAR,) + tile, F32), V((2 * NEAR, 8, 128), F32),
            D((2, 2, FAR, 2)), D((2, 2, FAR, 2)), D((2, 2, FAR, HEADS)), D((2, 2, FAR, HEADS)),
            D((N,)), D((N,)), D((N,)), D((N,)), D((2, NEAR, 2)), D((2, NEAR, 2)),
            pltpu.SemaphoreType.REGULAR,
            V((CB_DEV, BLK, DH), BF16), V((CB_DEV, BLK, DH), BF16), D((2,)),
        ],
        compiler_params=pltpu.CompilerParams(
            collective_id=0, has_side_effects=True, vmem_limit_bytes=60 * 1024 * 1024
        ),
        name="ring_attention",
    )(ids, q, k, v, ok, ov, g)


def hand_on_kernel(*refs):
    n = (len(refs) - 2) // 3
    held = refs[2 * n : 3 * n]
    into = [pltpu.make_async_copy(refs[j], held[j], refs[3 * n].at[j]) for j in range(n)]
    out = [pltpu.make_async_copy(held[j], refs[n + j], refs[3 * n + 1].at[j]) for j in range(n)]
    for copy in into:
        copy.start()
    for j in range(n):
        into[j].wait()
        out[j].start()
    for copy in out:
        copy.wait()


def hand_on(parts):
    hbm = pl.BlockSpec(memory_space=pl.ANY)
    n = len(parts)
    return pl.pallas_call(
        hand_on_kernel,
        in_specs=[hbm] * n,
        out_specs=[hbm] * n,
        out_shape=[jax.ShapeDtypeStruct(x.shape, x.dtype) for x in parts],
        scratch_shapes=[pltpu.VMEM(x.shape, x.dtype) for x in parts]
        + [pltpu.SemaphoreType.DMA((n,)), pltpu.SemaphoreType.DMA((n,))],
        compiler_params=pltpu.CompilerParams(vmem_limit_bytes=60 * 1024 * 1024),
        name="hand_on",
    )(*parts)


def on_device(queries, context_keys, context_values, own_keys, own_values, out_grad, block_ids):
    k = context_keys.reshape(CB_DEV, BLK, DH)
    v = context_values.reshape(CB_DEV, BLK, DH)
    parts = ring(block_ids, queries, k, v, own_keys, own_values, out_grad)
    att, qg, okg, ovg, dk, dv = hand_on(parts)
    return att, qg, dk.reshape(CB_DEV * BLK, DH), dv.reshape(CB_DEV * BLK, DH), okg, ovg


def solution(mesh):
    rows = P(("dp", "ctx"), "head")
    return jax.shard_map(
        on_device,
        mesh=mesh,
        in_specs=(rows,) * 6 + (P("dp", None),),
        out_specs=(rows,) * 6,
        check_vma=False,
    )
```

```python
import math

import jax
import jax.numpy as jnp
from jax import lax
from jax.experimental import pallas as pl
from jax.experimental.pallas import tpu as pltpu
from jax.sharding import PartitionSpec as P

N = 16
BLK = 128
DH = 128
HEADS = 4
ROWS = HEADS * 128
KEYS = 2 * BLK
SLOTS = 24
CB_DEV = 16
EMPTY = 2 * N
SCALE = 1.0 / math.sqrt(DH)
HIDDEN = -1e30
FLOOR = -(2.0**83)
NEAR = 2
FAR = 8
MARK = 256
F32 = jnp.float32
BF16 = jnp.bfloat16
NT = (((1,), (1,)), ((), ()))
NN = (((1,), (0,)), ((), ()))


def dot(a, b, dims=NN):
    return lax.dot_general(a, b, dims, preferred_element_type=F32)


def wrap(x):
    return lax.rem(x + 2 * N, N)


def head(h):
    return slice(h * 128, (h + 1) * 128)


def is_int(x):
    return isinstance(x, int)


def ring_kernel(
    ids_ref, q_ref, k_hbm, v_hbm, ok_ref, ov_ref, g_ref,
    att_ref, qg_ref, okg_ref, ovg_ref, dk_ref, dv_ref,
    q_all, g_all, nk, nv, lw, dp, ou, qu,
    own_lw, own_dp, own_ou, own_qu, own_st, own_del,
    st_out, st_in, lse_all, fac,
    ds_t, p_t, tr, dks, dvs, sel, sb, rb,
    fk, fv, f_lw, f_dp, f_ou, f_max,
    g_send, g_recv, c_send, c_recv, st_s, st_r, ls_s, ls_r, f_send, f_recv, pace_sem, k_ref, v_ref, kv_sem,
):
    me = lax.axis_index("ctx")
    low = me * CB_DEV
    nbr = (wrap(me + 1), wrap(me - 1))

    blocks_in = (
        pltpu.make_async_copy(k_hbm, k_ref, kv_sem.at[0]),
        pltpu.make_async_copy(v_hbm, v_ref, kv_sem.at[1]),
    )
    for copy in blocks_in:
        copy.start()
    barrier = pltpu.get_barrier_semaphore()

    def loop(lo, hi, fn):
        def body(t, _):
            fn(t)
            return 0

        lax.fori_loop(lo, hi, body, 0)

    def each_peer(fn):
        loop(1, N, fn)

    paired = lax.axis_size("head") % 2 == 0
    side = lax.axis_index("head")
    other = side + 1 - 2 * lax.rem(side, 2)

    def pace(wait=True):
        if paired:
            pl.semaphore_signal(pace_sem, inc=1, device_id={"head": other})
            if wait:
                pl.semaphore_wait(pace_sem, 1)

    each_peer(lambda p: pl.semaphore_signal(barrier, inc=1, device_id={"ctx": wrap(me + p)}))
    if paired:
        pl.semaphore_signal(barrier, inc=1, device_id={"head": other})
    for h in range(HEADS):
        q_all[me, h] = q_ref[:, head(h)]
        g_all[me, h] = g_ref[:, head(h)]
    pl.semaphore_wait(barrier, N if paired else N - 1)

    def gather_copy(stream, D, t, b, c):
        part = (q_all, g_all)[stream].at[c, pl.ds(2 * b, 2)]
        return pltpu.make_async_remote_copy(
            src_ref=part, dst_ref=part,
            send_sem=g_send.at[stream, D, t - 1, b], recv_sem=g_recv.at[stream, D, t - 1, b],
            device_id={"ctx": nbr[D]},
        )

    def toward(D, d):
        return wrap(me + d) if D == 0 else wrap(me - d)

    def from_behind(D, t):
        return toward(1 - D, t)

    def ways(d, b):
        return (b,) if is_int(d) and d == FAR else () if is_int(d) and d > FAR else (0, 1)

    def behind(t):
        if is_int(t) and t == FAR:
            return ((wrap(me + FAR), 0),)
        return ((from_behind(0, t), 0), (from_behind(1, t), 1))

    def gather_step(stream, t):
        for b in range(2):
            for D in ways(t, b):
                gather_copy(stream, D, t, b, from_behind(D, t)).wait_recv()
            for D in ways(t + 1, b):
                gather_copy(stream, D, t + 1, b, from_behind(D, t)).start()

    def gather_first(stream):
        for b in range(2):
            for D in range(2):
                gather_copy(stream, D, 1, b, me).start()

    def gather_sent(stream, t):
        for b in range(2):
            for D in ways(t, b):
                gather_copy(stream, D, t, b, me).wait_send()

    def to_candidate(src, dst, send, recv, c, slot):
        return pltpu.make_async_remote_copy(
            src_ref=src.at[c], dst_ref=dst.at[slot], send_sem=send.at[c], recv_sem=recv.at[slot],
            device_id={"ctx": c},
        )

    def to_holder(buf, send, recv, slot, p):
        return pltpu.make_async_remote_copy(
            src_ref=buf.at[slot], dst_ref=buf.at[slot], send_sem=send.at[p], recv_sem=recv.at[slot],
            device_id={"ctx": wrap(me + p)},
        )

    def biases(count):
        return (
            jnp.where(count >= 1, 0.0, HIDDEN).astype(F32),
            jnp.where(count >= 2, 0.0, HIDDEN).astype(F32),
        )

    def pick(c, low):
        first = jnp.int32(CB_DEV)
        last = jnp.int32(-1)
        count = jnp.int32(0)
        for j in range(SLOTS):
            b = ids_ref[c, j] - low
            inside = (b >= 0) & (b < CB_DEV)
            first = jnp.where(inside, jnp.minimum(first, b), first)
            last = jnp.where(inside, jnp.maximum(last, b), last)
            count = count + jnp.where(inside, 1, 0)
        return first, last, count

    def stage(c):
        first, last, count = pick(c, low)
        sel[c, 0] = jnp.where(count >= 1, first, -1)
        sel[c, 1] = jnp.where(count >= 2, last, -1)
        first = jnp.minimum(first, CB_DEV - 1)
        last = jnp.maximum(last, 0)
        nk[c, :BLK, :] = k_ref[first]
        nk[c, BLK:, :] = k_ref[last]
        nv[c, :BLK, :] = v_ref[first]
        nv[c, BLK:, :] = v_ref[last]

    def score_bias(c, D):
        tr[D] = nv[c].T
        return (
            jnp.where(sel[c, 0] >= 0, 0.0, HIDDEN).astype(F32),
            jnp.where(sel[c, 1] >= 0, 0.0, HIDDEN).astype(F32),
        )

    def local_scores(keys, q, bias):
        s = dot(keys, q, NT) * SCALE
        s0 = s[:BLK] + bias[0]
        s1 = s[BLK:] + bias[1]
        m = jnp.max(jnp.maximum(s0, s1), axis=0, keepdims=True)
        m = jnp.maximum(m, FLOOR)
        return m, jnp.exp(jnp.concatenate([s0, s1], axis=0) - m)

    def scores(c, D, h, bias):
        m, e = local_scores(nk[c], q_all[c, h], bias)
        lw[c, h] = e
        st_out[c, h : h + 1, :] = m
        st_out[c, HEADS + h : HEADS + h + 1, :] = jnp.sum(e, axis=0, keepdims=True)
        ou[c, h] = dot(tr[D], e.astype(BF16))

    def weights_grad(c, h):
        d = dot(nv[c], g_all[c, h], NT)
        dp[c, h] = d
        e = lw[c, h].astype(BF16).astype(F32)
        st_out[c, 2 * HEADS + h : 2 * HEADS + h + 1, :] = jnp.sum(e * d, axis=0, keepdims=True)

    def grads(c, D, back=True):
        if back:
            tr[D] = nk[c].T
        for h in range(HEADS):
            w = lw[c, h] * fac[c, h : h + 1, :]
            p_t[D, :, head(h)] = w.astype(BF16)
            ds = (w * (dp[c, h] - lse_all[c, HEADS + h : HEADS + h + 1, :])).astype(BF16)
            ds_t[D, :, head(h)] = ds
            if back:
                qu[c, h] = dot(tr[D], ds)
        a = dot(ds_t[D], q_all[c].reshape(ROWS, DH))
        b = dot(p_t[D], g_all[c].reshape(ROWS, DH))
        for slot in range(2):
            rows = slice(slot * BLK, (slot + 1) * BLK)
            dks[2 * c + slot] = a[rows]
            dvs[2 * c + slot] = b[rows]

    def own_scores():
        keys = ok_ref[...]
        vt = ov_ref[...].T
        seen = lax.broadcasted_iota(jnp.int32, (BLK, 128), 0) <= lax.broadcasted_iota(jnp.int32, (BLK, 128), 1)
        for h in range(HEADS):
            s = jnp.where(seen, dot(keys, q_all[me, h], NT) * SCALE, HIDDEN)
            m = jnp.max(s, axis=0, keepdims=True)
            e = jnp.exp(s - m)
            own_lw[h] = e
            own_st[h : h + 1, :] = m
            own_st[HEADS + h : HEADS + h + 1, :] = jnp.sum(e, axis=0, keepdims=True)
            own_ou[h] = dot(vt, e.astype(BF16))

    def own_weights_grad(h):
        d = dot(ov_ref[...], g_all[me, h], NT)
        own_dp[h] = d
        e = own_lw[h].astype(BF16).astype(F32)
        own_del[h : h + 1, :] = jnp.sum(e * d, axis=0, keepdims=True)

    def own_factor(h):
        return jnp.exp(own_st[h : h + 1, :] - lse_all[me, h : h + 1, :])

    def own_grads():
        kt = ok_ref[...].T
        for h in range(HEADS):
            w = own_lw[h] * own_factor(h)
            p_t[2, :BLK, head(h)] = w.astype(BF16)
            ds = (w * (own_dp[h] - lse_all[me, HEADS + h : HEADS + h + 1, :])).astype(BF16)
            ds_t[2, :BLK, head(h)] = ds
            own_qu[h] = dot(kt, ds)
        okg_ref[...] = (dot(ds_t[2, :BLK, :], q_all[me].reshape(ROWS, DH)) * SCALE).astype(BF16)
        ovg_ref[...] = dot(p_t[2, :BLK, :], g_all[me].reshape(ROWS, DH)).astype(BF16)

    def near_copy(D, d, w):
        return pltpu.make_async_remote_copy(
            src_ref=(nk, nv)[w].at[toward(D, d)], dst_ref=(fk, fv)[w].at[2 * D + d - 1],
            send_sem=f_send.at[D, d - 1, w], recv_sem=f_recv.at[D, d - 1, w],
            device_id={"ctx": toward(D, d)},
        )

    def near_send(d):
        for w in range(2):
            for D in range(2):
                near_copy(D, d, w).start()

    def near_scores(D, d):
        n = 2 * D + d - 1
        for w in range(2):
            near_copy(D, d, w).wait_recv()
        count = pick(me, from_behind(D, d) * CB_DEV)[2]
        bias = biases(count)
        tr[D] = fv[n].T
        for h in range(HEADS):
            m, e = local_scores(fk[n], q_all[me, h], bias)
            f_lw[n, h] = e
            f_max[n, h : h + 1, :] = m
            f_ou[n, h] = dot(tr[D], e.astype(BF16))
            f_dp[n, h] = dot(fv[n], g_all[me, h], NT)

    def near_grads(D, d):
        n = 2 * D + d - 1
        tr[D] = fk[n].T
        for h in range(HEADS):
            w = f_lw[n, h] * jnp.exp(f_max[n, h : h + 1, :] - lse_all[me, h : h + 1, :])
            ds = (w * (f_dp[n, h] - lse_all[me, HEADS + h : HEADS + h + 1, :])).astype(BF16)
            own_qu[h] += dot(tr[D], ds)

    def combine():
        st_in[me] = st_out[me]
        each_peer(lambda p: to_candidate(st_out, st_in, st_s, st_r, wrap(me + p), wrap(me + p)).wait_recv())
        maxima = st_in[:, :HEADS, :]
        totals = st_in[:, HEADS : 2 * HEADS, :]
        parts = st_in[:, 2 * HEADS : 3 * HEADS, :]
        own_max = own_st[:HEADS, :]
        top = jnp.maximum(jnp.max(maxima, axis=0), own_max)
        lift = jnp.exp(maxima - top[None])
        own_lift = jnp.exp(own_max - top)
        total = own_st[HEADS:, :] * own_lift + jnp.sum(totals * lift, axis=0)
        lse_all[me, :HEADS, :] = top + jnp.log(total)
        lse_all[me, HEADS:, :] = (own_del[:HEADS, :] * own_lift + jnp.sum(parts * lift, axis=0)) / total
        to_holder(lse_all, ls_s, ls_r, me, FAR).start()

        def both_sides(p):
            to_holder(lse_all, ls_s, ls_r, me, FAR - p).start()
            to_holder(lse_all, ls_s, ls_r, me, FAR + p).start()

        loop(1, FAR, both_sides)

    def buffers(chain, D, d):
        return sb.at[chain, D, d - 1 - NEAR], rb.at[chain, D, d - 1 - NEAR]

    PARTS = (((0, 1), (2, 3)), ((0,), (1,), (2,), (3,)))

    def chain_copy(chain, D, d, heads):
        src, dst = buffers(chain, D, d)
        b, j = heads[0] // 2, heads[0] % 2
        rows = pl.ds(0, MARK + 16) if chain == 0 else pl.ds(j * 128, 128)
        return pltpu.make_async_remote_copy(
            src_ref=src.at[b, rows], dst_ref=dst.at[b, rows],
            send_sem=c_send.at[chain, D, d - 1, heads[0]], recv_sem=c_recv.at[chain, D, d - 1, heads[0]],
            device_id={"ctx": toward(D, NEAR + 1) if d == NEAR + 1 else nbr[D]},
        )

    def chain_step(chain, i):
        d = FAR - i
        for heads in PARTS[chain]:
            b = heads[0] // 2
            for D in ways(d + 1, b):
                chain_copy(chain, D, d + 1, heads).wait_recv()
            for D in ways(d, b):
                c = toward(D, d)
                out = buffers(chain, D, d)[0]
                came = D in ways(d + 1, b)
                arrived = buffers(chain, D, d + 1)[1] if came else None
                if chain == 0 and came:
                    old = arrived[b, MARK:, :].astype(F32)
                marks = []
                for h in heads:
                    j = h % 2
                    if chain == 0:
                        m = st_out[c, h : h + 1, :]
                        r = jnp.ceil(m * 0.25) * 4.0
                        if came:
                            r = jnp.maximum(r, old[8 * j : 8 * j + 1])
                        x = ou[c, h] * jnp.exp(m - r)
                        if came:
                            x = x + arrived[b, head(j), :].astype(F32) * jnp.exp(old[8 * j : 8 * j + 1] - r)
                        marks.append(jnp.broadcast_to(r, (8, 128)))
                    else:
                        x = qu[c, h]
                        if came:
                            x = x + arrived[b, head(j), :].astype(F32)
                    out[b, head(j), :] = x.astype(out.dtype)
                if chain == 0:
                    out[b, MARK:, :] = jnp.concatenate(marks, axis=0).astype(out.dtype)
            for D in ways(d, b):
                chain_copy(chain, D, d, heads).start()

    def chain_sent(chain, i):
        for heads in PARTS[chain]:
            for D in ways(FAR - i, heads[0] // 2):
                chain_copy(chain, D, FAR - i, heads).wait_send()

    def chain_grads(i):
        if is_int(i) and i == 0:
            grads(wrap(me + FAR), 0)
        else:
            grads(toward(0, FAR - i), 0)
            grads(toward(1, FAR - i), 1)

    def block_sum(b):
        a = jnp.zeros((BLK, DH), F32)
        g = jnp.zeros((BLK, DH), F32)
        for c in range(N):
            at = jnp.where(sel[c, 0] == b, 2 * c, jnp.where(sel[c, 1] == b, 2 * c + 1, EMPTY))
            a = a + dks[at]
            g = g + dvs[at]
        dk_ref[b] = (a * SCALE).astype(BF16)
        dv_ref[b] = g.astype(BF16)

    def query_step(t):
        gather_step(0, t)
        for c, D in behind(t):
            if not is_int(t) or t > NEAR:
                stage(c)
            bias = score_bias(c, D)
            for h in range(HEADS):
                scores(c, D, h, bias)

    def grad_step(t):
        gather_step(1, t)
        for c, D in behind(t):
            for h in range(HEADS):
                weights_grad(c, h)
        for c, D in behind(t):
            to_candidate(st_out, st_in, st_s, st_r, c, me).start()

    def gather_slot(s):
        pace()
        query_step(s)
        grad_step(s - 1)

    gather_first(0)
    gather_first(1)
    for copy in blocks_in:
        copy.wait()
    for d in range(1, NEAR + 1):
        for D in range(2):
            stage(toward(D, d))
    own_scores()
    stage(me)
    bias_me = score_bias(me, 0)
    for h in range(HEADS):
        scores(me, 0, h, bias_me)
    pace(False)
    query_step(1)
    gather_slot(2)
    loop(3, 7, gather_slot)
    gather_slot(7)
    gather_slot(8)

    chain_step(0, 0)
    grad_step(8)
    for h in range(HEADS):
        weights_grad(me, h)
        own_weights_grad(h)
    dks[EMPTY] = jnp.zeros((BLK, DH), F32)
    dvs[EMPTY] = jnp.zeros((BLK, DH), F32)
    near_send(1)
    pace()
    chain_step(0, 1)
    near_send(2)
    pace()
    chain_step(0, 2)
    combine()
    pace()
    chain_step(0, 3)
    near_scores(0, 1)
    near_scores(1, 1)
    for t in range(1, 9):
        gather_sent(0, t)
    each_peer(lambda p: to_holder(lse_all, ls_s, ls_r, wrap(me + p), p).wait_recv())
    fac[:, :HEADS, :] = jnp.exp(st_out[:, :HEADS, :] - lse_all[:, :HEADS, :])

    chain_grads(0)
    chain_step(1, 0)
    chain_grads(1)
    pace()
    chain_step(0, 4)
    chain_step(1, 1)
    chain_grads(2)
    near_scores(0, 2)
    near_scores(1, 2)
    for D in range(2):
        grads(toward(D, 2), D, False)
    own_grads()
    pace()
    chain_step(0, 5)
    chain_step(1, 2)
    chain_grads(3)
    for D in range(2):
        grads(toward(D, 1), D, False)
    pace()
    chain_step(1, 3)
    chain_grads(4)
    grads(me, 0)
    last = NEAR + 1
    for h in range(HEADS):
        b, j = h // 2, h % 2
        x = own_ou[h] * own_factor(h) + ou[me, h] * fac[me, h : h + 1, :]
        for n in range(2 * NEAR):
            x = x + f_ou[n, h] * jnp.exp(f_max[n, h : h + 1, :] - lse_all[me, h : h + 1, :])
        for D in range(2):
            if j == 0:
                chain_copy(0, D, last, (h, h + 1)).wait_recv()
            came = buffers(0, D, last)[1]
            r = came[b, MARK:, :].astype(F32)[8 * j : 8 * j + 1]
            x = x + came[b, head(j), :].astype(F32) * jnp.exp(r - lse_all[me, h : h + 1, :])
        att_ref[:, head(h)] = x.T.astype(BF16)
    pace()
    chain_step(1, 4)
    chain_grads(5)
    near_grads(0, 1)
    near_grads(1, 1)
    near_grads(0, 2)
    near_grads(1, 2)
    for t in range(1, 9):
        gather_sent(1, t)
    pace()
    chain_step(1, 5)
    loop(0, CB_DEV, block_sum)
    each_peer(lambda p: to_candidate(st_out, st_in, st_s, st_r, wrap(me + p), me).wait_send())
    each_peer(lambda p: to_holder(lse_all, ls_s, ls_r, me, p).wait_send())
    for d in range(1, NEAR + 1):
        for D in range(2):
            for w in range(2):
                near_copy(D, d, w).wait_send()
    for i in range(6):
        chain_sent(0, i)
    for i in range(5):
        chain_sent(1, i)
    if paired:
        pl.semaphore_wait(pace_sem, 1)
    for h in range(HEADS):
        b, j = h // 2, h % 2
        x = own_qu[h] + qu[me, h]
        for D in range(2):
            chain_copy(1, D, last, (h,)).wait_recv()
            x = x + buffers(1, D, last)[1][b, head(j), :].astype(F32)
        qg_ref[:, head(h)] = (x * SCALE).T.astype(BF16)
    chain_sent(1, 5)


def ring(ids, q, k, v, ok, ov, g):
    vm = pl.BlockSpec(memory_space=pltpu.VMEM)
    hbm = pl.BlockSpec(memory_space=pl.ANY)
    shape = jax.ShapeDtypeStruct
    V = pltpu.VMEM
    D = pltpu.SemaphoreType.DMA
    message = (2, MARK + 16, 128)
    tile = (HEADS, 128, 128)
    return pl.pallas_call(
        ring_kernel,
        in_specs=[pl.BlockSpec(memory_space=pltpu.SMEM), vm, hbm, hbm, vm, vm, vm],
        out_specs=[vm] * 6,
        out_shape=[
            shape((128, ROWS), BF16), shape((128, ROWS), BF16),
            shape((BLK, DH), BF16), shape((BLK, DH), BF16),
            shape((CB_DEV, BLK, DH), BF16), shape((CB_DEV, BLK, DH), BF16),
        ],
        scratch_shapes=[
            V((N,) + tile, BF16), V((N,) + tile, BF16),
            V((N, KEYS, DH), BF16), V((N, KEYS, DH), BF16),
            V((N, HEADS, KEYS, 128), F32), V((N, HEADS, KEYS, 128), F32),
            V((N,) + tile, F32), V((N,) + tile, F32),
            V(tile, F32), V(tile, F32), V(tile, F32), V(tile, F32),
            V((8, 128), F32), V((8, 128), F32),
            V((N, 16, 128), F32), V((N, 16, 128), F32), V((N, 8, 128), F32), V((N, 8, 128), F32),
            V((3, KEYS, ROWS), BF16), V((3, KEYS, ROWS), BF16), V((2, DH, KEYS), BF16),
            V((2 * N + 1, BLK, DH), F32), V((2 * N + 1, BLK, DH), F32),
            pltpu.SMEM((N, 2), jnp.int32),
            V((2, 2, FAR - NEAR) + message, BF16), V((2, 2, FAR - NEAR) + message, BF16),
            V((2 * NEAR, KEYS, DH), BF16), V((2 * NEAR, KEYS, DH), BF16),
            V((2 * NEAR, HEADS, KEYS, 128), F32), V((2 * NEAR, HEADS, KEYS, 128), F32),
            V((2 * NEAR,) + tile, F32), V((2 * NEAR, 8, 128), F32),
            D((2, 2, FAR, 2)), D((2, 2, FAR, 2)), D((2, 2, FAR, HEADS)), D((2, 2, FAR, HEADS)),
            D((N,)), D((N,)), D((N,)), D((N,)), D((2, NEAR, 2)), D((2, NEAR, 2)),
            pltpu.SemaphoreType.REGULAR,
            V((CB_DEV, BLK, DH), BF16), V((CB_DEV, BLK, DH), BF16), D((2,)),
        ],
        compiler_params=pltpu.CompilerParams(
            collective_id=0, has_side_effects=True, vmem_limit_bytes=60 * 1024 * 1024
        ),
        name="ring_attention",
    )(ids, q, k, v, ok, ov, g)


def hand_on_kernel(*refs):
    n = (len(refs) - 2) // 3
    held = refs[2 * n : 3 * n]
    into = [pltpu.make_async_copy(refs[j], held[j], refs[3 * n].at[j]) for j in range(n)]
    out = [pltpu.make_async_copy(held[j], refs[n + j], refs[3 * n + 1].at[j]) for j in range(n)]
    for copy in into:
        copy.start()
    for j in range(n):
        into[j].wait()
        out[j].start()
    for copy in out:
        copy.wait()


def hand_on(parts):
    hbm = pl.BlockSpec(memory_space=pl.ANY)
    n = len(parts)
    return pl.pallas_call(
        hand_on_kernel,
        in_specs=[hbm] * n,
        out_specs=[hbm] * n,
        out_shape=[jax.ShapeDtypeStruct(x.shape, x.dtype) for x in parts],
        scratch_shapes=[pltpu.VMEM(x.shape, x.dtype) for x in parts]
        + [pltpu.SemaphoreType.DMA((n,)), pltpu.SemaphoreType.DMA((n,))],
        compiler_params=pltpu.CompilerParams(vmem_limit_bytes=60 * 1024 * 1024),
        name="hand_on",
    )(*parts)


def on_device(queries, context_keys, context_values, own_keys, own_values, out_grad, block_ids):
    k = context_keys.reshape(CB_DEV, BLK, DH)
    v = context_values.reshape(CB_DEV, BLK, DH)
    parts = ring(block_ids, queries, k, v, own_keys, own_values, out_grad)
    att, qg, okg, ovg, dk, dv = hand_on(parts)
    return att, qg, dk.reshape(CB_DEV * BLK, DH), dv.reshape(CB_DEV * BLK, DH), okg, ovg


def solution(mesh):
    rows = P(("dp", "ctx"), "head")
    return jax.shard_map(
        on_device,
        mesh=mesh,
        in_specs=(rows,) * 6 + (P("dp", None),),
        out_specs=(rows,) * 6,
        check_vma=False,
    )
```
